32 devices in a mesh: path: 2 (over core), dp: 16 (over z, y, x).
Axes of the slice: x: 2, y: 2, z: 4, core: 2. Of those that a mesh axis runs over, the one named last changes fastest.
Arguments:
- slow_in: bfloat16 [2, 128, 196, 1024], P(None, ('path', 'dp')), may hold values from -6 to 6
- fast_in: bfloat16 [2, 512, 196, 128], P(None, ('path', 'dp')), may hold values from -6 to 6
- clip_starts: int32 [2, 128], P(None, ('path', 'dp')), may hold values from 0 to 1, as said below
- w_lateral: bfloat16 [163840], P(('path', 'dp')), may hold values from -0.25 to 0.25
- w_slow_time: bfloat16 [983040], P(('path', 'dp')), may hold values from -0.09375 to 0.09375
- w_slow_space: bfloat16 [589824], P(('path', 'dp')), may hold values from -0.125 to 0.125
- w_slow_out: bfloat16 [262144], P(('path', 'dp')), may hold values from -0.375 to 0.375
- w_projection: bfloat16 [1310720], P(('path', 'dp')), may hold values from -0.15625 to 0.15625
- w_fast_time: bfloat16 [12288], P(('path', 'dp')), may hold values from -0.3125 to 0.3125
- w_fast_space: bfloat16 [9216], P(('path', 'dp')), may hold values from -0.375 to 0.375
- w_fast_out: bfloat16 [4096], P(('path', 'dp')), may hold values from -1 to 1
- slow_gain: bfloat16 [2816], P(('path', 'dp')), may hold values from 0.25 to 1.75
- slow_bias: bfloat16 [2816], P(('path', 'dp')), may hold values from -3 to 3
- fast_gain: bfloat16 [192], replicated, may hold values from 0.25 to 1.75
- fast_bias: bfloat16 [192], replicated, may hold values from -3 to 3
- slow_cotangent: bfloat16 [2, 128, 196, 1024], P(None, ('path', 'dp')), may hold values from -6 to 6
- fast_cotangent: bfloat16 [2, 512, 196, 128], P(None, ('path', 'dp')), may hold values from -6 to 6
Outputs:
- slow_out: bfloat16 [2, 128, 196, 1024], P(None, ('path', 'dp'))
- fast_out: bfloat16 [2, 512, 196, 128], P(None, ('path', 'dp'))
- slow_in_grad: bfloat16 [2, 128, 196, 1024], P(None, ('path', 'dp'))
- fast_in_grad: bfloat16 [2, 512, 196, 128], P(None, ('path', 'dp'))
- lateral_grad: float32 [163840], P(('path', 'dp'))
- slow_time_grad: float32 [983040], P(('path', 'dp'))
- slow_space_grad: float32 [589824], P(('path', 'dp'))
- slow_out_grad: float32 [262144], P(('path', 'dp'))
- projection_grad: float32 [1310720], P(('path', 'dp'))
- fast_time_grad: float32 [12288], P(('path', 'dp'))
- fast_space_grad: float32 [9216], P(('path', 'dp'))
- fast_out_grad: float32 [4096], P(('path', 'dp'))
- slow_gain_grad: float32 [2816], P(('path', 'dp'))
- slow_bias_grad: float32 [2816], P(('path', 'dp'))
- fast_gain_grad: float32 [192], replicated
- fast_bias_grad: float32 [192], replicated
The draws below stay inside these ranges and needn't reach their ends.
Inputs may be any that keep to these rules, and one draw needn't show every extreme that they name: `clip_starts`: 1 marks the first slow frame of a clip; frame 0 of every stream is 1; clips never span streams.
All inputs are finite; a program needn't handle non-finite values.
Results may differ from the reference program's by a relative error of at most 0.0085.
Values may be sent and summed in bfloat16 or wider, within the bound.
No kernel may reach another device: no remote copies, remote signals or barrier semaphores. Data moves between devices by JAX's collectives and lax.ppermute only.
A program may use at most 256 MiB of HBM per device.

```python
from functools import partial
import jax
import jax.numpy as jnp
from jax import lax

CS = 1024
CL = 256
CM = 256
CF = 128
CFM = 32
HH = 14
WW = 14
MICRO = 2
SLOW_FR = 128
FAST_FR = 512
PIX = 196
BN_SLOW = 2816
BN_FAST = 192
LAT_W = 163840
ST_W = 983040
SS_W = 589824
SO_W = 262144
PR_W = 1310720
FT_W = 12288
FSP_W = 9216
FO_W = 4096


def draw_clip_starts(key, part):
    key = jax.random.fold_in(key, 7)
    dice_rolls = jax.random.randint(key, (MICRO, SLOW_FR), 0, 8)
    starts = (dice_rolls == 0).astype(jnp.int32)
    return starts.at[:, 0].set(1)


def shard_levels(own_key, dims, pieces, least, top_value):
    def one(dim, parts):
        heights = jax.random.uniform(jax.random.fold_in(jax.random.fold_in(own_key, 6), dim), (parts,), jnp.float32, least / len(pieces), top_value / len(pieces))
        return jnp.repeat(jnp.exp(heights), dims[dim] // parts).reshape((-1,) + (1,) * (len(dims) - dim - 1))

    factor_of = one(*pieces[0])
    for cut in pieces[1:]:
        factor_of = factor_of * one(*cut)
    return factor_of


def bell_draw(rng, shape, deviation, limit, shards=(), held_as=jnp.bfloat16):
    factor_of = shard_levels(rng, shape, shards, -0.22, 0.18) if shards else 1.0
    values = jax.random.normal(rng, shape, jnp.float32) * deviation * factor_of
    return jnp.minimum(jnp.maximum(values, -limit), limit).astype(held_as)


def setup_inputs(seed: int = 0) -> dict:
    streams_of = jax.random.split(jax.random.key(seed), 18)
    return {
        "slow_in": bell_draw(streams_of[0], (MICRO, SLOW_FR, PIX, CS), 1.0, 6.0, ((1, 32),)),
        "fast_in": bell_draw(streams_of[1], (MICRO, FAST_FR, PIX, CF), 1.0, 6.0, ((1, 32),)),
        "clip_starts": draw_clip_starts(jax.random.fold_in(streams_of[17], 71), 0),
        "w_lateral": bell_draw(streams_of[3], (LAT_W,), (5 * CF) ** -0.5, 0.25, ((0, 32),)),
        "w_slow_time": bell_draw(streams_of[4], (ST_W,), (3 * (CS + CL)) ** -0.5, 0.09375, ((0, 32),)),
        "w_slow_space": bell_draw(streams_of[5], (SS_W,), (9 * CM) ** -0.5, 0.125, ((0, 32),)),
        "w_slow_out": bell_draw(streams_of[6], (SO_W,), CM ** -0.5, 0.375, ((0, 32),)),
        "w_projection": bell_draw(streams_of[7], (PR_W,), (CS + CL) ** -0.5, 0.15625, ((0, 32),)),
        "w_fast_time": bell_draw(streams_of[8], (FT_W,), (3 * CF) ** -0.5, 0.3125, ((0, 32),)),
        "w_fast_space": bell_draw(streams_of[9], (FSP_W,), (9 * CFM) ** -0.5, 0.375, ((0, 32),)),
        "w_fast_out": bell_draw(streams_of[10], (FO_W,), CFM ** -0.5, 1.0, ((0, 32),)),
        "slow_gain": jnp.clip(1.0 + 0.15 * jax.random.normal(streams_of[11], (BN_SLOW,), jnp.float32), 0.25, 1.75).astype(jnp.bfloat16),
        "slow_bias": bell_draw(streams_of[12], (BN_SLOW,), 0.5, 3.0, ((0, 32),)),
        "fast_gain": jnp.clip(1.0 + 0.15 * jax.random.normal(streams_of[13], (BN_FAST,), jnp.float32), 0.25, 1.75).astype(jnp.bfloat16),
        "fast_bias": bell_draw(streams_of[14], (BN_FAST,), 0.5, 3.0),
        "slow_cotangent": bell_draw(streams_of[15], (MICRO, SLOW_FR, PIX, CS), 1.0, 6.0, ((1, 32),)),
        "fast_cotangent": bell_draw(streams_of[16], (MICRO, FAST_FR, PIX, CF), 1.0, 6.0, ((1, 32),)),
    }


EPS = 1e-05
HIGHEST = lax.Precision.HIGHEST

@jax.custom_vjp
def low(v):
    return lax.optimization_barrier(v.astype(jnp.bfloat16)).astype(jnp.float32)

@jax.custom_vjp
def low_back(v):
    return v

def low_keep(v):
    return (low(v), None)

def low_pass(kept, grad):
    return (grad,)

def back_keep(v):
    return (v, None)

def back_low(kept, grad):
    return (low(grad),)
low.defvjp(low_keep, low_pass)
low_back.defvjp(back_keep, back_low)

def product(inputs, weight):
    return jnp.einsum('...c,co->...o', inputs, weight, precision=HIGHEST)

def smooth(inputs):
    return jax.nn.gelu(inputs, approximate=True)

def normalize(pre_norm, gain_vec, bias_vec):
    mean_val = lax.optimization_barrier(jnp.mean(pre_norm, (0, 1)))
    var_val = lax.optimization_barrier(jnp.mean(pre_norm * pre_norm, (0, 1))) - mean_val * mean_val
    return (pre_norm - mean_val) * lax.rsqrt(var_val + EPS) * gain_vec + bias_vec

def split_parts(vector, extents):
    parts_out = []
    start_at = 0
    for extent in extents:
        parts_out.append(vector[start_at:start_at + extent])
        start_at += extent
    return parts_out

def in_time(frames, linked, weight):
    blank = jnp.zeros_like(frames[:1])
    mask_col = linked[:, None, None]
    before = jnp.concatenate([blank, frames[:-1]], 0) * mask_col
    after = jnp.concatenate([frames[1:] * mask_col[1:], blank], 0)
    return product(before, weight[0]) + product(frames, weight[1]) + product(after, weight[2])

def in_space(frames, weight):
    grid_cells = frames.reshape(frames.shape[0], HH, WW, frames.shape[-1])
    padded = jnp.pad(grid_cells, ((0, 0), (1, 1), (1, 1), (0, 0)))
    result = jnp.zeros(frames.shape[:-1] + (weight.shape[-1],), jnp.float32)
    for row_at in range(3):
        for col_at in range(3):
            tap_item = padded[:, row_at:row_at + HH, col_at:col_at + WW, :].reshape(frames.shape)
            result = result + product(tap_item, weight[3 * row_at + col_at])
    return result

def lateral_conv(fast_frames, linked, weight):
    count_s = linked.shape[0]
    quads = fast_frames.reshape(count_s, 4, fast_frames.shape[1], fast_frames.shape[2])
    blank = jnp.zeros_like(quads[:1, 0])
    mask_col = linked[:, None, None]
    third = jnp.concatenate([blank, quads[:-1, 2]], 0) * mask_col
    fourth = jnp.concatenate([blank, quads[:-1, 3]], 0) * mask_col
    result = product(third, weight[0]) + product(fourth, weight[1])
    for tap_num in range(3):
        result = result + product(quads[:, tap_num], weight[tap_num + 2])
    return result

def forward(clip_starts, slow_in, fast_in, w_lateral, w_slow_time, w_slow_space, w_slow_out, w_projection, w_fast_time, w_fast_space, w_fast_out, slow_gain, slow_bias, fast_gain, fast_bias):
    lateral = w_lateral.reshape(5, CF, CL)
    slow_time = w_slow_time.reshape(3, CS + CL, CM)
    slow_space = w_slow_space.reshape(9, CM, CM)
    slow_proj = w_slow_out.reshape(CM, CS)
    projection = w_projection.reshape(CS + CL, CS)
    fast_time = w_fast_time.reshape(3, CF, CFM)
    fast_space = w_fast_space.reshape(9, CFM, CFM)
    fast_proj = w_fast_out.reshape(CFM, CF)
    slow_gains = split_parts(slow_gain, [CL, CM, CM, CS, CS])
    slow_biases = split_parts(slow_bias, [CL, CM, CM, CS, CS])
    fast_gains = split_parts(fast_gain, [CFM, CFM, CF])
    fast_biases = split_parts(fast_bias, [CFM, CFM, CF])
    slow_list = []
    fast_list = []
    for micro_step in range(MICRO):
        starts = clip_starts[micro_step]
        slow_link = (1 - starts).astype(jnp.float32)
        fast_link = jnp.where(jnp.arange(4 * SLOW_FR) % 4 == 0, jnp.repeat(slow_link, 4), 1.0).astype(jnp.float32)
        slow_block = slow_in[micro_step]
        fast_block = fast_in[micro_step]
        lat_pre = low_back(lateral_conv(fast_block, slow_link, lateral))
        lat_act = low(smooth(normalize(lat_pre, slow_gains[0], slow_biases[0])))
        joined = jnp.concatenate([slow_block, lat_act], -1)
        slow_one = low_back(in_time(joined, slow_link, slow_time))
        short_pre = low_back(product(joined, projection))
        act_one = low(smooth(normalize(slow_one, slow_gains[1], slow_biases[1])))
        slow_two = low_back(in_space(act_one, slow_space))
        act_two = low(smooth(normalize(slow_two, slow_gains[2], slow_biases[2])))
        slow_three = low_back(product(act_two, slow_proj))
        slow_result = smooth(normalize(slow_three, slow_gains[3], slow_biases[3]) + normalize(short_pre, slow_gains[4], slow_biases[4]))
        fast_one = low_back(in_time(fast_block, fast_link, fast_time))
        fact_one = low(smooth(normalize(fast_one, fast_gains[0], fast_biases[0])))
        fast_two = low_back(in_space(fact_one, fast_space))
        fact_two = low(smooth(normalize(fast_two, fast_gains[1], fast_biases[1])))
        fast_three = low_back(product(fact_two, fast_proj))
        fast_result = smooth(normalize(fast_three, fast_gains[2], fast_biases[2]) + fast_block)
        slow_list.append(slow_result)
        fast_list.append(fast_result)
    return (jnp.stack(slow_list, 0), jnp.stack(fast_list, 0))

def reference(slow_in, fast_in, clip_starts, w_lateral, w_slow_time, w_slow_space, w_slow_out, w_projection, w_fast_time, w_fast_space, w_fast_out, slow_gain, slow_bias, fast_gain, fast_bias, slow_cotangent, fast_cotangent):
    params = [array.astype(jnp.float32) for array in (slow_in, fast_in, w_lateral, w_slow_time, w_slow_space, w_slow_out, w_projection, w_fast_time, w_fast_space, w_fast_out, slow_gain, slow_bias, fast_gain, fast_bias)]
    outputs, pull_back = jax.vjp(partial(forward, clip_starts), *params)
    grads = pull_back((slow_cotangent.astype(jnp.float32), fast_cotangent.astype(jnp.float32)))
    return (outputs[0].astype(jnp.bfloat16), outputs[1].astype(jnp.bfloat16), grads[0].astype(jnp.bfloat16), grads[1].astype(jnp.bfloat16), grads[2], grads[3], grads[4], grads[5], grads[6], grads[7], grads[8], grads[9], grads[10], grads[11], grads[12], grads[13])
```

```python
import jax
import jax.numpy as jnp
from jax import lax
from jax.sharding import PartitionSpec as P

CS = 1024
CL = 256
CM = 256
CF = 128
CFM = 32
HH = 14
WW = 14
PIX = HH * WW
ROWS = 208
EPS = 1e-05
AXES = ("path", "dp")
BF = jnp.bfloat16
F32 = jnp.float32


def swap(value, bit):
    count = lax.axis_size(AXES)
    return lax.ppermute(value, AXES, [(i, i ^ bit) for i in range(count)])


def dp_bits():
    count = lax.axis_size("dp")
    bits = []
    bit = 1
    while bit < count:
        bits.append(bit)
        bit *= 2
    return bits


def all_sum(value):
    value = value + swap(value, lax.axis_size("dp"))
    bits = dp_bits()
    while bits:
        if len(bits) == 1:
            value = value + swap(value, bits[0])
            bits = []
        else:
            one, two = bits[:2]
            first, second, third = swap(value, one), swap(value, two), swap(value, one + two)
            value = (value + first) + (second + third)
            bits = bits[2:]
    return value


def has_bit(bit):
    return (lax.axis_index(AXES) & bit) != 0


def gather_bits(value, bits):
    for bit in bits:
        other = swap(value, bit)
        value = jnp.where(
            has_bit(bit),
            jnp.concatenate([other, value], 0),
            jnp.concatenate([value, other], 0),
        )
    return value


def gather_small(value):
    return gather_bits(value[None], dp_bits() + [lax.axis_size("dp")])


def scatter_route(value, order):
    places = [lax.axis_size("dp")] + dp_bits()[::-1]
    for bit in order:
        dim = places.index(bit)
        low = lax.index_in_dim(value, 0, dim, False)
        high = lax.index_in_dim(value, 1, dim, False)
        mine = has_bit(bit)
        keep = jnp.where(mine, high, low)
        send = jnp.where(mine, low, high).astype(BF)
        value = keep.astype(F32) + swap(send, bit).astype(F32)
        places.remove(bit)
    return value


def scatter_sum(value):
    bits = dp_bits()
    path = lax.axis_size("dp")
    shaped = value.reshape((2,) * (len(bits) + 1) + value.shape[1:])
    low, high = bits[:2], bits[2:][::-1]
    rows = value.shape[1]
    cut = rows // 16 * 8
    if cut == 0:
        return scatter_route(shaped, [path] + low + high)
    one = scatter_route(shaped[..., :cut, :], [path] + low + high)
    two = scatter_route(shaped[..., cut:, :], [path] + low[::-1] + high)
    return jnp.concatenate([one, two], 0)


def from_before(value):
    count = lax.axis_size(AXES)
    return lax.ppermute(value, AXES, [(i, i + 1) for i in range(count - 1)])


def from_after(value):
    count = lax.axis_size(AXES)
    return lax.ppermute(value, AXES, [(i + 1, i) for i in range(count - 1)])


def gelu_parts(value):
    cubic = 0.7978845608028654 * (value + 0.044715 * (value * value * value))
    return jnp.tanh(cubic)


def gelu(value):
    return 0.5 * value * (1.0 + gelu_parts(value))


def gelu_slope(value):
    tan = gelu_parts(value)
    inner = 0.7978845608028654 * (1.0 + (3 * 0.044715) * (value * value))
    return 0.5 * (1.0 + tan) + 0.5 * value * (1.0 - tan * tan) * inner


def dot(left, right):
    return lax.dot_general(
        left, right, (((left.ndim - 1,), (0,)), ((), ())), preferred_element_type=F32
    )


def dot_t(left, right):
    return lax.dot_general(
        left, right, (((left.ndim - 1,), (1,)), ((), ())), preferred_element_type=F32
    )


def outer(left, right):
    return lax.dot_general(
        left.reshape(-1, left.shape[-1]),
        right.reshape(-1, right.shape[-1]),
        (((0,), (0,)), ((), ())),
        preferred_element_type=F32,
    )


def row_masks():
    row = lax.broadcasted_iota(jnp.int32, (1, ROWS, 1), 1)
    col = row % WW
    real = row < PIX
    return dict(
        real=real,
        left=real & (col != 0),
        right=real & (col != WW - 1),
        top=real & (row >= WW),
        bottom=row < PIX - WW,
    )


def roll(value, step, mask):
    return jnp.where(mask, jnp.roll(value, step, 1), 0)


def column_taps(value, masks):
    return jnp.concatenate(
        [roll(value, 1, masks["left"]), value, roll(value, -1, masks["right"])], -1
    )


def in_space(value, weight, masks):
    lanes = value.shape[-1]
    taps = dot(column_taps(value, masks), weight)
    return (
        roll(taps[..., :lanes], WW, masks["top"])
        + taps[..., lanes : 2 * lanes]
        + roll(taps[..., 2 * lanes :], -WW, masks["bottom"])
    )


def row_taps(value, masks):
    return jnp.concatenate(
        [roll(value, -WW, masks["bottom"]), value, roll(value, WW, masks["top"])], -1
    )


def space_back(taps, weight, masks):
    lanes = taps.shape[-1] // 3
    back = dot_t(taps, weight)
    return (
        roll(back[..., :lanes], -1, masks["right"])
        + back[..., lanes : 2 * lanes]
        + roll(back[..., 2 * lanes :], 1, masks["left"])
    )


def pad_rows(value):
    return jnp.pad(value, [(0, 0)] * (value.ndim - 2) + [(0, ROWS - PIX), (0, 0)])


def to_quads(value):
    micro, frames, _, lanes = value.shape
    quads = pad_rows(value).reshape(micro * frames // 4, 4, ROWS, lanes)
    return jnp.concatenate([quads[:, place] for place in range(4)], -1)


def from_quads(value, micro):
    lanes = value.shape[-1] // 4
    parts = [value[:, :PIX, place * lanes : (place + 1) * lanes] for place in range(4)]
    return jnp.stack(parts, 1).reshape(micro, -1, PIX, lanes)


def fold(vector):
    parts = vector.reshape(vector.shape[:-1] + (4, -1))
    return jnp.tile(jnp.sum(parts, -2), 4)


def sums_of(micro, *values):
    return jnp.concatenate(
        [jnp.sum(value.reshape((micro, -1) + value.shape[-1:]), 1) for value in values], -1
    )


def local(
    slow_in,
    fast_in,
    clip_starts,
    w_lateral,
    w_slow_time,
    w_slow_space,
    w_slow_out,
    w_projection,
    w_fast_time,
    w_fast_space,
    w_fast_out,
    slow_gain,
    slow_bias,
    fast_gain,
    fast_bias,
    slow_cotangent,
    fast_cotangent,
):
    devices = lax.axis_size(AXES)
    micro, frames = slow_in.shape[:2]
    groups = micro * frames
    masks = row_masks()
    real = masks["real"]
    slow_count = float(frames * PIX * devices)
    fast_count = 4.0 * slow_count

    edge_down = from_before(fast_in[:, -2:])
    edge_up = from_after(fast_in[:, :1])

    shards = [w_lateral, w_fast_time, w_fast_space, w_fast_out, slow_gain, slow_bias]
    small = jnp.concatenate(shards)
    small = gather_small(jnp.pad(small, (0, -small.shape[0] % 1024)))
    pieces = []
    at = 0
    for shard in shards:
        pieces.append(small[:, at : at + shard.shape[0]].reshape(-1))
        at += shard.shape[0]
    lateral = pieces[0].reshape(5 * CF, CL)
    fast_time = pieces[1].reshape(3, CF, CFM)
    fast_space = pieces[2].reshape(3, 3, CFM, CFM)
    fast_proj = pieces[3].reshape(CFM, CF)
    gains = pieces[4].astype(F32)
    biases = pieces[5].astype(F32)

    def gathered(shard, lanes):
        return lax.all_gather(shard.reshape(-1, lanes), AXES, axis=0, tiled=True)

    slow_time = gathered(w_slow_time, CM)
    slow_time = jnp.concatenate(
        [slow_time[tap * (CS + CL) : (tap + 1) * (CS + CL)] for tap in range(3)], -1
    )
    projection = gathered(w_projection, CS)
    space = gathered(w_slow_space, CM).reshape(3, 3, CM, CM)
    slow_space = jnp.concatenate(
        [jnp.concatenate([space[a, c] for a in range(3)], -1) for c in range(3)], 0
    )
    slow_proj = gathered(w_slow_out, CS)

    band = jnp.stack([jnp.eye(7, 4, -1 - k, dtype=BF) for k in range(3)], 0)
    fast_band = jnp.sum(
        band[:, :, None, :, None] * fast_time[:, None, :, None, :], 0, dtype=F32
    ).astype(BF).reshape(7 * CF, 4 * CFM)
    lat_band = jnp.concatenate([lateral, jnp.zeros((2 * CF, CL), BF)], 0)
    w_first = jnp.concatenate([lat_band, fast_band], -1)
    eye4 = jnp.eye(4, dtype=BF)
    fspace = (
        fast_space.transpose(1, 2, 0, 3)[:, None, :, :, None, :]
        * eye4[None, :, None, None, :, None]
    )
    fspace = fspace.reshape(3 * 4 * CFM, 3 * 4 * CFM)
    fproj = (fast_proj[None, :, None, :] * eye4[:, None, :, None]).reshape(4 * CFM, 4 * CF)

    def cut(vector, start, extent):
        return vector[start : start + extent][None, None]

    places = [(0, CL), (CL, CM), (CL + CM, CM), (CL + 2 * CM, CS), (CL + 2 * CM + CS, CS)]
    sg = [cut(gains, *place) for place in places]
    sb = [cut(biases, *place) for place in places]
    fg_all, fb_all = fast_gain.astype(F32), fast_bias.astype(F32)
    fg = [
        jnp.tile(part, 4)[None, None]
        for part in (fg_all[:CFM], fg_all[CFM : 2 * CFM], fg_all[2 * CFM :])
    ]
    fb = [
        jnp.tile(part, 4)[None, None]
        for part in (fb_all[:CFM], fb_all[CFM : 2 * CFM], fb_all[2 * CFM :])
    ]

    def spread(vector):
        return jnp.repeat(vector, frames, 0)[:, None]

    def split(total, extents):
        out = []
        start = 0
        for extent in extents:
            out.append(total[:, start : start + extent])
            start += extent
        return out

    def hat(value, first, second, count):
        mean = first / count
        scale = lax.rsqrt(second / count - mean * mean + EPS)
        scale = spread(scale)
        return (value - spread(mean)) * scale, scale

    def back(grad, normed, scale, gain, one, two, count):
        value = gain * scale * (grad - spread(one) / count - normed * (spread(two) / count))
        return jnp.where(real, value, 0).astype(BF)

    def shifted(value, edge, link):
        parts = value.reshape((micro, frames) + value.shape[1:])
        parts = jnp.concatenate([edge[:, None].astype(value.dtype), parts[:, :-1]], 1)
        return parts.reshape(value.shape) * link.astype(value.dtype)

    def ahead(value, edge, link):
        parts = value.reshape((micro, frames) + value.shape[1:])
        parts = jnp.concatenate([parts[:, 1:], edge[:, None].astype(value.dtype)], 1)
        return parts.reshape(value.shape) * link.astype(value.dtype)

    link = (1 - clip_starts).astype(F32)
    next_link = jnp.concatenate([link[:, 1:], from_after(link[:, :1])], 1)
    link = link.reshape(groups, 1, 1)
    next_link = next_link.reshape(groups, 1, 1)

    quads = to_quads(fast_in)
    edge_down = pad_rows(edge_down)
    edge_down = jnp.concatenate([edge_down[:, 0], edge_down[:, 1]], -1)
    edge_up = pad_rows(edge_up[:, 0])
    z = jnp.concatenate(
        [
            shifted(quads[..., 2 * CF :], edge_down, link),
            quads,
            ahead(quads[..., :CF], edge_up, next_link),
        ],
        -1,
    )
    first = dot(z, w_first)
    lat_pre, fone = first[..., :CL], first[..., CL:]
    total = all_sum(sums_of(micro, lat_pre, fone, lat_pre * lat_pre, fone * fone))
    s = split(total, [CL, 128, CL, 128])
    lat_hat, lat_scale = hat(lat_pre, s[0], s[2], slow_count)
    fone_hat, fone_scale = hat(fone, fold(s[1]), fold(s[3]), fast_count)

    lat_norm = lat_hat * sg[0] + sb[0]
    lat_act = jnp.where(real, gelu(lat_norm), 0).astype(BF)
    joined = jnp.concatenate([pad_rows(slow_in).reshape(groups, ROWS, CS), lat_act], -1)
    taps = dot(joined, slow_time)
    last = taps.reshape(micro, frames, ROWS, 3 * CM)[:, -1, :, :CM].astype(BF)
    head = taps.reshape(micro, frames, ROWS, 3 * CM)[:, 0, :, 2 * CM :].astype(BF)
    last = from_before(last)
    head = from_after(head)
    short = dot(joined, projection)
    fone_norm = fone_hat * fg[0] + fb[0]
    fact_one = jnp.where(real, gelu(fone_norm), 0).astype(BF)
    ftwo = in_space(fact_one, fspace, masks)
    slow_one = (
        shifted(taps[..., :CM], last, link)
        + taps[..., CM : 2 * CM]
        + ahead(taps[..., 2 * CM :], head, next_link)
    )
    total = all_sum(
        sums_of(micro, slow_one, short, ftwo, slow_one * slow_one, short * short, ftwo * ftwo)
    )
    s = split(total, [CM, CS, 128, CM, CS, 128])
    one_hat, one_scale = hat(slow_one, s[0], s[3], slow_count)
    short_hat, short_scale = hat(short, s[1], s[4], slow_count)
    ftwo_hat, ftwo_scale = hat(ftwo, fold(s[2]), fold(s[5]), fast_count)

    one_norm = one_hat * sg[1] + sb[1]
    act_one = jnp.where(real, gelu(one_norm), 0).astype(BF)
    slow_two = in_space(act_one, slow_space, masks)
    ftwo_norm = ftwo_hat * fg[1] + fb[1]
    fact_two = jnp.where(real, gelu(ftwo_norm), 0).astype(BF)
    fthree = dot(fact_two, fproj)
    total = all_sum(sums_of(micro, slow_two, fthree, slow_two * slow_two, fthree * fthree))
    s = split(total, [CM, 512, CM, 512])
    two_hat, two_scale = hat(slow_two, s[0], s[2], slow_count)
    fthree_hat, fthree_scale = hat(fthree, fold(s[1]), fold(s[3]), fast_count)

    two_norm = two_hat * sg[2] + sb[2]
    act_two = jnp.where(real, gelu(two_norm), 0).astype(BF)
    slow_three = dot(act_two, slow_proj)
    total = all_sum(sums_of(micro, slow_three, slow_three * slow_three))
    s = split(total, [CS, CS])
    three_hat, three_scale = hat(slow_three, s[0], s[1], slow_count)

    fast_total = fthree_hat * fg[2] + fb[2] + quads.astype(F32)
    fast_out = from_quads(gelu(fast_total).astype(BF), micro)
    fast_grad = gelu_slope(fast_total) * to_quads(fast_cotangent).astype(F32)
    slow_total = three_hat * sg[3] + sb[3] + (short_hat * sg[4] + sb[4])
    slow_out = gelu(slow_total).astype(BF)[:, :PIX].reshape(slow_in.shape)
    slow_grad = gelu_slope(slow_total) * pad_rows(slow_cotangent).reshape(
        groups, ROWS, CS
    ).astype(F32)
    total = all_sum(
        sums_of(
            micro,
            slow_grad,
            slow_grad * three_hat,
            slow_grad * short_hat,
            fast_grad,
            fast_grad * fthree_hat,
        )
    )
    s = split(total, [CS, CS, CS, 512, 512])
    sum_a = s
    d_three = back(slow_grad, three_hat, three_scale, sg[3], s[0], s[1], slow_count)
    d_short = back(slow_grad, short_hat, short_scale, sg[4], s[0], s[2], slow_count)
    d_fthree = back(
        fast_grad, fthree_hat, fthree_scale, fg[2], fold(s[3]), fold(s[4]), fast_count
    )

    grad_two = gelu_slope(two_norm) * dot_t(d_three, slow_proj)
    fgrad_two = gelu_slope(ftwo_norm) * dot_t(d_fthree, fproj)
    total = all_sum(sums_of(micro, grad_two, grad_two * two_hat, fgrad_two, fgrad_two * ftwo_hat))
    s = split(total, [CM, CM, 128, 128])
    sum_b = s
    d_two = back(grad_two, two_hat, two_scale, sg[2], s[0], s[1], slow_count)
    d_ftwo = back(fgrad_two, ftwo_hat, ftwo_scale, fg[1], fold(s[2]), fold(s[3]), fast_count)
    out_grad = outer(act_two, d_three)
    fout_grad = outer(fact_two, d_fthree)
    proj_grad = outer(joined, d_short)

    two_taps = row_taps(d_two, masks)
    ftwo_taps = row_taps(d_ftwo, masks)
    grad_one = gelu_slope(one_norm) * space_back(two_taps, slow_space, masks)
    fgrad_one = gelu_slope(fone_norm) * space_back(ftwo_taps, fspace, masks)
    total = all_sum(sums_of(micro, grad_one, grad_one * one_hat, fgrad_one, fgrad_one * fone_hat))
    s = split(total, [CM, CM, 128, 128])
    sum_c = s
    d_one = back(grad_one, one_hat, one_scale, sg[1], s[0], s[1], slow_count)
    d_fone = back(fgrad_one, fone_hat, fone_scale, fg[0], fold(s[2]), fold(s[3]), fast_count)
    space_grad = outer(column_taps(act_one, masks), two_taps)
    fspace_grad = outer(column_taps(fact_one, masks), ftwo_taps)

    ends = jnp.concatenate([d_one, d_fone], -1).reshape(micro, frames, ROWS, CM + 128)
    before = from_before(ends[:, -1])
    after = from_after(ends[:, 0])
    trio = jnp.concatenate(
        [
            ahead(d_one, after[..., :CM], next_link),
            d_one,
            shifted(d_one, before[..., :CM], link),
        ],
        -1,
    )
    joined_grad = dot_t(trio, slow_time) + dot_t(d_short, projection)
    time_grad = outer(joined, trio)
    slow_in_grad = joined_grad[:, :PIX, :CS].astype(BF).reshape(slow_in.shape)
    lat_grad = gelu_slope(lat_norm) * joined_grad[..., CS:]
    total = all_sum(sums_of(micro, lat_grad, lat_grad * lat_hat))
    s = split(total, [CL, CL])
    sum_d = s
    d_lat = back(lat_grad, lat_hat, lat_scale, sg[0], s[0], s[1], slow_count)

    lat_after = from_after(d_lat.reshape(micro, frames, ROWS, CL)[:, 0])
    lat_next = ahead(d_lat, lat_after, next_link)
    lane = lax.broadcasted_iota(jnp.int32, (1, 1, 128), 2)
    rim = jnp.where(lane >= 96, shifted(d_fone, before[..., CM:], link), 0) + jnp.where(
        lane < 32, ahead(d_fone, after[..., CM:], next_link), 0
    )
    ins = w_first.reshape(7, CF, CL + 128)
    own = ins[2:6].reshape(4 * CF, CL + 128)
    lat_prev = jnp.concatenate(
        [jnp.zeros((2 * CF, CL), BF), lateral[: 2 * CF]], 0
    )
    blank = jnp.zeros((CF, 32), BF)
    rim_rows = [
        jnp.concatenate([blank, blank, blank, fast_time[2]], -1),
        jnp.zeros((2 * CF, 128), BF),
        jnp.concatenate([fast_time[0], blank, blank, blank], -1),
    ]
    w_back = jnp.concatenate([own, lat_prev, jnp.concatenate(rim_rows, 0)], -1)
    firsts = jnp.concatenate([d_lat, d_fone, lat_next, rim], -1)
    quad_grad = fast_grad + dot_t(firsts, w_back)
    fast_in_grad = from_quads(quad_grad.astype(BF), micro)
    first_grad = outer(z, jnp.concatenate([d_lat, d_fone], -1))

    def shares(value):
        return value.reshape(devices, -1, value.shape[-1])

    def sent(value):
        return scatter_sum(shares(value)).reshape(-1)

    lateral_grad = first_grad[: 5 * CF, :CL]
    bands = first_grad[:, CL:].reshape(7, CF, 4, CFM)
    ftime_grad = jnp.stack(
        [sum(bands[q + 1 + k, :, q] for q in range(4)) for k in range(3)], 0
    )
    fs = fspace_grad.reshape(3, 4, CFM, 3, 4, CFM)
    fs = sum(fs[:, q, :, :, q] for q in range(4)).transpose(2, 0, 1, 3)
    fo = fout_grad.reshape(4, CFM, 4, CF)
    fo = sum(fo[q, :, q] for q in range(4))
    space_grad = space_grad.reshape(3, CM, 3, CM).transpose(2, 0, 1, 3).reshape(-1, CM)
    time_grad = time_grad.reshape(CS + CL, 3, CM).transpose(1, 0, 2).reshape(-1, CM)
    proj_out = sent(proj_grad)
    out_out = sent(out_grad)
    space_out = sent(space_grad)
    time_out = sent(time_grad)
    flat = [
        part.reshape(devices, -1) for part in (lateral_grad, ftime_grad, fs, fo)
    ]
    sizes = [part.shape[1] for part in flat]
    flat = jnp.concatenate(flat, 1)
    flat = jnp.pad(flat, ((0, 0), (0, -flat.shape[1] % 1024)))
    flat = scatter_sum(flat.reshape(devices, -1, 128)).reshape(-1)
    smalls = []
    at = 0
    for size in sizes:
        smalls.append(flat[at : at + size])
        at += size

    def both(value):
        return jnp.sum(value, 0)

    gain_grad = jnp.concatenate(
        [both(v) for v in (sum_d[1], sum_c[1], sum_b[1], sum_a[1], sum_a[2])]
    )
    bias_grad = jnp.concatenate(
        [both(v) for v in (sum_d[0], sum_c[0], sum_b[0], sum_a[0], sum_a[0])]
    )
    share = slow_gain.shape[0]
    start = lax.axis_index(AXES) * share
    fast_gain_grad = jnp.concatenate(
        [both(fold(sum_c[3]))[:CFM], both(fold(sum_b[3]))[:CFM], both(fold(sum_a[4]))[:CF]]
    )
    fast_bias_grad = jnp.concatenate(
        [both(fold(sum_c[2]))[:CFM], both(fold(sum_b[2]))[:CFM], both(fold(sum_a[3]))[:CF]]
    )
    return (
        slow_out,
        fast_out,
        slow_in_grad,
        fast_in_grad,
        smalls[0],
        time_out,
        space_out,
        out_out,
        proj_out,
        smalls[1],
        smalls[2],
        smalls[3],
        lax.dynamic_slice_in_dim(gain_grad, start, share),
        lax.dynamic_slice_in_dim(bias_grad, start, share),
        fast_gain_grad,
        fast_bias_grad,
    )


def solution(mesh):
    frames = P(None, AXES, None, None)
    flat = P(AXES)
    return jax.shard_map(
        local,
        mesh=mesh,
        in_specs=(frames, frames, P(None, AXES))
        + (flat,) * 10
        + (P(), P(), frames, frames),
        out_specs=(frames,) * 4 + (flat,) * 10 + (P(), P()),
        check_vma=False,
    )
```

```python
import functools
import math

import jax
import jax.numpy as jnp
import numpy as np
from jax import lax
from jax.experimental import pallas as pl
from jax.experimental.pallas import tpu as pltpu
from jax.sharding import PartitionSpec as P

CS = 1024
CL = 256
CM = 256
CF = 128
CFM = 32
HH = 14
WW = 14
PIX = HH * WW
ROWS = 208
EPS = 1e-05
AXES = ("path", "dp")
BF = jnp.bfloat16
F32 = jnp.float32


def swap(value, bit):
    count = lax.axis_size(AXES)
    return lax.ppermute(value, AXES, [(i, i ^ bit) for i in range(count)])


def dp_pairs():
    bits = []
    bit = 1
    while bit < lax.axis_size("dp"):
        bits.append(bit)
        bit *= 2
    return [bits[at : at + 2] for at in range(0, len(bits), 2)]


def all_sum(value):
    value = value + swap(value, lax.axis_size("dp"))
    for pair in dp_pairs():
        if len(pair) == 1:
            value = value + swap(value, pair[0])
        else:
            one, two = pair
            first, second, third = swap(value, one), swap(value, two), swap(value, one + two)
            value = (value + first) + (second + third)
    return value


def has_bit(bit):
    return (lax.axis_index(AXES) & bit) != 0


def in_order(parts, bits):
    parts = [part[None] for part in parts]
    step = 1
    for bit in bits:
        mine = has_bit(bit)
        parts = [jnp.where(mine, parts[k ^ step], parts[k]) for k in range(len(parts))]
        step *= 2
    return jnp.concatenate(parts, 0)


def gather_rows(value):
    shape = value.shape
    value = value[None]
    for pair in dp_pairs()[::-1]:
        whole = [value] + [swap(value, bit) for bit in pair]
        if len(pair) == 2:
            whole.append(swap(value, sum(pair)))
        stacked = in_order(whole, pair)
        value = jnp.swapaxes(stacked, 0, 1).reshape((-1,) + shape)
    path = lax.axis_size("dp")
    value = in_order([value, swap(value, path)], [path])
    return value.reshape((-1,) + shape)


class Shares:
    def __init__(self, value):
        self.value = value
        self.stages = [[lax.axis_size("dp")]] + dp_pairs()
        self.flight = None
        self.start()

    def start(self):
        if not self.stages:
            return
        bits = self.stages.pop(0)
        count = 2 ** len(bits)
        rest = self.value.shape[-2:]
        if bits[0] == lax.axis_size("dp"):
            shaped = self.value.reshape((2, -1) + rest)
            axis = 0
        else:
            shaped = self.value.reshape((-1, count) + rest)
            axis = 1
        spot = lax.axis_index(AXES) // bits[0] % count
        pick = lambda k: lax.dynamic_index_in_dim(shaped, spot ^ k, axis, False)
        self.keep = pick(0)
        steps = [sum(bit for n, bit in enumerate(bits) if k >> n & 1) for k in range(1, count)]
        self.flight = [swap(pick(k + 1).astype(BF), step) for k, step in enumerate(steps)]

    def finish(self):
        terms = [self.keep.astype(F32)] + [part.astype(F32) for part in self.flight]
        while len(terms) > 1:
            terms = [sum(terms[at : at + 2]) for at in range(0, len(terms), 2)]
        self.value = terms[0]
        self.flight = None
        self.start()

    def result(self):
        while self.flight is not None:
            self.finish()
        return self.value.reshape(-1)


def tie(flows, *values):
    flows = [flow for flow in flows if flow.flight is not None]
    values, flights = lax.optimization_barrier((values, [flow.flight for flow in flows]))
    for flow, flight in zip(flows, flights):
        flow.flight = flight
        flow.finish()
    return values if len(values) > 1 else values[0]


def from_before(value):
    count = lax.axis_size(AXES)
    return lax.ppermute(value, AXES, [(i, i + 1) for i in range(count - 1)])


def from_after(value):
    count = lax.axis_size(AXES)
    return lax.ppermute(value, AXES, [(i + 1, i) for i in range(count - 1)])


def gelu_tan(value):
    return jnp.tanh(value * (0.7978845608028654 + 0.035677408136300125 * (value * value)))


def gelu(value):
    return value * (0.5 + 0.5 * gelu_tan(value))


def gelu_slope(value):
    tan = gelu_tan(value)
    inner = 0.7978845608028654 + 0.10703222440890037 * (value * value)
    return (0.5 + 0.5 * tan) + (0.5 * value) * (1.0 - tan * tan) * inner


def pad_rows(value):
    return jnp.pad(value, [(0, 0)] * (value.ndim - 2) + [(0, ROWS - PIX), (0, 0)])


def to_quads(value):
    micro, frames, _, lanes = value.shape
    quads = pad_rows(value).reshape(micro * frames // 4, 4, ROWS, lanes)
    return jnp.concatenate([quads[:, place] for place in range(4)], -1)


LIMIT = 58 * 1024 * 1024


def call(body, steps, ins, outs, scratch=(), flops=0, name=None):
    in_specs = []
    for _, block, index in ins:
        if block is None:
            in_specs.append(pl.BlockSpec(memory_space=pltpu.SMEM))
        else:
            in_specs.append(pl.BlockSpec(block, index))
    moved = sum(array.size * array.dtype.itemsize for array, _, _ in ins)
    moved += sum(math.prod(shape) * jnp.dtype(dtype).itemsize for shape, dtype, _, _ in outs)
    return pl.pallas_call(
        body,
        grid=(steps,),
        in_specs=in_specs,
        out_specs=[pl.BlockSpec(block, index) for _, _, block, index in outs],
        out_shape=[jax.ShapeDtypeStruct(shape, dtype) for shape, dtype, _, _ in outs],
        scratch_shapes=list(scratch),
        compiler_params=pltpu.CompilerParams(
            dimension_semantics=("arbitrary",), vmem_limit_bytes=LIMIT
        ),
        cost_estimate=pl.CostEstimate(
            flops=int(flops), bytes_accessed=int(moved), transcendentals=0
        ),
        name=name,
    )(*[array for array, _, _ in ins])


def group(array, per):
    tail = (0,) * (array.ndim - 1)
    return (array, (per,) + array.shape[1:], lambda g: (g,) + tail)


def whole(array):
    zeros = (0,) * array.ndim
    return (array, array.shape, lambda g: zeros)


def scalar(array):
    return (array, None, None)


def stream(array, steps):
    tail = (0,) * (array.ndim - 1)
    return (array, (1,) + array.shape[1:], lambda g: (g // steps,) + tail)


def out_group(shape, dtype, per):
    tail = (0,) * (len(shape) - 1)
    return (shape, dtype, (per,) + shape[1:], lambda g: (g,) + tail)


def out_stream(shape, dtype, steps):
    tail = (0,) * (len(shape) - 1)
    return (shape, dtype, (1,) + shape[1:], lambda g: (g // steps,) + tail)


def rows_of(ref):
    return ref[...].reshape(-1, ref.shape[-1])


def put(ref, value):
    ref[...] = value.reshape(ref.shape).astype(ref.dtype)


def spread(value, mask):
    lanes = value.shape[-1]
    shaped = value.reshape(-1, ROWS, lanes) * mask[None, :, :lanes]
    return shaped.reshape(value.shape)


def add_rows(ref, steps, lanes, *values):
    first = pl.program_id(0) % steps == 0
    for row, value in enumerate(values):
        total = jnp.sum(value, 0, keepdims=True)
        spot = (0, slice(row, row + 1), slice(lanes, lanes + value.shape[-1]))
        if steps > 1:
            total = jnp.where(first, 0.0, ref[spot]) + total
        ref[spot] = total


def stats(total, start, extent, count, folded=0):
    first = total[0, 0:1, start : start + extent]
    second = total[0, 1:2, start : start + extent]
    if folded:
        first, second = fold_lanes(first, folded), fold_lanes(second, folded)
    mean = first / count
    return mean, lax.rsqrt(second / count - mean * mean + EPS)


def fold_lanes(vector, width):
    lanes = vector.shape[-1]
    if width % 128 == 0:
        parts = [vector[:, at : at + width] for at in range(0, lanes, width)]
        one = (parts[0] + parts[1]) + (parts[2] + parts[3])
        return jnp.concatenate([one] * 4, -1)
    wide = jnp.broadcast_to(vector, (8, lanes))
    wide = wide + pltpu.roll(wide, 2 * width, 1)
    wide = wide + pltpu.roll(wide, width, 1)
    return wide[0:1]


def back_parts(sums, start, extent, count, folded=0, rows=(0, 1)):
    one = sums[0, rows[0] : rows[0] + 1, start : start + extent]
    two = sums[0, rows[1] : rows[1] + 1, start : start + extent]
    if folded:
        one, two = fold_lanes(one, folded), fold_lanes(two, folded)
    return one / count, two / count


def norm_back(grad, hat, factor, one, two):
    return factor * (grad - one - hat * two)


def turn(value, step):
    return pltpu.roll(value, step % value.shape[0], 0)


def mul(left, right):
    return jnp.dot(left, right, preferred_element_type=F32)


def mul_t(left, right):
    return lax.dot_general(left, right, (((1,), (1,)), ((), ())), preferred_element_type=F32)


def mul_rows(left, right):
    return lax.dot_general(
        rows_of(left), rows_of(right), (((0,), (0,)), ((), ())), preferred_element_type=F32
    )


def column_cat(act, masks):
    act = act.astype(BF).astype(F32)
    left = spread(turn(act, 1), masks[1])
    right = spread(turn(act, -1), masks[2])
    return jnp.concatenate([left.astype(BF), act.astype(BF), right.astype(BF)], -1)


def row_sum(taps, masks):
    lanes = taps.shape[-1] // 3
    return (
        spread(turn(taps[:, :lanes], WW), masks[3])
        + taps[:, lanes : 2 * lanes]
        + spread(turn(taps[:, 2 * lanes :], -WW), masks[4])
    )


def row_cat(grad, masks):
    grad = grad.astype(BF).astype(F32)
    above = spread(turn(grad, -WW), masks[4])
    below = spread(turn(grad, WW), masks[3])
    return jnp.concatenate([above.astype(BF), grad.astype(BF), below.astype(BF)], -1)


def column_sum(taps, masks):
    lanes = taps.shape[-1] // 3
    return (
        spread(turn(taps[:, :lanes], -1), masks[2])
        + taps[:, lanes : 2 * lanes]
        + spread(turn(taps[:, 2 * lanes :], 1), masks[1])
    )


def k_first(z, weight, lat, fone, total, *, steps):
    value = mul(rows_of(z), weight[...])
    put(lat, value[:, :CL])
    put(fone, value[:, CL:])
    add_rows(total, steps, 0, value, value * value)


def k_taps(links, lat, total, gb, slow, w_time, masks, lat_act, taps, tail, head, *, count):
    frames = slow.shape[0]
    mean, scale = stats(total, 0, CL, count)
    hat = (rows_of(lat) - mean) * scale
    act = spread(gelu(hat * gb[0:1, :CL] + gb[1:2, :CL]), masks[0]).astype(BF)
    put(lat_act, act)
    value = mul(rows_of(slow), w_time[:CS]) + mul(act, w_time[CS:])
    put(taps, value)
    tail[0] = value[(frames - 1) * ROWS :, :CM].astype(BF)
    head[0] = (links[pl.program_id(0) * frames] * value[:ROWS, 2 * CM :]).astype(BF)


def k_short(
    slow, lat_act, w_proj, fone, total, fgb, fspace, masks, short, fact, ftwo, sums, *, steps, count
):
    value = mul(rows_of(slow), w_proj[:CS]) + mul(rows_of(lat_act), w_proj[CS:])
    put(short, value)
    add_rows(sums, steps, 0, value, value * value)
    mean, scale = stats(total, CL, 128, 4.0 * count, CFM)
    hat = (rows_of(fone) - mean) * scale
    act = spread(gelu(hat * fgb[0:1, :128] + fgb[1:2, :128]), masks[0])
    cat = column_cat(act, masks)
    put(fact, cat)
    value = row_sum(mul(cat, fspace[...]), masks)
    put(ftwo, value)
    add_rows(sums, steps, CS, value, value * value)


def k_one(links, nexts, taps, rim_before, rim_after, given, slow_one, sums):
    frames = taps.shape[0]
    base = pl.program_id(0) * frames
    one = two = 0.0
    for f in range(frames):
        prev = rim_before[0].astype(F32) if f == 0 else taps[f - 1, :, :CM]
        follow = rim_after[0].astype(F32) if f == frames - 1 else taps[f + 1, :, 2 * CM :]
        value = links[base + f] * prev + taps[f, :, CM : 2 * CM] + nexts[base + f] * follow
        slow_one[f] = value
        one += jnp.sum(value, 0, keepdims=True)
        two += jnp.sum(value * value, 0, keepdims=True)
    sums[0, :, : CS + 128] = given[0]
    sums[0, 0:1, CS + 128 :] = one
    sums[0, 1:2, CS + 128 :] = two


def k_two(
    slow_one, ftwo, total, gb, fgb, w_space, fproj, masks,
    cat_out, two_out, fact_out, fthree, sums, *, steps, count
):
    mean, scale = stats(total, CS + 128, CM, count)
    hat = (rows_of(slow_one) - mean) * scale
    act = spread(gelu(hat * gb[0:1, CL : 2 * CL] + gb[1:2, CL : 2 * CL]), masks[0])
    cat = column_cat(act, masks)
    put(cat_out, cat)
    value = row_sum(mul(cat, w_space[...]), masks)
    put(two_out, value)
    add_rows(sums, steps, 0, value, value * value)
    mean, scale = stats(total, CS, 128, 4.0 * count, CFM)
    hat = (rows_of(ftwo) - mean) * scale
    act = spread(gelu(hat * fgb[0:1, 128:256] + fgb[1:2, 128:256]), masks[0]).astype(BF)
    put(fact_out, act)
    value = mul(act, fproj[...])
    put(fthree, value)
    add_rows(sums, steps, CM, value, value * value)


def k_three(slow_two, total, gb, w_out, masks, act_out, sums, *, steps, count):
    mean, scale = stats(total, 0, CM, count)
    hat = (rows_of(slow_two) - mean) * scale
    act = gelu(hat * gb[0:1, 2 * CL : 3 * CL] + gb[1:2, 2 * CL : 3 * CL])
    act = spread(act, masks[0]).astype(BF)
    put(act_out, act)
    value = mul(act, w_out[...])
    add_rows(sums, steps, 0, value, value * value)


CHUNK = 16
SPAN = 512


def gelu_both(value):
    square = value * value
    tan = jnp.tanh(value * (0.7978845608028654 + 0.035677408136300125 * square))
    half = 0.5 + 0.5 * tan
    inner = 0.7978845608028654 + 0.10703222440890037 * square
    slope = half + (0.5 * value) * (1.0 - tan * tan) * inner
    return value * half, slope


def chunked(body, frames, lanes):
    full = PIX // CHUNK
    last = full * CHUNK

    def frame(f, carry):
        def step(i, carry):
            at = pl.ds(pl.multiple_of(i * CHUNK, CHUNK), CHUNK)
            for start in range(0, lanes, SPAN):
                body(f, at, CHUNK, slice(start, start + SPAN))
            return carry

        lax.fori_loop(0, full, step, 0)
        for start in range(0, lanes, SPAN):
            body(f, pl.ds(last, CHUNK), PIX - last, slice(start, start + SPAN))
        return carry

    lax.fori_loop(0, frames, frame, 0)


def halves(value):
    return value[:8] + value[8:]


def k_fast_out(fthree, quads, cot, total, fgb, out, grad, sums, acc, *, steps, count):
    mean, scale = stats(total, CM, 4 * CF, 4.0 * count, CF)
    gain, bias = fgb[0:1, 256:], fgb[1:2, 256:]

    @pl.when(pl.program_id(0) % steps == 0)
    def _():
        acc[...] = jnp.zeros_like(acc)

    def body(f, rows, real, lanes):
        hat = (fthree[f, rows, lanes] - mean[:, lanes]) * scale[:, lanes]
        value = hat * gain[:, lanes] + bias[:, lanes] + quads[f, rows, lanes].astype(F32)
        act, slope = gelu_both(value)
        act = act.astype(BF)
        for q in range(4):
            piece = act[:real, q * CF : (q + 1) * CF]
            out[f, q, pl.ds(rows.start, real), :] = piece
        slope = slope * cot[f, rows, lanes].astype(F32)
        grad[f, rows, lanes] = slope
        acc[0] += halves(slope)
        acc[1] += halves(slope * hat)

    chunked(body, fthree.shape[0], 4 * CF)

    @pl.when(pl.program_id(0) % steps == steps - 1)
    def _():
        for row in range(2):
            sums[0, row : row + 1] = jnp.sum(acc[row], 0, keepdims=True)


def k_out(
    act, w_out, short, cot, total, short_total, gb, given, out, grad_out, sums, three, acc,
    *, steps, count
):
    three[...] = mul(rows_of(act), w_out[...]).reshape(three.shape)
    mean_a, scale_a = stats(total, 0, CS, count)
    mean_b, scale_b = stats(short_total, 0, CS, count)
    gain_a, gain_b = gb[0:1, 768:1792], gb[0:1, 1792:]
    bias = gb[1:2, 768:1792] + gb[1:2, 1792:]

    @pl.when(pl.program_id(0) % steps == 0)
    def _():
        acc[...] = jnp.zeros_like(acc)

    def body(f, rows, real, lanes):
        hat_a = (three[f, rows, lanes] - mean_a[:, lanes]) * scale_a[:, lanes]
        hat_b = (short[f, rows, lanes] - mean_b[:, lanes]) * scale_b[:, lanes]
        value = hat_a * gain_a[:, lanes] + (hat_b * gain_b[:, lanes] + bias[:, lanes])
        smooth, slope = gelu_both(value)
        out[f, pl.ds(rows.start, real), lanes] = smooth.astype(BF)[:real]
        grad = slope * cot[f, rows, lanes].astype(F32)
        grad_out[f, rows, lanes] = grad
        acc[0, :, lanes] += halves(grad)
        acc[1, :, lanes] += halves(grad * hat_a)
        acc[2, :, lanes] += halves(grad * hat_b)

    chunked(body, act.shape[0], CS)

    @pl.when(pl.program_id(0) % steps == steps - 1)
    def _():
        for row in range(3):
            sums[0, row : row + 1, :CS] = jnp.sum(acc[row], 0, keepdims=True)
        sums[0, 0:2, CS:] = given[0]
        sums[0, 2:3, CS:] = jnp.zeros((1, 4 * CF), F32)


def k_back_three(
    act, w_out, short, grad, total, short_total, sums, gb, slow_two, total3,
    fgrad, fthree, ftwo, fgb, fproj, masks,
    d_three, d_short, grad_two, d_fthree, fgrad_two, sums_out, three, *, steps, count
):
    three[...] = mul(rows_of(act), w_out[...]).reshape(three.shape)
    mean_a, scale_a = stats(total, 0, CS, count)
    mean_b, scale_b = stats(short_total, 0, CS, count)
    one, two_a = back_parts(sums, 0, CS, count)
    _, two_b = back_parts(sums, 0, CS, count, rows=(0, 2))
    factor_a = gb[0:1, 768:1792] * scale_a
    factor_b = gb[0:1, 1792:] * scale_b

    def body(f, rows, real, lanes):
        given = grad[f, rows, lanes] - one[:, lanes]
        hat_a = (three[f, rows, lanes] - mean_a[:, lanes]) * scale_a[:, lanes]
        hat_b = (short[f, rows, lanes] - mean_b[:, lanes]) * scale_b[:, lanes]
        value_a = factor_a[:, lanes] * (given - hat_a * two_a[:, lanes])
        value_b = factor_b[:, lanes] * (given - hat_b * two_b[:, lanes])
        if real < CHUNK:
            row = lax.broadcasted_iota(jnp.int32, value_a.shape, 0)
            value_a = jnp.where(row < real, value_a, 0.0)
            value_b = jnp.where(row < real, value_b, 0.0)
        d_three[f, rows, lanes] = value_a.astype(BF)
        d_short[f, rows, lanes] = value_b.astype(BF)

    chunked(body, act.shape[0], CS)
    mean, scale = stats(total3, 0, CM, count)
    hat = (rows_of(slow_two) - mean) * scale
    slope = gelu_slope(hat * gb[0:1, 2 * CL : 3 * CL] + gb[1:2, 2 * CL : 3 * CL])
    value = slope * mul_t(rows_of(d_three), w_out[...])
    put(grad_two, value)
    add_rows(sums_out, steps, 0, value, value * hat)

    mean, scale = stats(total3, CM, 4 * CF, 4.0 * count, CF)
    one, two = back_parts(sums, CS, 4 * CF, 4.0 * count, CF)
    hat = (rows_of(fthree) - mean) * scale
    value = norm_back(rows_of(fgrad), hat, fgb[0:1, 256:] * scale, one, two)
    lanes = value.shape[-1]
    row = lax.broadcasted_iota(jnp.int32, (1, ROWS, lanes), 1)
    value = jnp.where(row < PIX, value.reshape(-1, ROWS, lanes), 0.0)
    value = value.reshape(-1, lanes).astype(BF)
    put(d_fthree, value)
    mean, scale = stats(short_total, CS, 128, 4.0 * count, CFM)
    hat = (rows_of(ftwo) - mean) * scale
    slope = gelu_slope(hat * fgb[0:1, 128:256] + fgb[1:2, 128:256])
    value = slope * mul_t(value, fproj[...])
    put(fgrad_two, value)
    add_rows(sums_out, steps, CM, value, value * hat)


def k_back_two(
    slow_two, total3, grad_two, sums, gb, w_space, slow_one, total2,
    ftwo, fgrad_two, fgb, fspace, fone, total1, masks,
    taps_out, grad_one, ftaps_out, fgrad_one, sums_out, *, steps, count
):
    mean, scale = stats(total3, 0, CM, count)
    one, two = back_parts(sums, 0, CM, count)
    hat = (rows_of(slow_two) - mean) * scale
    value = norm_back(rows_of(grad_two), hat, gb[0:1, 2 * CL : 3 * CL] * scale, one, two)
    cat = row_cat(spread(value, masks[0]), masks)
    put(taps_out, cat)
    value = column_sum(mul_t(cat, w_space[...]), masks)
    mean, scale = stats(total2, CS + 128, CM, count)
    hat = (rows_of(slow_one) - mean) * scale
    value = gelu_slope(hat * gb[0:1, CL : 2 * CL] + gb[1:2, CL : 2 * CL]) * value
    put(grad_one, value)
    add_rows(sums_out, steps, 0, value, value * hat)

    mean, scale = stats(total2, CS, 128, 4.0 * count, CFM)
    one, two = back_parts(sums, CM, 128, 4.0 * count, CFM)
    hat = (rows_of(ftwo) - mean) * scale
    value = norm_back(rows_of(fgrad_two), hat, fgb[0:1, 128:256] * scale, one, two)
    cat = row_cat(spread(value, masks[0]), masks)
    put(ftaps_out, cat)
    value = column_sum(mul_t(cat, fspace[...]), masks)
    mean, scale = stats(total1, CL, 128, 4.0 * count, CFM)
    hat = (rows_of(fone) - mean) * scale
    value = gelu_slope(hat * fgb[0:1, :128] + fgb[1:2, :128]) * value
    put(fgrad_one, value)
    add_rows(sums_out, steps, CM, value, value * hat)


def k_back_one(
    links, slow_one, total2, grad_one, fone, total1, fgrad_one, sums, gb, fgb, masks,
    d_one, d_fone, tail, head, *, count
):
    frames = slow_one.shape[0]
    mean, scale = stats(total2, CS + 128, CM, count)
    one, two = back_parts(sums, 0, CM, count)
    hat = (rows_of(slow_one) - mean) * scale
    value = norm_back(rows_of(grad_one), hat, gb[0:1, CL : 2 * CL] * scale, one, two)
    value = spread(value, masks[0])
    put(d_one, value)
    mean, scale = stats(total1, CL, 128, 4.0 * count, CFM)
    one, two = back_parts(sums, CM, 128, 4.0 * count, CFM)
    hat = (rows_of(fone) - mean) * scale
    fvalue = norm_back(rows_of(fgrad_one), hat, fgb[0:1, :128] * scale, one, two)
    fvalue = spread(fvalue, masks[0])
    put(d_fone, fvalue)
    last = (frames - 1) * ROWS
    tail[0, :, :CM] = value[last:].astype(BF)
    tail[0, :, CM:] = fvalue[last:].astype(BF)
    link = links[pl.program_id(0) * frames]
    head[0, :, :CM] = (link * value[:ROWS]).astype(BF)
    head[0, :, CM:] = (link * fvalue[:ROWS]).astype(BF)


def k_trio(
    links, nexts, d_one, rim_before, rim_after, d_short, w_time, w_proj, lat, total1, gb,
    trio, grad, sums, *, count
):
    frames = d_one.shape[0]
    base = pl.program_id(0) * frames
    for f in range(frames):
        prev = rim_before[0, :, :CM] if f == 0 else d_one[f - 1]
        follow = rim_after[0, :, :CM] if f == frames - 1 else d_one[f + 1]
        trio[f, :, :CM] = (nexts[base + f] * follow.astype(F32)).astype(BF)
        trio[f, :, CM : 2 * CM] = d_one[f]
        trio[f, :, 2 * CM :] = (links[base + f] * prev.astype(F32)).astype(BF)
    value = mul_t(rows_of(trio), w_time[...]) + mul_t(rows_of(d_short), w_proj[...])
    mean, scale = stats(total1, 0, CL, count)
    hat = (rows_of(lat) - mean) * scale
    value = gelu_slope(hat * gb[0:1, :CL] + gb[1:2, :CL]) * value
    put(grad, value)
    add_rows(sums, 1, 0, value, value * hat)


def k_slow_grad(trio, d_short, w_time, w_proj, out):
    value = mul_t(rows_of(trio), w_time[...]) + mul_t(rows_of(d_short), w_proj[...])
    out[...] = value.reshape(-1, ROWS, CS)[:, :PIX].astype(BF)


def k_back_lat(links, lat, total1, grad, sums, gb, masks, d_lat, head, *, count):
    frames = lat.shape[0]
    mean, scale = stats(total1, 0, CL, count)
    one, two = back_parts(sums, 0, CL, count)
    hat = (rows_of(lat) - mean) * scale
    value = norm_back(rows_of(grad), hat, gb[0:1, :CL] * scale, one, two)
    value = spread(value, masks[0])
    put(d_lat, value)
    head[0] = (links[pl.program_id(0) * frames] * value[:ROWS]).astype(BF)


def k_fast_grad(
    links, nexts, fgrad, d_lat, lat_rim, d_fone, rim_before, rim_after, w_back, out, cat
):
    frames = d_lat.shape[0]
    base = pl.program_id(0) * frames
    for f in range(frames):
        last = f == frames - 1
        follow = lat_rim[0] if last else d_lat[f + 1]
        prev_f = rim_before[0, :, CM:] if f == 0 else d_fone[f - 1]
        next_f = rim_after[0, :, CM:] if last else d_fone[f + 1]
        lane = lax.broadcasted_iota(jnp.int32, prev_f.shape, 1)
        rim = jnp.where(lane >= 96, links[base + f] * prev_f.astype(F32), 0.0)
        rim += jnp.where(lane < 32, nexts[base + f] * next_f.astype(F32), 0.0)
        cat[f, :, :CL] = d_lat[f]
        cat[f, :, CL : CL + 128] = d_fone[f]
        cat[f, :, CL + 128 : 2 * CL + 128] = (nexts[base + f] * follow.astype(F32)).astype(BF)
        cat[f, :, 2 * CL + 128 :] = rim.astype(BF)
    value = rows_of(fgrad) + mul_t(rows_of(cat), w_back[...])
    value = value.reshape(-1, ROWS, 4 * CF)
    for q in range(4):
        out[:, q] = value[:, :PIX, q * CF : (q + 1) * CF].astype(BF)


def k_outer_joined(slow, lat, right, out, *, parts, taps):
    def fill(left):
        value = mul_rows(left, right)
        if taps == 1:
            out[...] = value
        else:
            for tap in range(taps):
                out[tap] = value[:, tap * CM : (tap + 1) * CM]

    pl.when(pl.program_id(0) < parts)(lambda: fill(slow))
    pl.when(pl.program_id(0) >= parts)(lambda: fill(lat))


def outer_joined(slow, lat, right, taps, name):
    wide = 256
    parts = slow.shape[-1] // wide
    block = slow.shape[:2] + (wide,)
    rows, lanes = slow.shape[-1] + lat.shape[-1], right.shape[-1]
    if taps == 1:
        out = ((rows, lanes), F32, (wide, lanes), lambda g: (g, 0))
    else:
        out = ((taps, rows, CM), F32, (taps, wide, CM), lambda g: (0, g, 0))
    return call(
        functools.partial(k_outer_joined, parts=parts, taps=taps),
        rows // wide,
        [
            (slow, block, lambda g: (0, 0, jnp.minimum(g, parts - 1))),
            (lat, block, lambda g: (0, 0, 0)),
            whole(right),
        ],
        [out],
        flops=2 * slow.shape[0] * slow.shape[1] * rows * lanes,
        name=name,
    )[0]


def k_outer_out(left, right, fleft, fright, out, fout):
    out[...] = mul_rows(left, right)
    fout[...] = mul_rows(fleft, fright)


def k_outer_space(left, right, fleft, fright, out, fout):
    value = mul_rows(left, right)
    for a in range(3):
        out[a, 0] = value[:, a * CM : (a + 1) * CM]

    @pl.when(pl.program_id(0) == 2)
    def _():
        fout[...] = mul_rows(fleft, fright)


def k_outer_first(z, d_lat, d_fone, out):
    out[:, :CL] = mul_rows(z, d_lat)
    out[:, CL:] = mul_rows(z, d_fone)


def mask_table():
    row = np.arange(ROWS)
    col = row % WW
    real = row < PIX
    table = [real, real & (col != 0), real & (col != WW - 1), real & (row >= WW), row < PIX - WW]
    return np.broadcast_to(np.stack(table)[:, :, None], (5, ROWS, CM)).astype(np.float32)


def frame_fold(value, width, height):
    return sum(
        value[q * height : (q + 1) * height, q * width : (q + 1) * width] for q in range(4)
    )


def local(
    slow_in,
    fast_in,
    clip_starts,
    w_lateral,
    w_slow_time,
    w_slow_space,
    w_slow_out,
    w_projection,
    w_fast_time,
    w_fast_space,
    w_fast_out,
    slow_gain,
    slow_bias,
    fast_gain,
    fast_bias,
    slow_cotangent,
    fast_cotangent,
):
    devices = lax.axis_size(AXES)
    micro, frames = slow_in.shape[:2]
    groups = micro * frames
    masks = jnp.asarray(mask_table())
    count = float(frames * PIX * devices)

    link = (1 - clip_starts).astype(F32)
    links = link.reshape(groups)
    nexts = jnp.concatenate([link[:, 1:], jnp.ones((micro, 1), F32)], 1).reshape(groups)
    edge_down = from_before(fast_in[:, -2:])
    edge_up = from_after(fast_in[:, :1] * link[:, :1, None, None].astype(BF))

    wide = jnp.concatenate(
        [w_projection.reshape(-1, CS), w_slow_out.reshape(-1, CS), w_slow_space.reshape(-1, CS)]
        if w_slow_space.shape[0] % CS == 0
        else [w_projection, w_slow_out, w_slow_space],
        0,
    )
    cuts = [w_projection.shape[0], w_slow_out.shape[0], w_slow_space.shape[0]]
    if wide.ndim == 2:
        cuts = [extent // CS for extent in cuts]
    wide = lax.all_gather(wide, AXES, axis=0, tiled=False)
    projection = wide[:, : cuts[0]].reshape(CS + CL, CS)
    slow_proj = wide[:, cuts[0] : cuts[0] + cuts[1]].reshape(CM, CS)
    space = wide[:, cuts[0] + cuts[1] :].reshape(3, 3, CM, CM)
    slow_space = jnp.concatenate(
        [jnp.concatenate([space[a, c] for a in range(3)], -1) for c in range(3)], 0
    )

    shards = [w_fast_time, w_fast_space, w_fast_out, slow_gain, slow_bias]
    if w_lateral.shape[0] % CM:
        shards = [w_lateral] + shards
    small = jnp.concatenate(shards)
    small = jnp.pad(small, (0, -small.shape[0] % CM)).reshape(-1, CM)
    time_rows = w_slow_time.shape[0] // CM
    lat_rows = w_lateral.shape[0] // CM if len(shards) == 5 else 0
    near = [w_slow_time.reshape(-1, CM)]
    if lat_rows:
        near.append(w_lateral.reshape(-1, CM))
    near = gather_rows(jnp.concatenate(near + [small], 0))
    slow_time = near[:, :time_rows].reshape(3, CS + CL, CM)
    slow_time = jnp.concatenate([slow_time[tap] for tap in range(3)], -1)
    small = near[:, time_rows + lat_rows :].reshape(devices, -1)
    pieces = []
    at = 0
    for shard in shards:
        pieces.append(small[:, at : at + shard.shape[0]].reshape(-1))
        at += shard.shape[0]
    if lat_rows:
        pieces = [near[:, time_rows : time_rows + lat_rows]] + pieces
    lateral = pieces[0].reshape(5 * CF, CL)
    fast_time = pieces[1].reshape(3, CF, CFM)
    fast_space = pieces[2].reshape(3, 3, CFM, CFM)
    fast_proj = pieces[3].reshape(CFM, CF)
    gb = jnp.stack([pieces[4], pieces[5]]).astype(F32)
    fast_both = jnp.stack([fast_gain, fast_bias]).astype(F32)
    fgb = jnp.concatenate(
        [
            jnp.tile(part, (1, 4))
            for part in (fast_both[:, :CFM], fast_both[:, CFM : 2 * CFM], fast_both[:, 2 * CFM :])
        ],
        1,
    )

    band = jnp.stack([jnp.eye(7, 4, -1 - k, dtype=BF) for k in range(3)], 0)
    fast_band = jnp.sum(
        band[:, :, None, :, None] * fast_time[:, None, :, None, :], 0, dtype=F32
    ).astype(BF).reshape(7 * CF, 4 * CFM)
    lat_band = jnp.concatenate([lateral, jnp.zeros((2 * CF, CL), BF)], 0)
    w_first = jnp.concatenate([lat_band, fast_band], -1)
    eye4 = jnp.eye(4, dtype=BF)
    fspace = (
        fast_space.transpose(1, 2, 0, 3)[:, None, :, :, None, :]
        * eye4[None, :, None, None, :, None]
    )
    fspace = fspace.reshape(3 * 4 * CFM, 3 * 4 * CFM)
    fproj = (fast_proj[None, :, None, :] * eye4[:, None, :, None]).reshape(4 * CFM, 4 * CF)
    own = w_first[2 * CF : 6 * CF]
    lat_prev = jnp.concatenate([jnp.zeros((2 * CF, CL), BF), lateral[: 2 * CF]], 0)
    blank = jnp.zeros((CF, 3 * CFM), BF)
    rim_rows = jnp.concatenate(
        [
            jnp.concatenate([blank, fast_time[2]], -1),
            jnp.zeros((2 * CF, 4 * CFM), BF),
            jnp.concatenate([fast_time[0], blank], -1),
        ],
        0,
    )
    w_back = jnp.concatenate([own, lat_prev, rim_rows], -1)

    slow = pad_rows(slow_in).reshape(groups, ROWS, CS)
    cot = pad_rows(slow_cotangent).reshape(groups, ROWS, CS)
    quads = to_quads(fast_in)
    fcot = to_quads(fast_cotangent)

    def placed(value, edge, first):
        shaped = value.reshape((micro, frames) + value.shape[1:])
        order = [edge[:, None], shaped[:, :-1]] if first else [shaped[:, 1:], edge[:, None]]
        return jnp.concatenate(order, 1).reshape(value.shape)

    edge_down = pad_rows(edge_down)
    edge_down = jnp.concatenate([edge_down[:, 0], edge_down[:, 1]], -1)
    edge_up = pad_rows(edge_up[:, 0])
    z = jnp.concatenate(
        [
            placed(quads[..., 2 * CF :], edge_down, True) * links.astype(BF)[:, None, None],
            quads,
            placed(quads[..., :CF], edge_up, False) * nexts.astype(BF)[:, None, None],
        ],
        -1,
    )

    rows = groups * ROWS
    bind = functools.partial

    def og(lanes, dtype, per):
        return out_group((groups, ROWS, lanes), dtype, per)

    def os(per, n, lanes):
        return out_stream((micro, n, lanes), F32, frames // per)

    def edge(lanes):
        return out_stream((micro, ROWS, lanes), BF, 1)

    per = 4
    steps = frames // per
    lat_pre, fone, sums = call(
        bind(k_first, steps=steps),
        groups // per,
        [group(z, per), whole(w_first)],
        [og(CL, F32, per), og(128, F32, per), os(per, 2, CL + 128)],
        flops=2 * rows * 896 * 384,
        name="lateral_and_fast_time",
    )
    total1 = all_sum(sums)

    lat_act, taps, tail, head = call(
        bind(k_taps, count=count),
        micro,
        [
            scalar(links), group(lat_pre, frames), stream(total1, 1), whole(gb),
            group(slow, frames), whole(slow_time), whole(masks),
        ],
        [og(CL, BF, frames), og(3 * CM, F32, frames), edge(CM), edge(CM)],
        flops=2 * rows * 1280 * 768,
        name="slow_time_taps",
    )
    rim_before, rim_after = from_before(tail), from_after(head)
    per = 4
    steps = frames // per
    short, fact_cat, ftwo, sums = call(
        bind(k_short, steps=steps, count=count),
        groups // per,
        [
            group(slow, per), group(lat_act, per), whole(projection), group(fone, per),
            stream(total1, steps), whole(fgb), whole(fspace), whole(masks),
        ],
        [og(CS, F32, per), og(384, BF, per), og(128, F32, per), os(per, 2, CS + 128)],
        flops=2 * rows * 1280 * 1024,
        name="shortcut_and_fast_space",
    )
    slow_one, sums = call(
        k_one,
        micro,
        [
            scalar(links), scalar(nexts), group(taps, frames),
            stream(rim_before, 1), stream(rim_after, 1), stream(sums, 1),
        ],
        [og(CM, F32, frames), os(frames, 2, CS + 128 + CM)],
        name="slow_one",
    )
    total2 = all_sum(sums)

    per = 4
    steps = frames // per
    cat_one, slow_two, fact_two, fthree, sums = call(
        bind(k_two, steps=steps, count=count),
        groups // per,
        [
            group(slow_one, per), group(ftwo, per), stream(total2, steps), whole(gb), whole(fgb),
            whole(slow_space), whole(fproj), whole(masks),
        ],
        [
            og(3 * CM, BF, per), og(CM, F32, per), og(128, BF, per), og(4 * CF, F32, per),
            os(per, 2, CM + 4 * CF),
        ],
        flops=2 * rows * 768 * 768,
        name="slow_space",
    )
    total3 = all_sum(sums)

    per = 4
    steps = frames // per
    act_two, sums = call(
        bind(k_three, steps=steps, count=count),
        groups // per,
        [
            group(slow_two, per), stream(total3, steps), whole(gb), whole(slow_proj),
            whole(masks),
        ],
        [og(CM, BF, per), os(per, 2, CS)],
        flops=2 * rows * 256 * 1024,
        name="slow_three",
    )
    total4 = all_sum(sums)
    per = 2
    steps = frames // per
    quarters = ((groups, 4, PIX, CF), BF)
    fast_out, fgrad, fsums = call(
        bind(k_fast_out, steps=steps, count=count),
        groups // per,
        [
            group(fthree, per), group(quads, per), group(fcot, per), stream(total3, steps),
            whole(fgb),
        ],
        [out_group(*quarters, per), og(4 * CF, F32, per), os(per, 2, 4 * CF)],
        scratch=[pltpu.VMEM((2, 8, 4 * CF), F32)],
        flops=rows * 512 * 200,
        name="fast_out",
    )

    slow_out, grad, sums = call(
        bind(k_out, steps=steps, count=count),
        groups // per,
        [
            group(act_two, per), whole(slow_proj), group(short, per), group(cot, per),
            stream(total4, steps), stream(total2, steps), whole(gb), stream(fsums, steps),
        ],
        [
            out_group((groups, PIX, CS), BF, per), og(CS, F32, per), os(per, 3, CS + 4 * CF),
        ],
        scratch=[pltpu.VMEM((per, ROWS, CS), F32), pltpu.VMEM((3, 8, CS), F32)],
        flops=2 * rows * 256 * 1024,
        name="slow_out",
    )
    sums_a = all_sum(sums)

    d_three, d_short, grad_two, d_fthree, fgrad_two, sums = call(
        bind(k_back_three, steps=steps, count=count),
        groups // per,
        [
            group(act_two, per), whole(slow_proj), group(short, per), group(grad, per),
            stream(total4, steps), stream(total2, steps), stream(sums_a, steps), whole(gb),
            group(slow_two, per), stream(total3, steps), group(fgrad, per), group(fthree, per),
            group(ftwo, per), whole(fgb), whole(fproj), whole(masks),
        ],
        [
            og(CS, BF, per), og(CS, BF, per), og(CM, F32, per), og(4 * CF, BF, per),
            og(128, F32, per), os(per, 2, CM + 128),
        ],
        scratch=[pltpu.VMEM((per, ROWS, CS), F32)],
        flops=4 * rows * 256 * 1024,
        name="back_three",
    )
    sums_b = all_sum(sums)
    proj_grad = outer_joined(slow, lat_act, d_short, 1, "projection_grad")
    out_grad, fout_grad = call(
        k_outer_out,
        1,
        [whole(act_two), whole(d_three), whole(fact_two), whole(d_fthree)],
        [
            ((CM, CS), F32, (CM, CS), lambda g: (0, 0)),
            ((128, 4 * CF), F32, (128, 4 * CF), lambda g: (0, 0)),
        ],
        flops=2 * rows * 256 * 1024,
        name="slow_out_grad",
    )

    def shares(value):
        return value.reshape(devices, -1, value.shape[-1])

    proj_rows = proj_grad.shape[0] // devices
    flows = [Shares(jnp.concatenate([shares(proj_grad), shares(out_grad)], 1))]

    sums_b, d_short = tie(flows, sums_b, d_short)
    per = 4
    steps = frames // per
    two_taps, grad_one, ftwo_taps, fgrad_one, sums = call(
        bind(k_back_two, steps=steps, count=count),
        groups // per,
        [
            group(slow_two, per), stream(total3, steps), group(grad_two, per),
            stream(sums_b, steps), whole(gb), whole(slow_space), group(slow_one, per),
            stream(total2, steps), group(ftwo, per), group(fgrad_two, per), whole(fgb),
            whole(fspace), group(fone, per), stream(total1, steps), whole(masks),
        ],
        [
            og(3 * CM, BF, per), og(CM, F32, per), og(384, BF, per), og(128, F32, per),
            os(per, 2, CM + 128),
        ],
        flops=2 * rows * 768 * 768,
        name="back_two",
    )
    sums_c = all_sum(sums)
    block = (groups, ROWS, CM)
    space_grad, fspace_grad = call(
        k_outer_space,
        3,
        [(cat_one, block, lambda g: (0, 0, g)), whole(two_taps), whole(fact_cat), whole(ftwo_taps)],
        [
            ((3, 3, CM, CM), F32, (3, 1, CM, CM), lambda g: (0, g, 0, 0)),
            ((384, 384), F32, (384, 384), lambda g: (0, 0)),
        ],
        flops=2 * rows * 768 * 768,
        name="slow_space_grad",
    )
    flows.append(Shares(shares(space_grad)))

    sums_c = tie(flows, sums_c)
    d_one, d_fone, tail, head = call(
        bind(k_back_one, count=count),
        micro,
        [
            scalar(links), group(slow_one, frames), stream(total2, 1), group(grad_one, frames),
            group(fone, frames), stream(total1, 1), group(fgrad_one, frames), stream(sums_c, 1),
            whole(gb), whole(fgb), whole(masks),
        ],
        [og(CM, BF, frames), og(128, BF, frames), edge(CM + 128), edge(CM + 128)],
        name="back_one",
    )
    rim_before, rim_after = from_before(tail), from_after(head)
    rim_before, rim_after = tie(flows, rim_before, rim_after)
    trio, lat_grad, sums = call(
        bind(k_trio, count=count),
        micro,
        [
            scalar(links), scalar(nexts), group(d_one, frames),
            stream(rim_before, 1), stream(rim_after, 1), group(d_short, frames),
            (slow_time, (CL, 3 * CM), lambda g: (4, 0)),
            (projection, (CL, CS), lambda g: (4, 0)),
            group(lat_pre, frames), stream(total1, 1), whole(gb),
        ],
        [og(3 * CM, BF, frames), og(CL, F32, frames), os(frames, 2, CL)],
        flops=2 * rows * 1792 * 256,
        name="back_lateral",
    )
    sums_d = all_sum(sums)
    time_grad = outer_joined(slow, lat_act, trio, 3, "slow_time_grad")
    flows.append(Shares(shares(time_grad)))
    sums_d, trio = tie(flows, sums_d, trio)

    d_lat, head = call(
        bind(k_back_lat, count=count),
        micro,
        [
            scalar(links), group(lat_pre, frames), stream(total1, 1), group(lat_grad, frames),
            stream(sums_d, 1), whole(gb), whole(masks),
        ],
        [og(CL, BF, frames), edge(CL)],
        name="back_lat",
    )
    lat_rim = from_after(head)
    wide = (groups, ROWS, 128)
    first_grad = call(
        k_outer_first,
        7,
        [(z, wide, lambda g: (0, 0, g)), whole(d_lat), whole(d_fone)],
        [((7 * CF, CL + 128), F32, (CF, CL + 128), lambda g: (g, 0))],
        flops=2 * rows * 896 * 384,
        name="lateral_grad",
    )[0]
    ftime_grad = jnp.stack(
        [
            sum(
                first_grad[(q + 1 + k) * CF : (q + 2 + k) * CF, CL + q * CFM : CL + (q + 1) * CFM]
                for q in range(4)
            )
            for k in range(3)
        ],
        0,
    )
    fs = jnp.stack(
        [
            frame_fold(fspace_grad[c * 128 : (c + 1) * 128, a * 128 : (a + 1) * 128], CFM, CFM)
            for a in range(3)
            for c in range(3)
        ],
        0,
    )
    fo = frame_fold(fout_grad, CF, CFM)
    flat = [
        part.reshape(devices, -1) for part in (first_grad[: 5 * CF, :CL], ftime_grad, fs, fo)
    ]
    sizes = [part.shape[1] for part in flat]
    flat = jnp.concatenate(flat, 1)
    flat = jnp.pad(flat, ((0, 0), (0, -flat.shape[1] % 1024)))
    flows.append(Shares(flat.reshape(devices, -1, 128)))
    per = 4
    slow_in_grad = call(
        k_slow_grad,
        groups // per,
        [
            group(trio, per), group(d_short, per), (slow_time, (CS, 3 * CM), lambda g: (0, 0)),
            (projection, (CS, CS), lambda g: (0, 0)),
        ],
        [out_group((groups, PIX, CS), BF, per)],
        flops=2 * rows * 1792 * 1024,
        name="slow_in_grad",
    )[0]
    fast_in_grad = call(
        k_fast_grad,
        micro,
        [
            scalar(links), scalar(nexts), group(fgrad, frames), group(d_lat, frames),
            stream(lat_rim, 1), group(d_fone, frames), stream(rim_before, 1),
            stream(rim_after, 1), whole(w_back),
        ],
        [out_group(*quarters, frames)],
        scratch=[pltpu.VMEM((frames, ROWS, 768), BF)],
        flops=2 * rows * 768 * 512,
        name="fast_in_grad",
    )[0]
    both_out = flows[0].result().reshape(-1, CS)
    proj_out, out_out = both_out[:proj_rows].reshape(-1), both_out[proj_rows:].reshape(-1)
    space_out, time_out = flows[1].result(), flows[2].result()
    flat = flows[3].result()
    smalls = []
    at = 0
    for size in sizes:
        smalls.append(flat[at : at + size])
        at += size

    sums_a, sums_b, sums_c, sums_d = (
        jnp.sum(value, 0) for value in (sums_a, sums_b, sums_c, sums_d)
    )
    bias_grad = jnp.concatenate(
        [sums_d[0], sums_c[0, :CM], sums_b[0, :CM], sums_a[0, :CS], sums_a[0, :CS]]
    )
    gain_grad = jnp.concatenate(
        [sums_d[1], sums_c[1, :CM], sums_b[1, :CM], sums_a[1, :CS], sums_a[2, :CS]]
    )
    share = slow_gain.shape[0]
    start = lax.axis_index(AXES) * share

    def quarter(vector):
        return jnp.sum(vector.reshape(4, -1), 0)

    fast_bias_grad, fast_gain_grad = (
        jnp.concatenate(
            [quarter(sums_c[row, CM:]), quarter(sums_b[row, CM:]), quarter(sums_a[row, CS:])]
        )
        for row in range(2)
    )
    return (
        slow_out.reshape(slow_in.shape),
        fast_out.reshape(fast_in.shape),
        slow_in_grad.reshape(slow_in.shape),
        fast_in_grad.reshape(fast_in.shape),
        smalls[0],
        time_out,
        space_out,
        out_out,
        proj_out,
        smalls[1],
        smalls[2],
        smalls[3],
        lax.dynamic_slice_in_dim(gain_grad, start, share),
        lax.dynamic_slice_in_dim(bias_grad, start, share),
        fast_gain_grad,
        fast_bias_grad,
    )


def solution(mesh):
    frames = P(None, AXES, None, None)
    flat = P(AXES)
    return jax.shard_map(
        local,
        mesh=mesh,
        in_specs=(frames, frames, P(None, AXES))
        + (flat,) * 10
        + (P(), P(), frames, frames),
        out_specs=(frames,) * 4 + (flat,) * 10 + (P(), P()),
        check_vma=False,
    )
```

```python
import functools
import math

import jax
import jax.numpy as jnp
import numpy as np
from jax import lax
from jax.experimental import pallas as pl
from jax.experimental.pallas import tpu as pltpu
from jax.sharding import PartitionSpec as P

CS = 1024
CL = 256
CM = 256
CF = 128
CFM = 32
HH = 14
WW = 14
PIX = HH * WW
ROWS = 208
EPS = 1e-05
AXES = ("path", "dp")
BF = jnp.bfloat16
F32 = jnp.float32


def swap(value, bit):
    count = lax.axis_size(AXES)
    return lax.ppermute(value, AXES, [(i, i ^ bit) for i in range(count)])


def dp_pairs():
    bits = []
    bit = 1
    while bit < lax.axis_size("dp"):
        bits.append(bit)
        bit *= 2
    return [bits[at : at + 2] for at in range(0, len(bits), 2)]


def all_sum(value, hook=lambda value, stage: value):
    value = hook(value + swap(value, lax.axis_size("dp")), 0)
    for stage, pair in enumerate(dp_pairs()):
        if len(pair) == 1:
            value = value + swap(value, pair[0])
        else:
            one, two = pair
            first, second, third = swap(value, one), swap(value, two), swap(value, one + two)
            value = (value + first) + (second + third)
        value = hook(value, stage + 1)
    return value


def has_bits(me):
    bits = [bit for pair in dp_pairs() for bit in pair] + [lax.axis_size("dp")]
    return {bit: (me & bit) != 0 for bit in bits}


def in_order(parts, bits, mine):
    parts = [part[None] for part in parts]
    step = 1
    for bit in bits:
        parts = [jnp.where(mine[bit], parts[k ^ step], parts[k]) for k in range(len(parts))]
        step *= 2
    return jnp.concatenate(parts, 0)


class Gather:
    def __init__(self, mine, value):
        self.mine = mine
        self.shape = value.shape
        self.value = value[None]
        self.stages = dp_pairs()[::-1] + [[lax.axis_size("dp")]]
        self.flight = None
        self.start()

    def start(self):
        if not self.stages:
            self.value = self.value.reshape((-1,) + self.shape)
            return
        self.bits = self.stages.pop(0)
        steps = [
            sum(bit for n, bit in enumerate(self.bits) if k >> n & 1)
            for k in range(1, 2 ** len(self.bits))
        ]
        self.flight = [swap(self.value, step) for step in steps]

    def finish(self):
        stacked = in_order([self.value] + self.flight, self.bits, self.mine)
        if self.stages:
            stacked = jnp.swapaxes(stacked, 0, 1)
        self.value = stacked.reshape((-1,) + self.shape)
        self.flight = None
        self.start()

    def result(self):
        while self.flight is not None:
            self.finish()
        return self.value


def pick(value, start, extent, axis):
    starts = [jnp.int32(0)] * value.ndim
    starts[axis] = start
    sizes = list(value.shape)
    sizes[axis] = extent
    return lax.dynamic_slice(value, starts, sizes, allow_negative_indices=False)


def share_stages():
    return [[lax.axis_size("dp")]] + dp_pairs()


def slice_spots(me):
    spots = []
    for bits in share_stages():
        count = 2 ** len(bits)
        spot = lax.shift_right_logical(me, bits[0].bit_length() - 1) & (count - 1)
        spots.append([spot ^ k for k in range(count)])
    return spots


class Shares:
    def __init__(self, spots, value):
        self.value = value
        self.stages = list(zip(share_stages(), spots))
        self.flight = None
        self.start()

    def start(self):
        if not self.stages:
            return
        bits, spots = self.stages.pop(0)
        count = 2 ** len(bits)
        rest = self.value.shape[-2:]
        axis = 0 if bits[0] == lax.axis_size("dp") else 1
        shaped = self.value.reshape(((2, -1), (-1, count))[axis] + rest)
        parts = [pick(shaped, spot, 1, axis) for spot in spots]
        parts = [part.reshape((-1,) + rest) for part in parts]
        self.keep = parts[0]
        steps = [sum(bit for n, bit in enumerate(bits) if k >> n & 1) for k in range(1, count)]
        self.flight = [swap(part.astype(BF), step) for part, step in zip(parts[1:], steps)]

    def finish(self):
        terms = [self.keep.astype(F32)] + [part.astype(F32) for part in self.flight]
        while len(terms) > 1:
            terms = [sum(terms[at : at + 2]) for at in range(0, len(terms), 2)]
        self.value = terms[0]
        self.flight = None
        self.start()

    def result(self):
        while self.flight is not None:
            self.finish()
        return self.value.reshape(-1)


def tie(flows, *values):
    flows = [flow for flow in flows if flow.flight is not None]
    values, flights = lax.optimization_barrier((values, [flow.flight for flow in flows]))
    for flow, flight in zip(flows, flights):
        flow.flight = flight
        flow.finish()
    return values if len(values) > 1 else values[0]


def from_before(value):
    count = lax.axis_size(AXES)
    return lax.ppermute(value, AXES, [(i, i + 1) for i in range(count - 1)])


def from_after(value):
    count = lax.axis_size(AXES)
    return lax.ppermute(value, AXES, [(i + 1, i) for i in range(count - 1)])


def gelu_tan(value):
    return jnp.tanh(value * (0.7978845608028654 + 0.035677408136300125 * (value * value)))


def gelu(value):
    return value * (0.5 + 0.5 * gelu_tan(value))


def gelu_slope(value):
    tan = gelu_tan(value)
    inner = 0.7978845608028654 + 0.10703222440890037 * (value * value)
    return (0.5 + 0.5 * tan) + (0.5 * value) * (1.0 - tan * tan) * inner


def pad_rows(value):
    return jnp.pad(value, [(0, 0)] * (value.ndim - 2) + [(0, ROWS - PIX), (0, 0)])


def to_quads(value):
    micro, frames, _, lanes = value.shape
    quads = pad_rows(value).reshape(micro * frames // 4, 4, ROWS, lanes)
    return jnp.concatenate([quads[:, place] for place in range(4)], -1)


def in_vmem(array):
    return pltpu.with_memory_space_constraint(array, pltpu.VMEM)


PARTS = dict(
    short=CS,
    grad=CS,
    grad_two=CM,
    fgrad_two=128,
    grad_one=CM,
    fgrad_one=128,
    lat_grad=CL,
    fthree=4 * CF,
    fgrad=4 * CF,
    one=CM,
    two=CM,
    ftwo=128,
)


def in_vmem(array):
    return pltpu.with_memory_space_constraint(array, pltpu.VMEM)


def call(body, steps, ins, outs, scratch=(), flops=0, name=None, limit=16, unroll=False, state=None):
    names = [given[0] if len(given) == 2 else None for given in outs]
    ins = [group(state[given[0]], given[1]) if len(given) == 2 else given for given in ins]
    if state is not None:
        groups = ins[0][0].shape[0] if not state else next(iter(state.values())).shape[0]
    outs = [
        out_group((groups, ROWS, PARTS[given[0]]), F32, given[1]) if len(given) == 2 else given
        for given in outs
    ]
    arrays = [array for array, _, _ in ins]
    blocks = [(array.shape, block, index) for array, block, index in ins]
    blocks += [(shape, block, index) for shape, _, block, index, _ in outs]

    def view(ref, shape, block, index, step):
        if block is None or tuple(block) == tuple(shape):
            return ref
        spot = [
            slice(None) if size == full else pl.ds(place * size, size)
            for place, size, full in zip(index(step), block, shape)
        ]
        return ref.at[tuple(spot)]

    def kernel(*refs):
        def run(step, carry):
            views = [view(ref, *given, step) for ref, given in zip(refs, blocks)]
            body(step, *views, *refs[len(blocks) :])
            return carry

        if steps == 1 or unroll:
            for step in range(steps):
                run(step, 0)
        else:
            lax.fori_loop(0, steps, run, 0)

    moved = sum(array.size * array.dtype.itemsize for array in arrays)
    moved += sum(math.prod(shape) * jnp.dtype(dtype).itemsize for shape, dtype, *_ in outs)
    vmem = pl.BlockSpec(memory_space=pltpu.VMEM)
    result = pl.pallas_call(
        kernel,
        in_specs=[
            pl.BlockSpec(memory_space=pltpu.SMEM) if block is None else vmem
            for _, block, _ in ins
        ],
        out_specs=[vmem] * len(outs),
        out_shape=[
            pltpu.VMEM(shape, dtype) if stays else jax.ShapeDtypeStruct(shape, dtype)
            for shape, dtype, _, _, stays in outs
        ],
        scratch_shapes=list(scratch),
        compiler_params=pltpu.CompilerParams(vmem_limit_bytes=limit * 1024 * 1024),
        cost_estimate=pl.CostEstimate(
            flops=int(flops), bytes_accessed=int(moved), transcendentals=0
        ),
        name=name,
    )(*[array if block is None else in_vmem(array) for array, block, _ in ins])
    if state is None:
        return result
    fresh = {name: array for name, array in zip(names, result) if name}
    return [{**state, **fresh}] + [array for name, array in zip(names, result) if not name]


def group(array, per):
    tail = (0,) * (array.ndim - 1)
    return (array, (per,) + array.shape[1:], lambda g: (g,) + tail)


def whole(array):
    return (array, array.shape, None)


def scalar(array):
    return (array, None, None)


def stream(array, steps):
    tail = (0,) * (array.ndim - 1)
    return (array, (1,) + array.shape[1:], lambda g: (g // steps,) + tail)


def out_group(shape, dtype, per, stays=True):
    tail = (0,) * (len(shape) - 1)
    return (shape, dtype, (per,) + shape[1:], lambda g: (g,) + tail, stays)


def out_stream(shape, dtype, steps, stays=True):
    tail = (0,) * (len(shape) - 1)
    return (shape, dtype, (1,) + shape[1:], lambda g: (g // steps,) + tail, stays)


def out_whole(shape, dtype, stays=True):
    return (shape, dtype, shape, None, stays)


def rows_of(ref):
    return ref[...].reshape(-1, ref.shape[-1])


def put(ref, value):
    ref[...] = value.reshape(ref.shape).astype(ref.dtype)


def spread(value, mask):
    lanes = value.shape[-1]
    shaped = value.reshape(-1, ROWS, lanes) * mask[None, :, :lanes]
    return shaped.reshape(value.shape)


def add_rows(ref, step, steps, lanes, *values):
    first = step % steps == 0
    for row, value in enumerate(values):
        total = jnp.sum(value, 0, keepdims=True)
        spot = (0, slice(row, row + 1), slice(lanes, lanes + value.shape[-1]))
        if steps > 1:
            total = jnp.where(first, 0.0, ref[spot]) + total
        ref[spot] = total


def stats(total, start, extent, count, folded=0):
    first = total[0, 0:1, start : start + extent]
    second = total[0, 1:2, start : start + extent]
    if folded:
        first, second = fold_lanes(first, folded), fold_lanes(second, folded)
    mean = first / count
    return mean, lax.rsqrt(second / count - mean * mean + EPS)


def fold_lanes(vector, width):
    lanes = vector.shape[-1]
    if width % 128 == 0:
        parts = [vector[:, at : at + width] for at in range(0, lanes, width)]
        one = (parts[0] + parts[1]) + (parts[2] + parts[3])
        return jnp.concatenate([one] * 4, -1)
    wide = jnp.broadcast_to(vector, (8, lanes))
    wide = wide + pltpu.roll(wide, 2 * width, 1)
    wide = wide + pltpu.roll(wide, width, 1)
    return wide[0:1]


def back_parts(sums, start, extent, count, folded=0, rows=(0, 1)):
    one = sums[0, rows[0] : rows[0] + 1, start : start + extent]
    two = sums[0, rows[1] : rows[1] + 1, start : start + extent]
    if folded:
        one, two = fold_lanes(one, folded), fold_lanes(two, folded)
    return one / count, two / count


def norm_back(grad, hat, factor, one, two):
    return factor * (grad - one - hat * two)


def turn(value, step):
    return pltpu.roll(value, step % value.shape[0], 0)


def mul(left, right):
    return jnp.dot(left, right, preferred_element_type=F32)


def mul_t(left, right):
    return lax.dot_general(left, right, (((1,), (1,)), ((), ())), preferred_element_type=F32)


def mul_rows(left, right):
    return lax.dot_general(
        rows_of(left), rows_of(right), (((0,), (0,)), ((), ())), preferred_element_type=F32
    )


def column_cat(act, masks):
    act = act.astype(BF).astype(F32)
    left = spread(turn(act, 1), masks[1])
    right = spread(turn(act, -1), masks[2])
    return jnp.concatenate([left.astype(BF), act.astype(BF), right.astype(BF)], -1)


def row_sum(taps, masks):
    lanes = taps.shape[-1] // 3
    return (
        spread(turn(taps[:, :lanes], WW), masks[3])
        + taps[:, lanes : 2 * lanes]
        + spread(turn(taps[:, 2 * lanes :], -WW), masks[4])
    )


def row_cat(grad, masks):
    grad = grad.astype(BF).astype(F32)
    above = spread(turn(grad, -WW), masks[4])
    below = spread(turn(grad, WW), masks[3])
    return jnp.concatenate([above.astype(BF), grad.astype(BF), below.astype(BF)], -1)


def column_sum(taps, masks):
    lanes = taps.shape[-1] // 3
    return (
        spread(turn(taps[:, :lanes], -1), masks[2])
        + taps[:, lanes : 2 * lanes]
        + spread(turn(taps[:, 2 * lanes :], 1), masks[1])
    )


def fill_z(z, at, links, nexts, fast, edge_down, edge_up):
    frames = fast.shape[0]
    for f in range(frames):
        link, following = links[at + f], nexts[at + f]
        for q in range(4):
            z[f, :PIX, q * CF : (q + 1) * CF] = fast[f, q]
        for q in range(2):
            prev = edge_down[0, q] if f == 0 else fast[f - 1, 2 + q]
            z[f, :PIX, (4 + q) * CF : (5 + q) * CF] = (link * prev.astype(F32)).astype(BF)
        follow = edge_up[0, 0] if f == frames - 1 else fast[f + 1, 0]
        z[f, :PIX, 6 * CF :] = (following * follow.astype(F32)).astype(BF)


def k_first(
    step, links, nexts, fast, edge_down, edge_up, weight, lat, fone, total, z
):
    z[...] = jnp.zeros_like(z)
    fill_z(z, step * fast.shape[0], links, nexts, fast, edge_down, edge_up)
    value = mul(rows_of(z), weight[...])
    put(lat, value[:, :CL])
    put(fone, value[:, CL:])
    add_rows(total, step, 1, 0, value, value * value)


def k_taps(step, links, lat, total, gb, slow, w_time, masks, lat_act, taps, tail, head, *, count):
    frames = slow.shape[0]
    mean, scale = stats(total, 0, CL, count)
    hat = (rows_of(lat) - mean) * scale
    act = spread(gelu(hat * gb[0:1, :CL] + gb[1:2, :CL]), masks[0]).astype(BF)
    put(lat_act, act)
    value = mul(rows_of(slow), w_time[:CS]) + mul(act, w_time[CS:])
    put(taps, value)
    tail[0] = value[(frames - 1) * ROWS :, :CM].astype(BF)
    head[0] = (links[step * frames] * value[:ROWS, 2 * CM :]).astype(BF)


def block_taps(taps, out):
    lane = lax.broadcasted_iota(jnp.int32, (CFM, 128), 1)
    row = lax.broadcasted_iota(jnp.int32, (CFM, 128), 0)
    four = sum(jnp.where(lane == row + q * CFM, 1.0, 0.0) for q in range(4))
    wide = mul(taps[...], four.astype(BF))
    for a in range(3):
        for c in range(3):
            tap = wide[(3 * a + c) * CFM : (3 * a + c + 1) * CFM]
            for q in range(4):
                mine = (lane >= q * CFM) & (lane < (q + 1) * CFM)
                at = c * 128 + q * CFM
                out[at : at + CFM, a * 128 : (a + 1) * 128] = jnp.where(mine, tap, 0.0).astype(BF)


def k_short(
    step, slow, lat_act, w_proj, fone, total, fgb, fast_taps, masks,
    short, fact, ftwo, sums, fspace, *, steps, count
):
    block_taps(fast_taps, fspace)
    value = mul(rows_of(slow), w_proj[:CS]) + mul(rows_of(lat_act), w_proj[CS:])
    put(short, value)
    add_rows(sums, step, steps, 0, value, value * value)
    mean, scale = stats(total, CL, 128, 4.0 * count, CFM)
    hat = (rows_of(fone) - mean) * scale
    act = spread(gelu(hat * fgb[0:1, :128] + fgb[1:2, :128]), masks[0])
    cat = column_cat(act, masks)
    put(fact, cat)
    value = row_sum(mul(cat, fspace[...]), masks)
    put(ftwo, value)
    add_rows(sums, step, steps, CS, value, value * value)


def k_one(step, links, nexts, taps, rim_before, rim_after, given, slow_one, sums):
    frames = taps.shape[0]
    base = step * frames
    one = two = 0.0
    for f in range(frames):
        prev = rim_before[0].astype(F32) if f == 0 else taps[f - 1, :, :CM]
        follow = rim_after[0].astype(F32) if f == frames - 1 else taps[f + 1, :, 2 * CM :]
        value = links[base + f] * prev + taps[f, :, CM : 2 * CM] + nexts[base + f] * follow
        slow_one[f] = value
        one += jnp.sum(value, 0, keepdims=True)
        two += jnp.sum(value * value, 0, keepdims=True)
    sums[0, :, : CS + 128] = given[0]
    sums[0, 0:1, CS + 128 :] = one
    sums[0, 1:2, CS + 128 :] = two


def k_two(
    step, slow_one, ftwo, total, gb, fgb, space, fproj, masks,
    cat_out, two_out, fact_out, fthree, sums, w_space, *, steps, count
):
    for a in range(3):
        for c in range(3):
            tap = space[(3 * a + c) * CM : (3 * a + c + 1) * CM]
            w_space[c * CM : (c + 1) * CM, a * CM : (a + 1) * CM] = tap

    mean, scale = stats(total, CS + 128, CM, count)
    hat = (rows_of(slow_one) - mean) * scale
    act = spread(gelu(hat * gb[0:1, CL : 2 * CL] + gb[1:2, CL : 2 * CL]), masks[0])
    cat = column_cat(act, masks)
    put(cat_out, cat)
    value = row_sum(mul(cat, w_space[...]), masks)
    put(two_out, value)
    add_rows(sums, step, steps, 0, value, value * value)
    mean, scale = stats(total, CS, 128, 4.0 * count, CFM)
    hat = (rows_of(ftwo) - mean) * scale
    act = spread(gelu(hat * fgb[0:1, 128:256] + fgb[1:2, 128:256]), masks[0]).astype(BF)
    put(fact_out, act)
    value = mul(act, fproj[...])
    put(fthree, value)
    add_rows(sums, step, steps, CM, value, value * value)


def k_three(step, slow_two, total, gb, w_out, masks, act_out, sums, *, steps, count):
    mean, scale = stats(total, 0, CM, count)
    hat = (rows_of(slow_two) - mean) * scale
    act = gelu(hat * gb[0:1, 2 * CL : 3 * CL] + gb[1:2, 2 * CL : 3 * CL])
    act = spread(act, masks[0]).astype(BF)
    put(act_out, act)
    value = mul(act, w_out[...])
    add_rows(sums, step, steps, 0, value, value * value)


CHUNK = 16
SPAN = 512


def gelu_both(value):
    square = value * value
    tan = jnp.tanh(value * (0.7978845608028654 + 0.035677408136300125 * square))
    half = 0.5 + 0.5 * tan
    inner = 0.7978845608028654 + 0.10703222440890037 * square
    slope = half + (0.5 * value) * (1.0 - tan * tan) * inner
    return value * half, slope


def chunked(body, frames, lanes):
    full = PIX // CHUNK
    last = full * CHUNK

    def frame(f, carry):
        def step(i, carry):
            at = pl.ds(pl.multiple_of(i * CHUNK, CHUNK), CHUNK)
            for start in range(0, lanes, SPAN):
                body(f, at, CHUNK, slice(start, start + SPAN))
            return carry

        lax.fori_loop(0, full, step, 0)
        for start in range(0, lanes, SPAN):
            body(f, pl.ds(last, CHUNK), PIX - last, slice(start, start + SPAN))
        return carry

    lax.fori_loop(0, frames, frame, 0)


def halves(value):
    return value[:8] + value[8:]


def k_fast_out(step, fthree, fast, cot, total, fgb, out, grad, sums, acc, *, steps, count):
    mean, scale = stats(total, CM, 4 * CF, 4.0 * count, CF)
    gain, bias = fgb[0:1, 256:], fgb[1:2, 256:]

    @pl.when(step % steps == 0)
    def _():
        acc[...] = jnp.zeros_like(acc)

    def body(f, rows, real, lanes):
        hat = (fthree[f, rows, lanes] - mean[:, lanes]) * scale[:, lanes]
        quads = [fast[f, q, pl.ds(rows.start, real), :].astype(F32) for q in range(4)]
        if real < CHUNK:
            blank = jnp.zeros((CHUNK - real, CF), F32)
            quads = [jnp.concatenate([part, blank], 0) for part in quads]
        value = hat * gain[:, lanes] + bias[:, lanes] + jnp.concatenate(quads, -1)
        act, slope = gelu_both(value)
        act = act.astype(BF)
        for q in range(4):
            piece = act[:real, q * CF : (q + 1) * CF]
            out[f, q, pl.ds(rows.start, real), :] = piece
        slope = slope * cot[f, rows, lanes].astype(F32)
        grad[f, rows, lanes] = slope
        acc[0] += halves(slope)
        acc[1] += halves(slope * hat)

    chunked(body, fthree.shape[0], 4 * CF)

    @pl.when(step % steps == steps - 1)
    def _():
        for row in range(2):
            sums[0, row : row + 1] = jnp.sum(acc[row], 0, keepdims=True)


def k_out(
    step, act, w_out, short, cot, total, short_total, gb, given, out, grad_out, sums, three, acc,
    *, steps, count
):
    three[...] = mul(rows_of(act), w_out[...]).reshape(three.shape)
    mean_a, scale_a = stats(total, 0, CS, count)
    mean_b, scale_b = stats(short_total, 0, CS, count)
    gain_a, gain_b = gb[0:1, 768:1792], gb[0:1, 1792:]
    bias = gb[1:2, 768:1792] + gb[1:2, 1792:]

    @pl.when(step % steps == 0)
    def _():
        acc[...] = jnp.zeros_like(acc)

    def body(f, rows, real, lanes):
        hat_a = (three[f, rows, lanes] - mean_a[:, lanes]) * scale_a[:, lanes]
        hat_b = (short[f, rows, lanes] - mean_b[:, lanes]) * scale_b[:, lanes]
        value = hat_a * gain_a[:, lanes] + (hat_b * gain_b[:, lanes] + bias[:, lanes])
        smooth, slope = gelu_both(value)
        out[f, pl.ds(rows.start, real), lanes] = smooth.astype(BF)[:real]
        grad = slope * cot[f, rows, lanes].astype(F32)
        grad_out[f, rows, lanes] = grad
        acc[0, :, lanes] += halves(grad)
        acc[1, :, lanes] += halves(grad * hat_a)
        acc[2, :, lanes] += halves(grad * hat_b)

    chunked(body, act.shape[0], CS)

    @pl.when(step % steps == steps - 1)
    def _():
        for row in range(3):
            sums[0, row : row + 1, :CS] = jnp.sum(acc[row], 0, keepdims=True)
        sums[0, 0:2, CS:] = given[0]
        sums[0, 2:3, CS:] = jnp.zeros((1, 4 * CF), F32)


def k_back_three(
    step, act, w_out, short, grad, total, short_total, sums, gb, slow_two, total3,
    fgrad, fthree, ftwo, fgb, fproj, masks,
    d_three, d_short, grad_two, d_fthree, fgrad_two, sums_out, three, *, steps, count
):
    three[...] = mul(rows_of(act), w_out[...]).reshape(three.shape)
    mean_a, scale_a = stats(total, 0, CS, count)
    mean_b, scale_b = stats(short_total, 0, CS, count)
    one, two_a = back_parts(sums, 0, CS, count)
    _, two_b = back_parts(sums, 0, CS, count, rows=(0, 2))
    factor_a = gb[0:1, 768:1792] * scale_a
    factor_b = gb[0:1, 1792:] * scale_b

    def body(f, rows, real, lanes):
        given = grad[f, rows, lanes] - one[:, lanes]
        hat_a = (three[f, rows, lanes] - mean_a[:, lanes]) * scale_a[:, lanes]
        hat_b = (short[f, rows, lanes] - mean_b[:, lanes]) * scale_b[:, lanes]
        value_a = factor_a[:, lanes] * (given - hat_a * two_a[:, lanes])
        value_b = factor_b[:, lanes] * (given - hat_b * two_b[:, lanes])
        if real < CHUNK:
            row = lax.broadcasted_iota(jnp.int32, value_a.shape, 0)
            value_a = jnp.where(row < real, value_a, 0.0)
            value_b = jnp.where(row < real, value_b, 0.0)
        d_three[f, rows, lanes] = value_a.astype(BF)
        d_short[f, rows, lanes] = value_b.astype(BF)

    chunked(body, act.shape[0], CS)
    mean, scale = stats(total3, 0, CM, count)
    hat = (rows_of(slow_two) - mean) * scale
    slope = gelu_slope(hat * gb[0:1, 2 * CL : 3 * CL] + gb[1:2, 2 * CL : 3 * CL])
    value = slope * mul_t(rows_of(d_three), w_out[...])
    put(grad_two, value)
    add_rows(sums_out, step, steps, 0, value, value * hat)

    mean, scale = stats(total3, CM, 4 * CF, 4.0 * count, CF)
    one, two = back_parts(sums, CS, 4 * CF, 4.0 * count, CF)
    hat = (rows_of(fthree) - mean) * scale
    value = norm_back(rows_of(fgrad), hat, fgb[0:1, 256:] * scale, one, two)
    lanes = value.shape[-1]
    row = lax.broadcasted_iota(jnp.int32, (1, ROWS, lanes), 1)
    value = jnp.where(row < PIX, value.reshape(-1, ROWS, lanes), 0.0)
    value = value.reshape(-1, lanes).astype(BF)
    put(d_fthree, value)
    mean, scale = stats(short_total, CS, 128, 4.0 * count, CFM)
    hat = (rows_of(ftwo) - mean) * scale
    slope = gelu_slope(hat * fgb[0:1, 128:256] + fgb[1:2, 128:256])
    value = slope * mul_t(value, fproj[...])
    put(fgrad_two, value)
    add_rows(sums_out, step, steps, CM, value, value * hat)


def k_back_two(
    step, slow_two, total3, grad_two, sums, gb, w_space, slow_one, total2,
    ftwo, fgrad_two, fgb, fspace, fone, total1, masks,
    taps_out, grad_one, ftaps_out, fgrad_one, sums_out, *, steps, count
):
    mean, scale = stats(total3, 0, CM, count)
    one, two = back_parts(sums, 0, CM, count)
    hat = (rows_of(slow_two) - mean) * scale
    value = norm_back(rows_of(grad_two), hat, gb[0:1, 2 * CL : 3 * CL] * scale, one, two)
    cat = row_cat(spread(value, masks[0]), masks)
    put(taps_out, cat)
    value = column_sum(mul_t(cat, w_space[...]), masks)
    mean, scale = stats(total2, CS + 128, CM, count)
    hat = (rows_of(slow_one) - mean) * scale
    value = gelu_slope(hat * gb[0:1, CL : 2 * CL] + gb[1:2, CL : 2 * CL]) * value
    put(grad_one, value)
    add_rows(sums_out, step, steps, 0, value, value * hat)

    mean, scale = stats(total2, CS, 128, 4.0 * count, CFM)
    one, two = back_parts(sums, CM, 128, 4.0 * count, CFM)
    hat = (rows_of(ftwo) - mean) * scale
    value = norm_back(rows_of(fgrad_two), hat, fgb[0:1, 128:256] * scale, one, two)
    cat = row_cat(spread(value, masks[0]), masks)
    put(ftaps_out, cat)
    value = column_sum(mul_t(cat, fspace[...]), masks)
    mean, scale = stats(total1, CL, 128, 4.0 * count, CFM)
    hat = (rows_of(fone) - mean) * scale
    value = gelu_slope(hat * fgb[0:1, :128] + fgb[1:2, :128]) * value
    put(fgrad_one, value)
    add_rows(sums_out, step, steps, CM, value, value * hat)


def k_back_one(
    step, links, slow_one, total2, grad_one, fone, total1, fgrad_one, sums, gb, fgb, masks,
    d_one, d_fone, tail, head, *, count
):
    frames = slow_one.shape[0]
    mean, scale = stats(total2, CS + 128, CM, count)
    one, two = back_parts(sums, 0, CM, count)
    hat = (rows_of(slow_one) - mean) * scale
    value = norm_back(rows_of(grad_one), hat, gb[0:1, CL : 2 * CL] * scale, one, two)
    value = spread(value, masks[0])
    put(d_one, value)
    mean, scale = stats(total1, CL, 128, 4.0 * count, CFM)
    one, two = back_parts(sums, CM, 128, 4.0 * count, CFM)
    hat = (rows_of(fone) - mean) * scale
    fvalue = norm_back(rows_of(fgrad_one), hat, fgb[0:1, :128] * scale, one, two)
    fvalue = spread(fvalue, masks[0])
    put(d_fone, fvalue)
    last = (frames - 1) * ROWS
    tail[0, :, :CM] = value[last:].astype(BF)
    tail[0, :, CM:] = fvalue[last:].astype(BF)
    link = links[step * frames]
    head[0, :, :CM] = (link * value[:ROWS]).astype(BF)
    head[0, :, CM:] = (link * fvalue[:ROWS]).astype(BF)


def k_trio(
    step, links, nexts, d_one, rim_before, rim_after, d_short, w_time, w_proj, lat, total1, gb,
    trio, grad, sums, *, count
):
    frames = d_one.shape[0]
    base = step * frames
    for f in range(frames):
        prev = rim_before[0, :, :CM] if f == 0 else d_one[f - 1]
        follow = rim_after[0, :, :CM] if f == frames - 1 else d_one[f + 1]
        trio[f, :, :CM] = (nexts[base + f] * follow.astype(F32)).astype(BF)
        trio[f, :, CM : 2 * CM] = d_one[f]
        trio[f, :, 2 * CM :] = (links[base + f] * prev.astype(F32)).astype(BF)
    value = mul_t(rows_of(trio), w_time[CS:]) + mul_t(rows_of(d_short), w_proj[CS:])
    mean, scale = stats(total1, 0, CL, count)
    hat = (rows_of(lat) - mean) * scale
    value = gelu_slope(hat * gb[0:1, :CL] + gb[1:2, :CL]) * value
    put(grad, value)
    add_rows(sums, step, 1, 0, value, value * hat)


def k_slow_grad(step, trio, d_short, w_time, w_proj, out):
    value = mul_t(rows_of(trio), w_time[:CS]) + mul_t(rows_of(d_short), w_proj[:CS])
    out[...] = value.reshape(-1, ROWS, CS)[:, :PIX].astype(BF)


def k_back_lat(step, links, lat, total1, grad, sums, gb, masks, d_lat, head, *, count):
    frames = lat.shape[0]
    mean, scale = stats(total1, 0, CL, count)
    one, two = back_parts(sums, 0, CL, count)
    hat = (rows_of(lat) - mean) * scale
    value = norm_back(rows_of(grad), hat, gb[0:1, :CL] * scale, one, two)
    value = spread(value, masks[0])
    put(d_lat, value)
    head[0] = (links[step * frames] * value[:ROWS]).astype(BF)


def k_fast_grad(
    step, links, nexts, fgrad, d_lat, lat_rim, d_fone, rim_before, rim_after, w_back, out, cat
):
    frames = d_lat.shape[0]
    base = step * frames
    for f in range(frames):
        last = f == frames - 1
        follow = lat_rim[0] if last else d_lat[f + 1]
        prev_f = rim_before[0, :, CM:] if f == 0 else d_fone[f - 1]
        next_f = rim_after[0, :, CM:] if last else d_fone[f + 1]
        lane = lax.broadcasted_iota(jnp.int32, prev_f.shape, 1)
        rim = jnp.where(lane >= 96, links[base + f] * prev_f.astype(F32), 0.0)
        rim += jnp.where(lane < 32, nexts[base + f] * next_f.astype(F32), 0.0)
        cat[f, :, :CL] = d_lat[f]
        cat[f, :, CL : CL + 128] = d_fone[f]
        cat[f, :, CL + 128 : 2 * CL + 128] = (nexts[base + f] * follow.astype(F32)).astype(BF)
        cat[f, :, 2 * CL + 128 :] = rim.astype(BF)
    value = rows_of(fgrad) + mul_t(rows_of(cat), w_back[...])
    value = value.reshape(-1, ROWS, 4 * CF)
    for q in range(4):
        out[:, q] = value[:, :PIX, q * CF : (q + 1) * CF].astype(BF)


def k_outer_joined(step, slow, lat, right, out, *, parts, taps):
    value = mul_rows(slow if step < parts else lat, right).astype(BF)
    if taps == 1:
        out[...] = value
    else:
        for tap in range(taps):
            out[tap] = value[:, tap * CM : (tap + 1) * CM]


def outer_joined(slow, lat, right, taps, name):
    wide = 256
    parts = slow.shape[-1] // wide
    block = slow.shape[:2] + (wide,)
    rows, lanes = slow.shape[-1] + lat.shape[-1], right.shape[-1]
    if taps == 1:
        out = ((rows, lanes), BF, (wide, lanes), lambda g: (g, 0), True)
    else:
        out = ((taps, rows, CM), BF, (taps, wide, CM), lambda g: (0, g, 0), True)
    return call(
        functools.partial(k_outer_joined, parts=parts, taps=taps),
        rows // wide,
        [
            (slow, block, lambda g: (0, 0, min(g, parts - 1))),
            whole(lat),
            whole(right),
        ],
        [out],
        flops=2 * slow.shape[0] * slow.shape[1] * rows * lanes,
        name=name,
        unroll=True,
    )[0]


def k_outer_out(step, left, right, fleft, fright, out, fout):
    out[...] = mul_rows(left, right).astype(BF)
    value = mul_rows(fleft, fright)
    fout[...] = sum(
        value[q * CFM : (q + 1) * CFM, q * CF : (q + 1) * CF] for q in range(4)
    ).astype(BF)


def lanes_at(value, at):
    return (pltpu.roll(value, (128 - at) % 128, 1) if at else value)[:, :CFM]


def k_outer_space(step, left, right, fleft, fright, out, fout):
    value = mul_rows(left, right).astype(BF)
    for a in range(3):
        out[a, 0] = value[:, a * CM : (a + 1) * CM]
    value = mul_rows(fleft, fright)
    for a in range(3):
        block = value[:, a * 128 : (a + 1) * 128]
        folded = sum(
            lanes_at(block[q * CFM : (q + 1) * CFM], q * CFM) for q in range(4)
        )
        fout[a, 0] = folded.astype(BF)


def k_outer_first(
    step, links, nexts, fast, edge_down, edge_up, d_lat, d_fone, out, fout, z, *, micro
):
    z[...] = jnp.zeros_like(z)
    frames = z.shape[0] // micro
    for m in range(micro):
        part = pl.ds(m * frames, frames)
        fill_z(
            z.at[part], m * frames, links, nexts, fast.at[part],
            edge_down.at[pl.ds(m, 1)], edge_up.at[pl.ds(m, 1)],
        )
    blocks = [4, 5, 0, 1, 2]
    taps = [0.0, 0.0, 0.0]
    fast = mul_rows(z, d_fone)
    lat = mul_rows(z, d_lat)
    for tap, block in enumerate(blocks):
        out[tap * CF : (tap + 1) * CF] = lat[block * CF : (block + 1) * CF].astype(BF)
    for q in range(4):
        for k in range(3):
            block = [5, 0, 1, 2, 3, 6][q + k]
            taps[k] += lanes_at(fast[block * CF : (block + 1) * CF], q * CFM)
    for k in range(3):
        fout[k] = taps[k].astype(BF)


def k_params(step, sums_a, sums_b, sums_c, sums_d, out, fast):
    a, b, c, d = (ref[0] + ref[1] for ref in (sums_a, sums_b, sums_c, sums_d))
    for row, place in enumerate((1, 0)):
        out[row : row + 1, :CL] = d[place : place + 1]
        out[row : row + 1, CL : 2 * CL] = c[place : place + 1, :CM]
        out[row : row + 1, 2 * CL : 3 * CL] = b[place : place + 1, :CM]
        out[row : row + 1, 768:1792] = a[place : place + 1, :CS]
        third = 2 if row == 0 else 0
        out[row : row + 1, 1792:] = a[third : third + 1, :CS]
        fast[row : row + 1] = fold_lanes(c[place : place + 1, CM:], CFM)
        fast[row + 2 : row + 3] = fold_lanes(b[place : place + 1, CM:], CFM)
        fast[row + 4 : row + 5] = fold_lanes(a[place : place + 1, CS:], CF)[:, :128]


def mask_table():
    row = np.arange(ROWS)
    col = row % WW
    real = row < PIX
    table = [real, real & (col != 0), real & (col != WW - 1), real & (row >= WW), row < PIX - WW]
    return np.broadcast_to(np.stack(table)[:, :, None], (5, ROWS, CM)).astype(np.float32)


def as_rows(shard):
    return jnp.pad(shard, (0, -shard.shape[0] % CM)).reshape(-1, CM)


def flat_of(gathered, at, shard, lanes):
    rows = -(-shard.shape[0] // CM)
    part = gathered[:, at : at + rows]
    if shard.shape[0] % CM:
        part = part.reshape(part.shape[0], -1)[:, : shard.shape[0]]
    return part.reshape(-1, lanes)


def local(
    slow_in,
    fast_in,
    clip_starts,
    w_lateral,
    w_slow_time,
    w_slow_space,
    w_slow_out,
    w_projection,
    w_fast_time,
    w_fast_space,
    w_fast_out,
    slow_gain,
    slow_bias,
    fast_gain,
    fast_bias,
    slow_cotangent,
    fast_cotangent,
):
    devices = lax.axis_size(AXES)
    micro, frames = slow_in.shape[:2]
    groups = micro * frames
    masks = jnp.asarray(mask_table())
    count = float(frames * PIX * devices)
    me = lax.axis_index(AXES)
    share = slow_gain.shape[0]
    mine, spots, share_start = has_bits(me), slice_spots(me), me * share

    shards = [
        w_slow_time, w_lateral, w_fast_time, w_fast_space, w_fast_out, slow_gain, slow_bias
    ]
    packed = [as_rows(shard) for shard in shards]
    places = np.cumsum([0] + [part.shape[0] for part in packed])
    packed = jnp.concatenate(packed, 0)
    near = Gather(mine, jnp.pad(packed, ((0, -packed.shape[0] % 8), (0, 0))))
    projection = lax.all_gather(w_projection.reshape(-1, CS), AXES, axis=0, tiled=True)

    slow = pad_rows(slow_in).reshape(groups, ROWS, CS)
    cot = pad_rows(slow_cotangent).reshape(groups, ROWS, CS)
    fast = fast_in.reshape(groups, 4, PIX, CF)
    fcot = to_quads(fast_cotangent)

    link = (1 - clip_starts).astype(F32)
    links = link.reshape(groups)
    nexts = jnp.concatenate([link[:, 1:], jnp.ones((micro, 1), F32)], 1).reshape(groups)
    edge_down = from_before(fast_in[:, -2:])
    edge_up = from_after(fast_in[:, :1] * link[:, :1, None, None].astype(BF))
    slow = tie([near], slow)
    fast, fcot = tie([near], fast, fcot)
    cot = tie([near], cot)

    weights = near.result()
    cuts = [
        flat_of(weights, int(at), shard, lanes)
        for at, shard, lanes in zip(places, shards, (CM, CL, CFM, CFM, CF, share, share))
    ]
    slow_time = cuts[0].reshape(3, CS + CL, CM)
    slow_time = jnp.concatenate([slow_time[tap] for tap in range(3)], -1)
    lateral, fast_time, fast_space, fast_proj = cuts[1:5]
    gb = jnp.stack([cuts[5].reshape(-1), cuts[6].reshape(-1)]).astype(F32)
    fast_both = jnp.stack([fast_gain, fast_bias]).astype(F32)
    fgb = jnp.concatenate(
        [
            jnp.tile(part, (1, 4))
            for part in (fast_both[:, :CFM], fast_both[:, CFM : 2 * CFM], fast_both[:, 2 * CFM :])
        ],
        1,
    )

    fast_time = fast_time.reshape(3, CF, CFM)
    order = [5, 0, 1, 2, 3, 6]
    band = np.zeros((3, 7, 4), np.float32)
    for q in range(4):
        for k in range(3):
            band[k, order[q + k], q] = 1
    band = jnp.asarray(band, BF)
    fast_band = jnp.sum(
        band[:, :, None, :, None] * fast_time[:, None, :, None, :], 0, dtype=F32
    ).astype(BF).reshape(7 * CF, 4 * CFM)
    none = jnp.zeros((CF, CL), BF)
    lat_band = jnp.concatenate([lateral[2 * CF :], none, lateral[: 2 * CF], none], 0)
    w_first = jnp.concatenate([lat_band, fast_band], -1)
    eye4 = jnp.eye(4, dtype=BF)
    fproj = (fast_proj[None, :, None, :] * eye4[:, None, :, None]).reshape(4 * CFM, 4 * CF)
    lat_prev = jnp.concatenate([jnp.zeros((2 * CF, CL), BF), lateral[: 2 * CF]], 0)
    blank = jnp.zeros((CF, 3 * CFM), BF)
    rim_rows = jnp.concatenate(
        [
            jnp.concatenate([blank, fast_time[2]], -1),
            jnp.zeros((2 * CF, 4 * CFM), BF),
            jnp.concatenate([fast_time[0], blank], -1),
        ],
        0,
    )
    w_back = jnp.concatenate([w_first[: 4 * CF], lat_prev, rim_rows], -1)

    links, nexts, w_first, spots, mine, share_start, *mids = tie(
        [], links, nexts, w_first, spots, mine, share_start,
        gb, fgb, fast_space, fproj, w_back, projection, slow_time,
    )
    gb, fgb, fast_space, fproj, w_back, projection, slow_time = mids
    far = Gather(mine, jnp.concatenate([as_rows(w_slow_space), as_rows(w_slow_out)], 0))
    space_rows = -(-w_slow_space.shape[0] // CM)

    rows = groups * ROWS
    bind = functools.partial

    def og(lanes, dtype, per):
        return out_group((groups, ROWS, lanes), dtype, per)

    def os(per, n, lanes):
        return out_stream((micro, n, lanes), F32, frames // per)

    def edge(lanes):
        return out_stream((micro, ROWS, lanes), BF, 1)

    def hooked(*stages):
        return lambda value, stage: tie(stages[stage], value) if stage < len(stages) else value

    lat_pre, fone, sums = call(
        k_first,
        micro,
        [
            scalar(links), scalar(nexts), group(fast, frames), stream(edge_down, 1),
            stream(edge_up, 1), whole(w_first),
        ],
        [og(CL, F32, frames), og(128, F32, frames), os(frames, 2, CL + 128)],
        scratch=[pltpu.VMEM((frames, ROWS, 7 * CF), BF)],
        flops=2 * rows * 896 * 384,
        name="lateral_and_fast_time",
    )
    total1 = all_sum(sums, hooked([far]))

    lat_act, taps, tail, head = call(
        bind(k_taps, count=count),
        micro,
        [
            scalar(links), group(lat_pre, frames), stream(total1, 1), whole(gb),
            group(slow, frames), whole(slow_time), whole(masks),
        ],
        [og(CL, BF, frames), og(3 * CM, F32, frames), edge(CM), edge(CM)],
        flops=2 * rows * 1280 * 768,
        name="slow_time_taps",
    )
    rim_before, rim_after = from_before(tail), from_after(head)
    lat_act, taps = tie([far], lat_act, taps)
    per = frames
    state, fact_cat, sums, fspace = call(
        bind(k_short, steps=1, count=count),
        micro,
        [
            group(slow, per), group(lat_act, per), whole(projection), group(fone, per),
            stream(total1, 1), whole(fgb), whole(fast_space), whole(masks),
        ],
        [
            ("short", per), og(384, BF, per), ("ftwo", per), os(per, 2, CS + 128),
            out_whole((384, 384), BF),
        ],
        state={},
        flops=2 * rows * 1280 * 1024,
        name="shortcut_and_fast_space",
    )
    state, sums = call(
        k_one,
        micro,
        [
            scalar(links), scalar(nexts), group(taps, frames),
            stream(rim_before, 1), stream(rim_after, 1), stream(sums, 1),
        ],
        [("one", frames), os(frames, 2, CS + 128 + CM)],
        state=state,
        name="slow_one",
    )
    total2 = all_sum(sums, hooked([far]))
    weights = far.result()
    space = flat_of(weights, 0, w_slow_space, CM)
    slow_proj = flat_of(weights, space_rows, w_slow_out, CM).reshape(CM, 4, CM)
    slow_proj = jnp.concatenate([slow_proj[:, part] for part in range(4)], -1)

    state, cat_one, fact_two, sums, slow_space = call(
        bind(k_two, steps=1, count=count),
        micro,
        [
            ("one", per), ("ftwo", per), stream(total2, 1), whole(gb), whole(fgb),
            whole(space), whole(fproj), whole(masks),
        ],
        [
            og(3 * CM, BF, per), ("two", per), og(128, BF, per), ("fthree", per),
            os(per, 2, CM + 4 * CF), out_whole((3 * CM, 3 * CM), BF),
        ],
        state=state,
        flops=2 * rows * 768 * 768,
        name="slow_space",
    )
    total3 = all_sum(sums)

    state, act_two, sums = call(
        bind(k_three, steps=1, count=count),
        micro,
        [
            ("two", per), stream(total3, 1), whole(gb), whole(slow_proj),
            whole(masks),
        ],
        [og(CM, BF, per), os(per, 2, CS)],
        state=state,
        flops=2 * rows * 256 * 1024,
        name="slow_three",
    )
    per = 2 if frames % 2 == 0 else 1
    steps = frames // per
    quarters = ((groups, 4, PIX, CF), BF)
    state, fast_out, fsums = call(
        bind(k_fast_out, steps=steps, count=count),
        groups // per,
        [
            ("fthree", per), group(fast, per), group(fcot, per), stream(total3, steps),
            whole(fgb),
        ],
        [out_group(*quarters, per, False), ("fgrad", per), os(per, 2, 4 * CF)],
        state=state,
        scratch=[pltpu.VMEM((2, 8, 4 * CF), F32)],
        flops=rows * 512 * 200,
        name="fast_out",
    )
    total4 = all_sum(sums)

    state, slow_out, sums = call(
        bind(k_out, steps=steps, count=count),
        groups // per,
        [
            group(act_two, per), whole(slow_proj), ("short", per), group(cot, per),
            stream(total4, steps), stream(total2, steps), whole(gb), stream(fsums, steps),
        ],
        [
            out_group((groups, PIX, CS), BF, per, False), ("grad", per), os(per, 3, CS + 4 * CF),
        ],
        state=state,
        scratch=[pltpu.VMEM((per, ROWS, CS), F32), pltpu.VMEM((3, 8, CS), F32)],
        flops=2 * rows * 256 * 1024,
        name="slow_out",
    )
    sums_a = all_sum(sums)

    def pixels_first(value, whole_shape):
        return jnp.swapaxes(value.reshape(whole_shape), 1, 2)

    state, d_three, d_short, d_fthree, sums = call(
        bind(k_back_three, steps=steps, count=count),
        groups // per,
        [
            group(act_two, per), whole(slow_proj), ("short", per), ("grad", per),
            stream(total4, steps), stream(total2, steps), stream(sums_a, steps), whole(gb),
            ("two", per), stream(total3, steps), ("fgrad", per), ("fthree", per),
            ("ftwo", per), whole(fgb), whole(fproj), whole(masks),
        ],
        [
            og(CS, BF, per), og(CS, BF, per), ("grad_two", per), og(4 * CF, BF, per),
            ("fgrad_two", per), os(per, 2, CM + 128),
        ],
        state=state,
        scratch=[pltpu.VMEM((per, ROWS, CS), F32)],
        flops=4 * rows * 256 * 1024,
        name="back_three",
    )

    def shares(value):
        return value.reshape(devices, -1, value.shape[-1])

    flows = {}

    def weights_of_three(value, stage):
        if stage == 0:
            proj_grad = outer_joined(slow, lat_act, d_short, 1, "projection_grad")
            out_grad, flows["fast_out"] = call(
                k_outer_out,
                1,
                [whole(act_two), whole(d_three), whole(fact_two), whole(d_fthree)],
                [out_whole((CM, CS), BF), out_whole((CFM, CF), BF)],
                flops=2 * rows * 256 * 1024,
                name="slow_out_grad",
            )
            value, proj_grad, out_grad = tie([], value, proj_grad, out_grad)
            both = jnp.concatenate([shares(proj_grad), shares(out_grad)], 1)
            flows["a"] = Shares(spots, both)
            flows["proj_rows"] = proj_grad.shape[0] // devices
        elif stage == 1:
            value = tie([flows["a"]], value)
        return value

    sums_b = all_sum(sums, weights_of_three)

    per = frames
    state, two_taps, ftwo_taps, sums = call(
        bind(k_back_two, steps=1, count=count),
        micro,
        [
            ("two", per), stream(total3, 1), ("grad_two", per),
            stream(sums_b, 1), whole(gb), whole(slow_space), ("one", per),
            stream(total2, 1), ("ftwo", per), ("fgrad_two", per), whole(fgb),
            whole(fspace), group(fone, per), stream(total1, 1), whole(masks),
        ],
        [
            og(3 * CM, BF, per), ("grad_one", per), og(384, BF, per), ("fgrad_one", per),
            os(per, 2, CM + 128),
        ],
        state=state,
        flops=2 * rows * 768 * 768,
        name="back_two",
    )
    block = (groups, ROWS, CM)
    slim = (groups, ROWS, 128)

    def weights_of_two(value, stage):
        if stage == 0:
            flows["space"], flows["fspace"] = call(
                k_outer_space,
                3,
                [
                    (cat_one, block, lambda g: (0, 0, g)), whole(two_taps),
                    (fact_cat, slim, lambda g: (0, 0, g)), whole(ftwo_taps),
                ],
                [
                    ((3, 3, CM, CM), BF, (3, 1, CM, CM), lambda g: (0, g, 0, 0), True),
                    ((3, 3, CFM, CFM), BF, (3, 1, CFM, CFM), lambda g: (0, g, 0, 0), True),
                ],
                flops=2 * rows * 768 * 768,
                name="slow_space_grad",
                unroll=True,
            )
            value, flows["space"] = tie([], value, flows["space"])
        elif stage == 1:
            value = tie([flows["a"]], value)
        return value

    sums_c = all_sum(sums, weights_of_two)

    state, d_one, d_fone, tail, head = call(
        bind(k_back_one, count=count),
        micro,
        [
            scalar(links), ("one", frames), stream(total2, 1), ("grad_one", frames),
            group(fone, frames), stream(total1, 1), ("fgrad_one", frames), stream(sums_c, 1),
            whole(gb), whole(fgb), whole(masks),
        ],
        [og(CM, BF, frames), og(128, BF, frames), edge(CM + 128), edge(CM + 128)],
        state=state,
        name="back_one",
    )
    rim_before, rim_after = from_before(tail), from_after(head)
    slow_out = pixels_first(slow_out, slow_in.shape)
    rim_before, rim_after, slow_out = tie([], rim_before, rim_after, slow_out)
    state, trio, sums = call(
        bind(k_trio, count=count),
        micro,
        [
            scalar(links), scalar(nexts), group(d_one, frames),
            stream(rim_before, 1), stream(rim_after, 1), group(d_short, frames),
            whole(slow_time), whole(projection),
            group(lat_pre, frames), stream(total1, 1), whole(gb),
        ],
        [og(3 * CM, BF, frames), ("lat_grad", frames), os(frames, 2, CL)],
        state=state,
        flops=2 * rows * 1792 * 256,
        name="back_lateral",
    )

    def weights_of_one(value, stage):
        if stage == 0:
            time_grad = outer_joined(slow, lat_act, trio, 3, "slow_time_grad")
            value, time_grad = tie([flows["a"]], value, time_grad)
            both = jnp.concatenate([shares(time_grad), shares(flows["space"])], 1)
            flows["b"] = Shares(spots, both)
            flows["time_rows"] = time_grad.shape[0] * time_grad.shape[1] // devices
        elif stage == 1:
            value = tie([flows["b"]], value)
        return value

    sums_d = all_sum(sums, weights_of_one)

    state, d_lat, head = call(
        bind(k_back_lat, count=count),
        micro,
        [
            scalar(links), group(lat_pre, frames), stream(total1, 1), ("lat_grad", frames),
            stream(sums_d, 1), whole(gb), whole(masks),
        ],
        [og(CL, BF, frames), edge(CL)],
        state=state,
        name="back_lat",
    )
    lat_rim = from_after(head)
    first_grad, ftime_grad = call(
        bind(k_outer_first, micro=micro),
        1,
        [
            scalar(links), scalar(nexts), whole(fast), whole(edge_down), whole(edge_up),
            whole(d_lat), whole(d_fone),
        ],
        [out_whole((5 * CF, CL), BF), out_whole((3, CF, CFM), BF)],
        scratch=[pltpu.VMEM((groups, ROWS, 7 * CF), BF)],
        flops=2 * rows * 896 * 384,
        name="lateral_grad",
    )
    flat = [
        part.reshape(devices, -1)
        for part in (first_grad, ftime_grad, flows["fspace"], flows["fast_out"])
    ]
    sizes = [part.shape[1] for part in flat]
    flat = jnp.concatenate(flat, 1)
    flat = jnp.pad(flat, ((0, 0), (0, -flat.shape[1] % 1024)))
    flat = flat.reshape(devices, -1, 128)
    trio, flat = tie([], trio, flat)
    last = Shares(spots, flat)
    per = frames
    slow_in_grad = call(
        k_slow_grad,
        micro,
        [group(trio, per), group(d_short, per), whole(slow_time), whole(projection)],
        [out_group((groups, PIX, CS), BF, per, False)],
        flops=2 * rows * 1792 * 1024,
        name="slow_in_grad",
    )[0]
    lat_rim, slow_in_grad = tie([flows["b"], last], lat_rim, slow_in_grad)
    state, fast_in_grad = call(
        k_fast_grad,
        micro,
        [
            scalar(links), scalar(nexts), ("fgrad", frames), group(d_lat, frames),
            stream(lat_rim, 1), group(d_fone, frames), stream(rim_before, 1),
            stream(rim_after, 1), whole(w_back),
        ],
        [out_group(*quarters, frames, False)],
        state=state,
        scratch=[pltpu.VMEM((frames, ROWS, 768), BF)],
        flops=2 * rows * 768 * 512,
        name="fast_in_grad",
    )
    fast_in_grad, slow_in_grad = tie([flows["b"], last], fast_in_grad, slow_in_grad)
    both_out = flows["a"].result().reshape(-1, CS)
    cut = flows["proj_rows"]
    proj_out, out_out = both_out[:cut].reshape(-1), both_out[cut:].reshape(-1)
    both_out = flows["b"].result().reshape(-1, CM)
    cut = flows["time_rows"]
    time_out, space_out = both_out[:cut].reshape(-1), both_out[cut:].reshape(-1)
    flat = last.result()
    smalls = []
    at = 0
    for size in sizes:
        smalls.append(flat[at : at + size])
        at += size

    norms, fnorms = call(
        k_params,
        1,
        [whole(sums_a), whole(sums_b), whole(sums_c), whole(sums_d)],
        [out_whole((2, 2816), F32), out_whole((8, 128), F32)],
        name="norm_grads",
    )
    norms = pick(norms, share_start, share, 1)
    fast_gain_grad, fast_bias_grad = (
        jnp.concatenate([fnorms[row, :CFM], fnorms[row + 2, :CFM], fnorms[row + 4]])
        for row in range(2)
    )
    return (
        jnp.swapaxes(slow_out, 1, 2),
        fast_out.reshape(fast_in.shape),
        slow_in_grad.reshape(slow_in.shape),
        fast_in_grad.reshape(fast_in.shape),
        smalls[0],
        time_out,
        space_out,
        out_out,
        proj_out,
        smalls[1],
        smalls[2],
        smalls[3],
        norms[0],
        norms[1],
        fast_gain_grad,
        fast_bias_grad,
    )


def solution(mesh):
    frames = P(None, AXES, None, None)
    flat = P(AXES)
    return jax.shard_map(
        local,
        mesh=mesh,
        in_specs=(frames, frames, P(None, AXES))
        + (flat,) * 10
        + (P(), P(), frames, frames),
        out_specs=(frames,) * 4 + (flat,) * 10 + (P(), P()),
        check_vma=False,
    )
```

```python
import functools
import math

import jax
import jax.numpy as jnp
import numpy as np
from jax import lax
from jax.experimental import pallas as pl
from jax.experimental.pallas import tpu as pltpu
from jax.sharding import PartitionSpec as P

CS = 1024
CL = 256
CM = 256
CF = 128
CFM = 32
HH = 14
WW = 14
PIX = HH * WW
ROWS = 208
EPS = 1e-05
AXES = ("path", "dp")
BF = jnp.bfloat16
F32 = jnp.float32


def swap(value, bit):
    count = lax.axis_size(AXES)
    return lax.ppermute(value, AXES, [(i, i ^ bit) for i in range(count)])


def dp_pairs():
    bits = []
    bit = 1
    while bit < lax.axis_size("dp"):
        bits.append(bit)
        bit *= 2
    return [bits[at : at + 2] for at in range(0, len(bits), 2)]


def all_sum(value, hook=lambda value, stage: value):
    value = hook(value + swap(value, lax.axis_size("dp")), 0)
    for stage, pair in enumerate(dp_pairs()):
        if len(pair) == 1:
            value = value + swap(value, pair[0])
        else:
            one, two = pair
            first, second, third = swap(value, one), swap(value, two), swap(value, one + two)
            value = (value + first) + (second + third)
        value = hook(value, stage + 1)
    return value


def has_bits(me):
    bits = [bit for pair in dp_pairs() for bit in pair] + [lax.axis_size("dp")]
    return {bit: (me & bit) != 0 for bit in bits}


def in_order(parts, bits, mine):
    parts = [part[None] for part in parts]
    step = 1
    for bit in bits:
        parts = [jnp.where(mine[bit], parts[k ^ step], parts[k]) for k in range(len(parts))]
        step *= 2
    return jnp.concatenate(parts, 0)


class Gather:
    def __init__(self, mine, value):
        self.mine = mine
        self.shape = value.shape
        self.value = value[None]
        self.stages = dp_pairs()[::-1] + [[lax.axis_size("dp")]]
        self.flight = None
        self.start()

    def start(self):
        if not self.stages:
            self.value = self.value.reshape((-1,) + self.shape)
            return
        self.bits = self.stages.pop(0)
        steps = [
            sum(bit for n, bit in enumerate(self.bits) if k >> n & 1)
            for k in range(1, 2 ** len(self.bits))
        ]
        self.flight = [swap(self.value, step) for step in steps]

    def finish(self):
        stacked = in_order([self.value] + self.flight, self.bits, self.mine)
        if self.stages:
            stacked = jnp.swapaxes(stacked, 0, 1)
        self.value = stacked.reshape((-1,) + self.shape)
        self.flight = None
        self.start()

    def result(self):
        while self.flight is not None:
            self.finish()
        return self.value


def pick(value, start, extent, axis):
    starts = [jnp.int32(0)] * value.ndim
    starts[axis] = start
    sizes = list(value.shape)
    sizes[axis] = extent
    return lax.dynamic_slice(value, starts, sizes, allow_negative_indices=False)


def share_stages():
    return [[lax.axis_size("dp")]] + dp_pairs()


def slice_spots(me):
    spots = []
    for bits in share_stages():
        count = 2 ** len(bits)
        spot = lax.shift_right_logical(me, bits[0].bit_length() - 1) & (count - 1)
        spots.append([spot ^ k for k in range(count)])
    return spots


class Shares:
    def __init__(self, spots, value):
        self.value = value
        self.stages = list(zip(share_stages(), spots))
        self.flight = None
        self.start()

    def start(self):
        if not self.stages:
            return
        bits, spots = self.stages.pop(0)
        count = 2 ** len(bits)
        rest = self.value.shape[-2:]
        axis = 0 if bits[0] == lax.axis_size("dp") else 1
        shaped = self.value.reshape(((2, -1), (-1, count))[axis] + rest)
        parts = [pick(shaped, spot, 1, axis) for spot in spots]
        parts = [part.reshape((-1,) + rest) for part in parts]
        self.keep = parts[0]
        steps = [sum(bit for n, bit in enumerate(bits) if k >> n & 1) for k in range(1, count)]
        self.flight = [swap(part.astype(BF), step) for part, step in zip(parts[1:], steps)]

    def finish(self):
        terms = [self.keep.astype(F32)] + [part.astype(F32) for part in self.flight]
        while len(terms) > 1:
            terms = [sum(terms[at : at + 2]) for at in range(0, len(terms), 2)]
        self.value = terms[0]
        self.flight = None
        self.start()

    def result(self):
        while self.flight is not None:
            self.finish()
        return self.value.reshape(-1)


def tie(flows, *values):
    flows = [flow for flow in flows if flow.flight is not None]
    values, flights = lax.optimization_barrier((values, [flow.flight for flow in flows]))
    for flow, flight in zip(flows, flights):
        flow.flight = flight
        flow.finish()
    return values if len(values) > 1 else values[0]


def from_before(value):
    count = lax.axis_size(AXES)
    return lax.ppermute(value, AXES, [(i, i + 1) for i in range(count - 1)])


def from_after(value):
    count = lax.axis_size(AXES)
    return lax.ppermute(value, AXES, [(i + 1, i) for i in range(count - 1)])


def gelu_tan(value):
    return jnp.tanh(value * (0.7978845608028654 + 0.035677408136300125 * (value * value)))


def gelu(value):
    return value * (0.5 + 0.5 * gelu_tan(value))


def gelu_slope(value):
    tan = gelu_tan(value)
    inner = 0.7978845608028654 + 0.10703222440890037 * (value * value)
    return (0.5 + 0.5 * tan) + (0.5 * value) * (1.0 - tan * tan) * inner


def pad_rows(value):
    return jnp.pad(value, [(0, 0)] * (value.ndim - 2) + [(0, ROWS - PIX), (0, 0)])


def to_quads(value):
    micro, frames, _, lanes = value.shape
    quads = pad_rows(value).reshape(micro * frames // 4, 4, ROWS, lanes)
    return jnp.concatenate([quads[:, place] for place in range(4)], -1)


def in_vmem(array):
    return pltpu.with_memory_space_constraint(array, pltpu.VMEM)


PARTS = dict(
    short=CS,
    grad=CS,
    grad_two=CM,
    fgrad_two=128,
    grad_one=CM,
    fgrad_one=128,
    lat_grad=CL,
    fthree=4 * CF,
    fgrad=4 * CF,
    one=CM,
    two=CM,
    ftwo=128,
)


def in_vmem(array):
    return pltpu.with_memory_space_constraint(array, pltpu.VMEM)


def call(body, steps, ins, outs, scratch=(), flops=0, name=None, limit=8, unroll=False, state=None):
    names = [given[0] if len(given) == 2 else None for given in outs]
    ins = [group(state[given[0]], given[1]) if len(given) == 2 else given for given in ins]
    if state is not None:
        groups = ins[0][0].shape[0] if not state else next(iter(state.values())).shape[0]
    outs = [
        out_group((groups, ROWS, PARTS[given[0]]), F32, given[1]) if len(given) == 2 else given
        for given in outs
    ]
    arrays = [array for array, _, _ in ins]
    blocks = [(array.shape, block, index) for array, block, index in ins]
    blocks += [(shape, block, index) for shape, _, block, index, _ in outs]

    def view(ref, shape, block, index, step):
        if block is None or tuple(block) == tuple(shape):
            return ref
        spot = [
            slice(None) if size == full else pl.ds(place * size, size)
            for place, size, full in zip(index(step), block, shape)
        ]
        return ref.at[tuple(spot)]

    def kernel(*refs):
        def run(step, carry):
            views = [view(ref, *given, step) for ref, given in zip(refs, blocks)]
            body(step, *views, *refs[len(blocks) :])
            return carry

        if steps == 1 or unroll:
            for step in range(steps):
                run(step, 0)
        else:
            lax.fori_loop(0, steps, run, 0)

    moved = sum(array.size * array.dtype.itemsize for array in arrays)
    moved += sum(math.prod(shape) * jnp.dtype(dtype).itemsize for shape, dtype, *_ in outs)
    vmem = pl.BlockSpec(memory_space=pltpu.VMEM)
    result = pl.pallas_call(
        kernel,
        in_specs=[
            pl.BlockSpec(memory_space=pltpu.SMEM) if block is None else vmem
            for _, block, _ in ins
        ],
        out_specs=[vmem] * len(outs),
        out_shape=[
            pltpu.VMEM(shape, dtype) if stays else jax.ShapeDtypeStruct(shape, dtype)
            for shape, dtype, _, _, stays in outs
        ],
        scratch_shapes=list(scratch),
        compiler_params=pltpu.CompilerParams(vmem_limit_bytes=limit * 1024 * 1024),
        cost_estimate=pl.CostEstimate(
            flops=int(flops), bytes_accessed=int(moved), transcendentals=0
        ),
        name=name,
    )(*[array if block is None else in_vmem(array) for array, block, _ in ins])
    if state is None:
        return result
    fresh = {name: array for name, array in zip(names, result) if name}
    return [{**state, **fresh}] + [array for name, array in zip(names, result) if not name]


def group(array, per):
    tail = (0,) * (array.ndim - 1)
    return (array, (per,) + array.shape[1:], lambda g: (g,) + tail)


def whole(array):
    return (array, array.shape, None)


def scalar(array):
    return (array, None, None)


def stream(array, steps):
    tail = (0,) * (array.ndim - 1)
    return (array, (1,) + array.shape[1:], lambda g: (g // steps,) + tail)


def out_group(shape, dtype, per, stays=True):
    tail = (0,) * (len(shape) - 1)
    return (shape, dtype, (per,) + shape[1:], lambda g: (g,) + tail, stays)


def out_stream(shape, dtype, steps, stays=True):
    tail = (0,) * (len(shape) - 1)
    return (shape, dtype, (1,) + shape[1:], lambda g: (g // steps,) + tail, stays)


def out_whole(shape, dtype, stays=True):
    return (shape, dtype, shape, None, stays)


def rows_of(ref):
    return ref[...].reshape(-1, ref.shape[-1])


def put(ref, value):
    ref[...] = value.reshape(ref.shape).astype(ref.dtype)


def spread(value, mask):
    lanes = value.shape[-1]
    shaped = value.reshape(-1, ROWS, lanes) * mask[None, :, :lanes]
    return shaped.reshape(value.shape)


def add_rows(ref, step, steps, lanes, *values):
    first = step % steps == 0
    for row, value in enumerate(values):
        total = jnp.sum(value, 0, keepdims=True)
        spot = (0, slice(row, row + 1), slice(lanes, lanes + value.shape[-1]))
        if steps > 1:
            total = jnp.where(first, 0.0, ref[spot]) + total
        ref[spot] = total


def stats(total, start, extent, count, folded=0):
    first = total[0, 0:1, start : start + extent]
    second = total[0, 1:2, start : start + extent]
    if folded:
        first, second = fold_lanes(first, folded), fold_lanes(second, folded)
    mean = first / count
    return mean, lax.rsqrt(second / count - mean * mean + EPS)


def fold_lanes(vector, width):
    lanes = vector.shape[-1]
    if width % 128 == 0:
        parts = [vector[:, at : at + width] for at in range(0, lanes, width)]
        one = (parts[0] + parts[1]) + (parts[2] + parts[3])
        return jnp.concatenate([one] * 4, -1)
    wide = jnp.broadcast_to(vector, (8, lanes))
    wide = wide + pltpu.roll(wide, 2 * width, 1)
    wide = wide + pltpu.roll(wide, width, 1)
    return wide[0:1]


def back_parts(sums, start, extent, count, folded=0, rows=(0, 1)):
    one = sums[0, rows[0] : rows[0] + 1, start : start + extent]
    two = sums[0, rows[1] : rows[1] + 1, start : start + extent]
    if folded:
        one, two = fold_lanes(one, folded), fold_lanes(two, folded)
    return one / count, two / count


def norm_back(grad, hat, factor, one, two):
    return factor * (grad - one - hat * two)


def turn(value, step):
    return pltpu.roll(value, step % value.shape[0], 0)


def mul(left, right):
    return jnp.dot(left, right, preferred_element_type=F32)


def mul_t(left, right):
    return lax.dot_general(left, right, (((1,), (1,)), ((), ())), preferred_element_type=F32)


def mul_rows(left, right):
    return lax.dot_general(
        rows_of(left), rows_of(right), (((0,), (0,)), ((), ())), preferred_element_type=F32
    )


def column_cat(act, masks):
    act = act.astype(BF).astype(F32)
    left = spread(turn(act, 1), masks[1])
    right = spread(turn(act, -1), masks[2])
    return jnp.concatenate([left.astype(BF), act.astype(BF), right.astype(BF)], -1)


def row_sum(taps, masks):
    lanes = taps.shape[-1] // 3
    return (
        spread(turn(taps[:, :lanes], WW), masks[3])
        + taps[:, lanes : 2 * lanes]
        + spread(turn(taps[:, 2 * lanes :], -WW), masks[4])
    )


def row_cat(grad, masks):
    grad = grad.astype(BF).astype(F32)
    above = spread(turn(grad, -WW), masks[4])
    below = spread(turn(grad, WW), masks[3])
    return jnp.concatenate([above.astype(BF), grad.astype(BF), below.astype(BF)], -1)


def column_sum(taps, masks):
    lanes = taps.shape[-1] // 3
    return (
        spread(turn(taps[:, :lanes], -1), masks[2])
        + taps[:, lanes : 2 * lanes]
        + spread(turn(taps[:, 2 * lanes :], 1), masks[1])
    )


def k_prep(
    step, near, w_time, w_first, w_back, fproj, fspace, gb, wide, lat, fast, *, shares
):
    places = [sum(shares[:n]) for n in range(len(shares))]
    devices = near.shape[0]
    starts = [0, 3 * CF, 3 * CF + 9 * CFM]
    for d in range(devices):
        block = near[d].astype(F32)
        parts = [block[at : at + rows] for at, rows in zip(places, shares)]
        wide[d * shares[0] : (d + 1) * shares[0]] = parts[0]
        lat[d * shares[1] : (d + 1) * shares[1]] = parts[1]
        for start, part in zip(starts, parts[2:5]):
            at = start + d * part.shape[0]
            fast[at : at + part.shape[0]] = part[:, :128]
    for tap in range(3):
        rows = CS + CL
        w_time[:, tap * CM : (tap + 1) * CM] = wide[tap * rows : (tap + 1) * rows].astype(BF)

    w_first[...] = jnp.zeros_like(w_first)
    w_first[: 3 * CF, :CL] = lat[2 * CF :].astype(BF)
    w_first[4 * CF : 6 * CF, :CL] = lat[: 2 * CF].astype(BF)
    taps = [fast[k * CF : (k + 1) * CF] for k in range(3)]
    order = [5, 0, 1, 2, 3, 6]
    for block in range(7):
        band = [
            pltpu.roll(taps[k], q * CFM, 1) if q else taps[k]
            for q in range(4)
            for k in range(3)
            if order[q + k] == block
        ]
        if band:
            w_first[block * CF : (block + 1) * CF, CL:] = sum(band).astype(BF)
    w_back[...] = jnp.zeros_like(w_back)
    w_back[:, : CL + 128] = w_first[: 4 * CF]
    w_back[2 * CF :, CL + 128 : 2 * CL + 128] = lat[: 2 * CF].astype(BF)
    w_back[:CF, 2 * CL + 128 :] = pltpu.roll(taps[2], 3 * CFM, 1).astype(BF)
    w_back[3 * CF :, 2 * CL + 128 :] = taps[0].astype(BF)

    fproj[...] = jnp.zeros_like(fproj)
    last = fast[starts[2] : starts[2] + CFM].astype(BF)
    for q in range(4):
        fproj[q * CFM : (q + 1) * CFM, q * CF : (q + 1) * CF] = last
    for a in range(3):
        for c in range(3):
            at = starts[1] + (3 * a + c) * CFM
            tap = fast[at : at + CFM]
            for q in range(4):
                rows = c * 128 + q * CFM
                moved = pltpu.roll(tap, q * CFM, 1) if q else tap
                fspace[rows : rows + CFM, a * 128 : (a + 1) * 128] = moved.astype(BF)

    lane = lax.broadcasted_iota(jnp.int32, (8, 128), 1)
    extent = gb.shape[1] // devices
    for row in range(2):
        own = [
            jnp.broadcast_to(
                near[d, places[5 + row] : places[5 + row] + 1, :128].astype(F32), (8, 128)
            )
            for d in range(devices)
        ]
        for tile in range(gb.shape[1] // 128):
            value = jnp.zeros((8, 128), F32)
            for d in range(devices):
                at = d * extent - tile * 128
                if -extent < at < 128:
                    mine = (lane >= at) & (lane < at + extent)
                    moved = pltpu.roll(own[d], at % 128, 1) if at % 128 else own[d]
                    value = jnp.where(mine, moved, value)
            gb[row : row + 1, tile * 128 : (tile + 1) * 128] = value[0:1]


def fill_z(z, at, links, nexts, fast, edge_down, edge_up):
    frames = fast.shape[0]
    for f in range(frames):
        link, following = links[at + f], nexts[at + f]
        for q in range(4):
            z[f, :PIX, q * CF : (q + 1) * CF] = fast[f, q]
        for q in range(2):
            prev = edge_down[0, q] if f == 0 else fast[f - 1, 2 + q]
            z[f, :PIX, (4 + q) * CF : (5 + q) * CF] = (link * prev.astype(F32)).astype(BF)
        follow = edge_up[0, 0] if f == frames - 1 else fast[f + 1, 0]
        z[f, :PIX, 6 * CF :] = (following * follow.astype(F32)).astype(BF)


def k_first(
    step, links, nexts, fast, edge_down, edge_up, weight, lat, fone, total, z
):
    z[...] = jnp.zeros_like(z)
    fill_z(z, step * fast.shape[0], links, nexts, fast, edge_down, edge_up)
    value = mul(rows_of(z), weight[...])
    put(lat, value[:, :CL])
    put(fone, value[:, CL:])
    add_rows(total, step, 1, 0, value, value * value)


def k_taps(step, links, lat, total, gb, slow, w_time, masks, lat_act, taps, tail, head, *, count):
    frames = slow.shape[0]
    mean, scale = stats(total, 0, CL, count)
    hat = (rows_of(lat) - mean) * scale
    act = spread(gelu(hat * gb[0:1, :CL] + gb[1:2, :CL]), masks[0]).astype(BF)
    put(lat_act, act)
    value = mul(rows_of(slow), w_time[:CS]) + mul(act, w_time[CS:])
    put(taps, value)
    tail[0] = value[(frames - 1) * ROWS :, :CM].astype(BF)
    head[0] = (links[step * frames] * value[:ROWS, 2 * CM :]).astype(BF)


def k_short(
    step, slow, lat_act, w_proj, fone, total, fgb, fspace, masks,
    short, fact, ftwo, sums, *, steps, count
):
    value = mul(rows_of(slow), w_proj[:CS]) + mul(rows_of(lat_act), w_proj[CS:])
    put(short, value)
    add_rows(sums, step, steps, 0, value, value * value)
    mean, scale = stats(total, CL, 128, 4.0 * count, CFM)
    hat = (rows_of(fone) - mean) * scale
    act = spread(gelu(hat * fgb[0:1, :128] + fgb[1:2, :128]), masks[0])
    cat = column_cat(act, masks)
    put(fact, cat)
    value = row_sum(mul(cat, fspace[...]), masks)
    put(ftwo, value)
    add_rows(sums, step, steps, CS, value, value * value)


def k_one(step, links, nexts, taps, rim_before, rim_after, given, slow_one, sums):
    frames = taps.shape[0]
    base = step * frames
    one = two = 0.0
    for f in range(frames):
        prev = rim_before[0].astype(F32) if f == 0 else taps[f - 1, :, :CM]
        follow = rim_after[0].astype(F32) if f == frames - 1 else taps[f + 1, :, 2 * CM :]
        value = links[base + f] * prev + taps[f, :, CM : 2 * CM] + nexts[base + f] * follow
        slow_one[f] = value
        one += jnp.sum(value, 0, keepdims=True)
        two += jnp.sum(value * value, 0, keepdims=True)
    sums[0, :, : CS + 128] = given[0]
    sums[0, 0:1, CS + 128 :] = one
    sums[0, 1:2, CS + 128 :] = two


def k_two(
    step, slow_one, ftwo, total, gb, fgb, space, fproj, masks,
    cat_out, two_out, fact_out, fthree, sums, w_space, *, steps, count
):
    @pl.when(step == 0)
    def _():
        for a in range(3):
            for c in range(3):
                tap = space[(3 * a + c) * CM : (3 * a + c + 1) * CM]
                w_space[c * CM : (c + 1) * CM, a * CM : (a + 1) * CM] = tap

    mean, scale = stats(total, CS + 128, CM, count)
    hat = (rows_of(slow_one) - mean) * scale
    act = spread(gelu(hat * gb[0:1, CL : 2 * CL] + gb[1:2, CL : 2 * CL]), masks[0])
    cat = column_cat(act, masks)
    put(cat_out, cat)
    value = row_sum(mul(cat, w_space[...]), masks)
    put(two_out, value)
    add_rows(sums, step, steps, 0, value, value * value)
    mean, scale = stats(total, CS, 128, 4.0 * count, CFM)
    hat = (rows_of(ftwo) - mean) * scale
    act = spread(gelu(hat * fgb[0:1, 128:256] + fgb[1:2, 128:256]), masks[0]).astype(BF)
    put(fact_out, act)
    value = mul(act, fproj[...])
    put(fthree, value)
    add_rows(sums, step, steps, CM, value, value * value)


def k_three(
    step, slow_two, total, gb, rows_out, masks, act_out, sums, w_out, wide, *, steps, count
):
    @pl.when(step == 0)
    def _():
        for half in range(2):
            wide[half] = rows_out[:, half * 128 : (half + 1) * 128].astype(F32)
            for j in range(4):
                at = j * CM + half * 128
                w_out[:, at : at + 128] = wide[half, pl.ds(j, CM, stride=4), :].astype(BF)
    mean, scale = stats(total, 0, CM, count)
    hat = (rows_of(slow_two) - mean) * scale
    act = gelu(hat * gb[0:1, 2 * CL : 3 * CL] + gb[1:2, 2 * CL : 3 * CL])
    act = spread(act, masks[0]).astype(BF)
    put(act_out, act)
    value = mul(act, w_out[...])
    add_rows(sums, step, steps, 0, value, value * value)


CHUNK = 16
SPAN = 512


def gelu_both(value):
    square = value * value
    tan = jnp.tanh(value * (0.7978845608028654 + 0.035677408136300125 * square))
    half = 0.5 + 0.5 * tan
    inner = 0.7978845608028654 + 0.10703222440890037 * square
    slope = half + (0.5 * value) * (1.0 - tan * tan) * inner
    return value * half, slope


def chunked(body, frames, lanes, first=lambda f: None):
    full = PIX // CHUNK
    last = full * CHUNK

    def frame(f, carry):
        first(f)

        def step(i, carry):
            at = pl.ds(pl.multiple_of(i * CHUNK, CHUNK), CHUNK)
            for start in range(0, lanes, SPAN):
                body(f, at, CHUNK, slice(start, start + SPAN))
            return carry

        lax.fori_loop(0, full, step, 0)
        for start in range(0, lanes, SPAN):
            body(f, pl.ds(last, CHUNK), PIX - last, slice(start, start + SPAN))
        return carry

    lax.fori_loop(0, frames, frame, 0)


def halves(value):
    return value[:8] + value[8:]


def k_fast_out(step, fthree, fast, cot, total, fgb, out, grad, sums, acc, *, steps, count):
    mean, scale = stats(total, CM, 4 * CF, 4.0 * count, CF)
    gain, bias = fgb[0:1, 256:], fgb[1:2, 256:]

    @pl.when(step % steps == 0)
    def _():
        acc[...] = jnp.zeros_like(acc)

    def body(f, rows, real, lanes):
        hat = (fthree[f, rows, lanes] - mean[:, lanes]) * scale[:, lanes]
        quads = [fast[f, q, pl.ds(rows.start, real), :].astype(F32) for q in range(4)]
        if real < CHUNK:
            blank = jnp.zeros((CHUNK - real, CF), F32)
            quads = [jnp.concatenate([part, blank], 0) for part in quads]
        value = hat * gain[:, lanes] + bias[:, lanes] + jnp.concatenate(quads, -1)
        act, slope = gelu_both(value)
        act = act.astype(BF)
        for q in range(4):
            piece = act[:real, q * CF : (q + 1) * CF]
            out[f, q, pl.ds(rows.start, real), :] = piece
        slope = slope * cot[f, rows, lanes].astype(F32)
        grad[f, rows, lanes] = slope
        acc[0] += halves(slope)
        acc[1] += halves(slope * hat)

    chunked(body, fthree.shape[0], 4 * CF)

    @pl.when(step % steps == steps - 1)
    def _():
        for row in range(2):
            sums[0, row : row + 1] = jnp.sum(acc[row], 0, keepdims=True)


def k_out(
    step, act, w_out, short, cot, total, short_total, gb, given, out, grad_out, sums, three, acc,
    *, steps, count
):
    def expand(f):
        three[...] = mul(act[f], w_out[...])

    mean_a, scale_a = stats(total, 0, CS, count)
    mean_b, scale_b = stats(short_total, 0, CS, count)
    gain_a, gain_b = gb[0:1, 768:1792], gb[0:1, 1792:]
    bias = gb[1:2, 768:1792] + gb[1:2, 1792:]

    @pl.when(step % steps == 0)
    def _():
        acc[...] = jnp.zeros_like(acc)

    def body(f, rows, real, lanes):
        hat_a = (three[rows, lanes] - mean_a[:, lanes]) * scale_a[:, lanes]
        hat_b = (short[f, rows, lanes] - mean_b[:, lanes]) * scale_b[:, lanes]
        value = hat_a * gain_a[:, lanes] + (hat_b * gain_b[:, lanes] + bias[:, lanes])
        smooth, slope = gelu_both(value)
        out[f, pl.ds(rows.start, real), lanes] = smooth.astype(BF)[:real]
        grad = slope * cot[f, rows, lanes].astype(F32)
        grad_out[f, rows, lanes] = grad
        acc[0, :, lanes] += halves(grad)
        acc[1, :, lanes] += halves(grad * hat_a)
        acc[2, :, lanes] += halves(grad * hat_b)

    chunked(body, act.shape[0], CS, expand)

    @pl.when(step % steps == steps - 1)
    def _():
        for row in range(3):
            sums[0, row : row + 1, :CS] = jnp.sum(acc[row], 0, keepdims=True)
        sums[0, 0:2, CS:] = given[0]
        sums[0, 2:3, CS:] = jnp.zeros((1, 4 * CF), F32)


def k_back_three(
    step, act, w_out, short, grad, total, short_total, sums, gb, slow_two, total3,
    d_three, d_short, grad_two, sums_out, three, *, steps, count
):
    def expand(f):
        three[...] = mul(act[f], w_out[...])

    mean_a, scale_a = stats(total, 0, CS, count)
    mean_b, scale_b = stats(short_total, 0, CS, count)
    one, two_a = back_parts(sums, 0, CS, count)
    _, two_b = back_parts(sums, 0, CS, count, rows=(0, 2))
    factor_a = gb[0:1, 768:1792] * scale_a
    factor_b = gb[0:1, 1792:] * scale_b

    def body(f, rows, real, lanes):
        given = grad[f, rows, lanes] - one[:, lanes]
        hat_a = (three[rows, lanes] - mean_a[:, lanes]) * scale_a[:, lanes]
        hat_b = (short[f, rows, lanes] - mean_b[:, lanes]) * scale_b[:, lanes]
        value_a = factor_a[:, lanes] * (given - hat_a * two_a[:, lanes])
        value_b = factor_b[:, lanes] * (given - hat_b * two_b[:, lanes])
        if real < CHUNK:
            row = lax.broadcasted_iota(jnp.int32, value_a.shape, 0)
            value_a = jnp.where(row < real, value_a, 0.0)
            value_b = jnp.where(row < real, value_b, 0.0)
        d_three[f, rows, lanes] = value_a.astype(BF)
        d_short[f, rows, lanes] = value_b.astype(BF)

    chunked(body, act.shape[0], CS, expand)
    mean, scale = stats(total3, 0, CM, count)
    hat = (rows_of(slow_two) - mean) * scale
    slope = gelu_slope(hat * gb[0:1, 2 * CL : 3 * CL] + gb[1:2, 2 * CL : 3 * CL])
    value = slope * mul_t(rows_of(d_three), w_out[...])
    put(grad_two, value)
    add_rows(sums_out, step, steps, 0, value, value * hat)


def k_back_fast_three(
    step, given, sums, total3, fgrad, fthree, ftwo, fgb, fproj, total2,
    d_fthree, fgrad_two, sums_out, *, steps, count
):
    @pl.when(step % steps == 0)
    def _():
        sums_out[0, :, :CM] = given[0]

    mean, scale = stats(total3, CM, 4 * CF, 4.0 * count, CF)
    one, two = back_parts(sums, CS, 4 * CF, 4.0 * count, CF)
    factor = fgb[0:1, 256:] * scale

    def fast_body(f, rows, real, lanes):
        hat = (fthree[f, rows, lanes] - mean[:, lanes]) * scale[:, lanes]
        value = fgrad[f, rows, lanes] - one[:, lanes] - hat * two[:, lanes]
        value = factor[:, lanes] * value
        if real < CHUNK:
            row = lax.broadcasted_iota(jnp.int32, value.shape, 0)
            value = jnp.where(row < real, value, 0.0)
        d_fthree[f, rows, lanes] = value.astype(BF)

    chunked(fast_body, fthree.shape[0], 4 * CF)
    mean, scale = stats(total2, CS, 128, 4.0 * count, CFM)
    hat = (rows_of(ftwo) - mean) * scale
    slope = gelu_slope(hat * fgb[0:1, 128:256] + fgb[1:2, 128:256])
    value = slope * mul_t(rows_of(d_fthree), fproj[...])
    put(fgrad_two, value)
    add_rows(sums_out, step, steps, CM, value, value * hat)


def k_back_two(
    step, slow_two, total3, grad_two, sums, gb, w_space, slow_one, total2,
    ftwo, fgrad_two, fgb, fspace, fone, total1, masks,
    taps_out, grad_one, ftaps_out, fgrad_one, sums_out, *, steps, count
):
    mean, scale = stats(total3, 0, CM, count)
    one, two = back_parts(sums, 0, CM, count)
    hat = (rows_of(slow_two) - mean) * scale
    value = norm_back(rows_of(grad_two), hat, gb[0:1, 2 * CL : 3 * CL] * scale, one, two)
    cat = row_cat(spread(value, masks[0]), masks)
    put(taps_out, cat)
    value = column_sum(mul_t(cat, w_space[...]), masks)
    mean, scale = stats(total2, CS + 128, CM, count)
    hat = (rows_of(slow_one) - mean) * scale
    value = gelu_slope(hat * gb[0:1, CL : 2 * CL] + gb[1:2, CL : 2 * CL]) * value
    put(grad_one, value)
    add_rows(sums_out, step, steps, 0, value, value * hat)

    mean, scale = stats(total2, CS, 128, 4.0 * count, CFM)
    one, two = back_parts(sums, CM, 128, 4.0 * count, CFM)
    hat = (rows_of(ftwo) - mean) * scale
    value = norm_back(rows_of(fgrad_two), hat, fgb[0:1, 128:256] * scale, one, two)
    cat = row_cat(spread(value, masks[0]), masks)
    put(ftaps_out, cat)
    value = column_sum(mul_t(cat, fspace[...]), masks)
    mean, scale = stats(total1, CL, 128, 4.0 * count, CFM)
    hat = (rows_of(fone) - mean) * scale
    value = gelu_slope(hat * fgb[0:1, :128] + fgb[1:2, :128]) * value
    put(fgrad_one, value)
    add_rows(sums_out, step, steps, CM, value, value * hat)


def k_back_one(
    step, links, slow_one, total2, grad_one, fone, total1, fgrad_one, sums, gb, fgb, masks,
    d_one, d_fone, tail, head, *, count
):
    frames = slow_one.shape[0]
    mean, scale = stats(total2, CS + 128, CM, count)
    one, two = back_parts(sums, 0, CM, count)
    hat = (rows_of(slow_one) - mean) * scale
    value = norm_back(rows_of(grad_one), hat, gb[0:1, CL : 2 * CL] * scale, one, two)
    value = spread(value, masks[0])
    put(d_one, value)
    mean, scale = stats(total1, CL, 128, 4.0 * count, CFM)
    one, two = back_parts(sums, CM, 128, 4.0 * count, CFM)
    hat = (rows_of(fone) - mean) * scale
    fvalue = norm_back(rows_of(fgrad_one), hat, fgb[0:1, :128] * scale, one, two)
    fvalue = spread(fvalue, masks[0])
    put(d_fone, fvalue)
    last = (frames - 1) * ROWS
    tail[0, :, :CM] = value[last:].astype(BF)
    tail[0, :, CM:] = fvalue[last:].astype(BF)
    link = links[step * frames]
    head[0, :, :CM] = (link * value[:ROWS]).astype(BF)
    head[0, :, CM:] = (link * fvalue[:ROWS]).astype(BF)


def k_trio(
    step, links, nexts, d_one, rim_before, rim_after, d_short, w_time, w_proj, lat, total1, gb,
    trio, grad, sums, *, count
):
    frames = d_one.shape[0]
    base = step * frames
    for f in range(frames):
        prev = rim_before[0, :, :CM] if f == 0 else d_one[f - 1]
        follow = rim_after[0, :, :CM] if f == frames - 1 else d_one[f + 1]
        trio[f, :, :CM] = (nexts[base + f] * follow.astype(F32)).astype(BF)
        trio[f, :, CM : 2 * CM] = d_one[f]
        trio[f, :, 2 * CM :] = (links[base + f] * prev.astype(F32)).astype(BF)
    value = mul_t(rows_of(trio), w_time[CS:]) + mul_t(rows_of(d_short), w_proj[CS:])
    mean, scale = stats(total1, 0, CL, count)
    hat = (rows_of(lat) - mean) * scale
    value = gelu_slope(hat * gb[0:1, :CL] + gb[1:2, :CL]) * value
    put(grad, value)
    add_rows(sums, step, 1, 0, value, value * hat)


def k_slow_grad(step, trio, d_short, w_time, w_proj, out):
    value = mul_t(rows_of(trio), w_time[:CS]) + mul_t(rows_of(d_short), w_proj[:CS])
    out[...] = value.reshape(-1, ROWS, CS)[:, :PIX].astype(BF)


def k_back_lat(step, links, lat, total1, grad, sums, gb, masks, d_lat, head, *, count):
    frames = lat.shape[0]
    mean, scale = stats(total1, 0, CL, count)
    one, two = back_parts(sums, 0, CL, count)
    hat = (rows_of(lat) - mean) * scale
    value = norm_back(rows_of(grad), hat, gb[0:1, :CL] * scale, one, two)
    value = spread(value, masks[0])
    put(d_lat, value)
    head[0] = (links[step * frames] * value[:ROWS]).astype(BF)


def k_fast_grad(
    step, links, nexts, fgrad, d_lat, lat_rim, d_fone, rim_before, rim_after, w_back, out, cat
):
    frames = d_lat.shape[0]
    base = step * frames
    for f in range(frames):
        last = f == frames - 1
        follow = lat_rim[0] if last else d_lat[f + 1]
        prev_f = rim_before[0, :, CM:] if f == 0 else d_fone[f - 1]
        next_f = rim_after[0, :, CM:] if last else d_fone[f + 1]
        lane = lax.broadcasted_iota(jnp.int32, prev_f.shape, 1)
        rim = jnp.where(lane >= 96, links[base + f] * prev_f.astype(F32), 0.0)
        rim += jnp.where(lane < 32, nexts[base + f] * next_f.astype(F32), 0.0)
        cat[f, :, :CL] = d_lat[f]
        cat[f, :, CL : CL + 128] = d_fone[f]
        cat[f, :, CL + 128 : 2 * CL + 128] = (nexts[base + f] * follow.astype(F32)).astype(BF)
        cat[f, :, 2 * CL + 128 :] = rim.astype(BF)
    value = rows_of(fgrad) + mul_t(rows_of(cat), w_back[...])
    value = value.reshape(-1, ROWS, 4 * CF)
    for q in range(4):
        out[:, q] = value[:, :PIX, q * CF : (q + 1) * CF].astype(BF)


def k_outer_joined(step, slow, lat, right, out, *, parts, taps):
    value = mul_rows(slow if step < parts else lat, right).astype(BF)
    if taps == 1:
        out[...] = value
    else:
        for tap in range(taps):
            out[tap] = value[:, tap * CM : (tap + 1) * CM]


def outer_joined(slow, lat, right, taps, name):
    wide = 256
    parts = slow.shape[-1] // wide
    block = slow.shape[:2] + (wide,)
    rows, lanes = slow.shape[-1] + lat.shape[-1], right.shape[-1]
    if taps == 1:
        out = ((rows, lanes), BF, (wide, lanes), lambda g: (g, 0), True)
    else:
        out = ((taps, rows, CM), BF, (taps, wide, CM), lambda g: (0, g, 0), True)
    return call(
        functools.partial(k_outer_joined, parts=parts, taps=taps),
        rows // wide,
        [
            (slow, block, lambda g: (0, 0, min(g, parts - 1))),
            whole(lat),
            whole(right),
        ],
        [out],
        flops=2 * slow.shape[0] * slow.shape[1] * rows * lanes,
        name=name,
        unroll=True,
    )[0]


def k_outer_out(step, left, right, fleft, fright, out, fout):
    out[...] = mul_rows(left, right).astype(BF)
    value = mul_rows(fleft, fright)
    fout[...] = sum(
        value[q * CFM : (q + 1) * CFM, q * CF : (q + 1) * CF] for q in range(4)
    ).astype(BF)


def lanes_at(value, at):
    return (pltpu.roll(value, (128 - at) % 128, 1) if at else value)[:, :CFM]


def k_outer_space(step, left, right, fleft, fright, out, fout):
    value = mul_rows(left, right).astype(BF)
    for a in range(3):
        out[a, 0] = value[:, a * CM : (a + 1) * CM]
    value = mul_rows(fleft, fright)
    for a in range(3):
        block = value[:, a * 128 : (a + 1) * 128]
        folded = sum(
            lanes_at(block[q * CFM : (q + 1) * CFM], q * CFM) for q in range(4)
        )
        fout[a, 0] = folded.astype(BF)


def k_outer_first(
    step, links, nexts, fast, edge_down, edge_up, d_lat, d_fone, *rest, micro
):
    z = rest[-1]
    z[...] = jnp.zeros_like(z)
    frames = z.shape[0] // micro
    for m in range(micro):
        part = pl.ds(m * frames, frames)
        fill_z(
            z.at[part], m * frames, links, nexts, fast.at[part],
            edge_down.at[pl.ds(m, 1)], edge_up.at[pl.ds(m, 1)],
        )
    blocks = [4, 5, 0, 1, 2]
    taps = [0.0, 0.0, 0.0]
    fast = mul_rows(z, d_fone)
    lat = mul_rows(z, d_lat)
    lat = jnp.concatenate([lat[block * CF : (block + 1) * CF] for block in blocks], 0)
    for q in range(4):
        for k in range(3):
            block = [5, 0, 1, 2, 3, 6][q + k]
            taps[k] += lanes_at(fast[block * CF : (block + 1) * CF], q * CFM)
    if len(rest) == 3:
        out, fout, _ = rest
        out[...] = lat.astype(BF)
        for k in range(3):
            fout[k] = taps[k].astype(BF)
        return
    fspace, fproj, out, _ = rest
    devices = out.shape[0]
    taps = jnp.concatenate(taps, 0)
    at = 0
    for value in (lat[:, :128], lat[:, 128:], taps, fspace[...].astype(F32), fproj[...].astype(F32)):
        rows, lanes = value.shape[0] // devices, value.shape[1]
        for d in range(devices):
            out[d, at : at + rows, :lanes] = value[d * rows : (d + 1) * rows].astype(BF)
        at += rows


def k_params(step, sums_a, sums_b, sums_c, sums_d, out, fast):
    a, b, c, d = (ref[0] + ref[1] for ref in (sums_a, sums_b, sums_c, sums_d))
    for row, place in enumerate((1, 0)):
        out[row : row + 1, :CL] = d[place : place + 1]
        out[row : row + 1, CL : 2 * CL] = c[place : place + 1, :CM]
        out[row : row + 1, 2 * CL : 3 * CL] = b[place : place + 1, :CM]
        out[row : row + 1, 768:1792] = a[place : place + 1, :CS]
        third = 2 if row == 0 else 0
        out[row : row + 1, 1792:] = a[third : third + 1, :CS]
        fast[row : row + 1] = fold_lanes(c[place : place + 1, CM:], CFM)
        fast[row + 2 : row + 3] = fold_lanes(b[place : place + 1, CM:], CFM)
        fast[row + 4 : row + 5] = fold_lanes(a[place : place + 1, CS:], CF)[:, :128]


def mask_table():
    row = np.arange(ROWS)
    col = row % WW
    real = row < PIX
    table = [real, real & (col != 0), real & (col != WW - 1), real & (row >= WW), row < PIX - WW]
    return np.broadcast_to(np.stack(table)[:, :, None], (5, ROWS, CM)).astype(np.float32)


def as_rows(shard):
    return jnp.pad(shard, (0, -shard.shape[0] % CM)).reshape(-1, CM)


def flat_of(gathered, at, shard, lanes):
    rows = -(-shard.shape[0] // CM)
    part = gathered[:, at : at + rows]
    if shard.shape[0] % CM:
        part = part.reshape(part.shape[0], -1)[:, : shard.shape[0]]
    return part.reshape(-1, lanes)


def local(
    slow_in,
    fast_in,
    clip_starts,
    w_lateral,
    w_slow_time,
    w_slow_space,
    w_slow_out,
    w_projection,
    w_fast_time,
    w_fast_space,
    w_fast_out,
    slow_gain,
    slow_bias,
    fast_gain,
    fast_bias,
    slow_cotangent,
    fast_cotangent,
):
    devices = lax.axis_size(AXES)
    micro, frames = slow_in.shape[:2]
    groups = micro * frames
    masks = jnp.asarray(mask_table())
    count = float(frames * PIX * devices)
    me = lax.axis_index(AXES)
    share = slow_gain.shape[0]
    mine, spots, share_start = has_bits(me), slice_spots(me), me * share

    wide = w_projection.reshape(-1, CS)
    shards = [
        w_slow_time, w_lateral, w_fast_time, w_fast_space, w_fast_out, slow_gain, slow_bias
    ]
    widths = (CM, CM, CFM, CFM, CF, share, share)
    whole_rows = all(shard.shape[0] % width == 0 for shard, width in zip(shards, widths))
    if whole_rows:
        packed = [shard.reshape(-1, width) for shard, width in zip(shards, widths)]
        packed = [jnp.pad(part, ((0, 0), (0, CM - part.shape[1]))) for part in packed]
    else:
        packed = [as_rows(shard) for shard in shards]
    near_rows = [part.shape[0] for part in packed]
    places = np.cumsum([0] + near_rows)
    packed = jnp.concatenate(packed, 0)
    near = Gather(mine, jnp.pad(packed, ((0, -packed.shape[0] % 8), (0, 0))))

    fast = tie([], fast_in.reshape(groups, 4, PIX, CF))
    fast, fast_in, wide, slow_in, slow_cotangent, fast_cotangent = tie(
        [near], fast, fast_in, wide, slow_in, slow_cotangent, fast_cotangent
    )
    wide = Gather(mine, wide)
    link = (1 - clip_starts).astype(F32)
    links = link.reshape(groups)
    nexts = jnp.concatenate([link[:, 1:], jnp.ones((micro, 1), F32)], 1).reshape(groups)
    edge_down = from_before(fast_in[:, -2:])
    edge_up = from_after(fast_in[:, :1] * link[:, :1, None, None].astype(BF))
    slow = pad_rows(slow_in).reshape(groups, ROWS, CS)
    cot = pad_rows(slow_cotangent).reshape(groups, ROWS, CS)
    fcot = to_quads(fast_cotangent)
    slow, fcot, edge_down, edge_up = tie([near, wide], slow, fcot, edge_down, edge_up)
    cot = tie([near], cot)

    fast_both = jnp.stack([fast_gain, fast_bias]).astype(F32)
    fgb = jnp.concatenate(
        [
            jnp.tile(part, (1, 4))
            for part in (fast_both[:, :CFM], fast_both[:, CFM : 2 * CFM], fast_both[:, 2 * CFM :])
        ],
        1,
    )

    if whole_rows:
        slow_time, w_first, w_back, fproj, fspace, gb = call(
            functools.partial(k_prep, shares=near_rows),
            1,
            [whole(near.result())],
            [
                out_whole((CS + CL, 3 * CM), BF), out_whole((7 * CF, CL + 128), BF),
                out_whole((4 * CF, 768), BF), out_whole((128, 4 * CF), BF),
                out_whole((384, 384), BF), out_whole((2, 2816), F32),
            ],
            scratch=[
                pltpu.VMEM((3 * (CS + CL), CM), F32), pltpu.VMEM((5 * CF, CL), F32),
                pltpu.VMEM((3 * CF + 9 * CFM + CFM, 128), F32),
            ],
            name="first_weights",
            limit=16,
        )
    else:
        weights = near.result()
        cuts = [
            flat_of(weights, int(at), shard, lanes)
            for at, shard, lanes in zip(places, shards, (CM, CL, CFM, CFM, CF, share, share))
        ]
        slow_time = cuts[0].reshape(3, CS + CL, CM)
        slow_time = jnp.concatenate([slow_time[tap] for tap in range(3)], -1)
        lateral, fast_time, fast_space, fast_proj = cuts[1:5]
        gb = jnp.stack([cuts[5].reshape(-1), cuts[6].reshape(-1)]).astype(F32)
        fast_time = fast_time.reshape(3, CF, CFM)
        order = [5, 0, 1, 2, 3, 6]
        band = np.zeros((3, 7, 4), np.float32)
        for q in range(4):
            for k in range(3):
                band[k, order[q + k], q] = 1
        band = jnp.asarray(band, BF)
        fast_band = jnp.sum(
            band[:, :, None, :, None] * fast_time[:, None, :, None, :], 0, dtype=F32
        ).astype(BF).reshape(7 * CF, 4 * CFM)
        none = jnp.zeros((CF, CL), BF)
        lat_band = jnp.concatenate([lateral[2 * CF :], none, lateral[: 2 * CF], none], 0)
        w_first = jnp.concatenate([lat_band, fast_band], -1)
        eye4 = jnp.eye(4, dtype=BF)
        fproj = (fast_proj[None, :, None, :] * eye4[:, None, :, None]).reshape(4 * CFM, 4 * CF)
        lat_prev = jnp.concatenate([jnp.zeros((2 * CF, CL), BF), lateral[: 2 * CF]], 0)
        blank = jnp.zeros((CF, 3 * CFM), BF)
        rim_rows = jnp.concatenate(
            [
                jnp.concatenate([blank, fast_time[2]], -1),
                jnp.zeros((2 * CF, 4 * CFM), BF),
                jnp.concatenate([fast_time[0], blank], -1),
            ],
            0,
        )
        fspace = fast_space.reshape(3, 3, CFM, CFM).transpose(1, 2, 0, 3)
        fspace = fspace[:, None, :, :, None, :] * eye4[None, :, None, None, :, None]
        fspace = fspace.reshape(3 * 4 * CFM, 3 * 4 * CFM)
        w_back = jnp.concatenate([w_first[: 4 * CF], lat_prev, rim_rows], -1)

    far = jnp.concatenate([as_rows(w_slow_space), as_rows(w_slow_out)], 0)
    links, nexts, w_first, spots, mine, share_start, far, *mids = tie(
        [], links, nexts, w_first, spots, mine, share_start, far,
        gb, fgb, fspace, fproj, w_back,
    )
    gb, fgb, fspace, fproj, w_back = mids
    fars = []
    space_rows = -(-w_slow_space.shape[0] // CM)

    rows = groups * ROWS
    bind = functools.partial

    def og(lanes, dtype, per):
        return out_group((groups, ROWS, lanes), dtype, per)

    def os(per, n, lanes):
        return out_stream((micro, n, lanes), F32, frames // per)

    def edge(lanes):
        return out_stream((micro, ROWS, lanes), BF, 1)

    def hooked(*stages):
        return lambda value, stage: tie(stages[stage], value) if stage < len(stages) else value

    def first_hook(value, stage):
        if stage == 1:
            value = tie([wide], value)
            fars.append(Gather(mine, far))
        return value

    lat_pre, fone, sums = call(
        k_first,
        micro,
        [
            scalar(links), scalar(nexts), group(fast, frames), stream(edge_down, 1),
            stream(edge_up, 1), whole(w_first),
        ],
        [og(CL, F32, frames), og(128, F32, frames), os(frames, 2, CL + 128)],
        scratch=[pltpu.VMEM((frames, ROWS, 7 * CF), BF)],
        flops=2 * rows * 896 * 384,
        name="lateral_and_fast_time",
    )
    total1 = all_sum(sums, first_hook)

    lat_act, taps, tail, head = call(
        bind(k_taps, count=count),
        micro,
        [
            scalar(links), group(lat_pre, frames), stream(total1, 1), whole(gb),
            group(slow, frames), whole(slow_time), whole(masks),
        ],
        [og(CL, BF, frames), og(3 * CM, F32, frames), edge(CM), edge(CM)],
        flops=2 * rows * 1280 * 768,
        name="slow_time_taps",
    )
    rim_before, rim_after = from_before(tail), from_after(head)
    far = fars[0]
    lat_act = tie([wide, far], lat_act)
    projection = wide.result().reshape(CS + CL, CS)
    per = frames
    state, fact_cat, sums = call(
        bind(k_short, steps=1, count=count),
        micro,
        [
            group(slow, per), group(lat_act, per), whole(projection), group(fone, per),
            stream(total1, 1), whole(fgb), whole(fspace), whole(masks),
        ],
        [
            ("short", per), og(384, BF, per), ("ftwo", per), os(per, 2, CS + 128),
        ],
        state={},
        flops=2 * rows * 1280 * 1024,
        name="shortcut_and_fast_space",
    )
    state, sums = call(
        k_one,
        micro,
        [
            scalar(links), scalar(nexts), group(taps, frames),
            stream(rim_before, 1), stream(rim_after, 1), stream(sums, 1),
        ],
        [("one", frames), os(frames, 2, CS + 128 + CM)],
        state=state,
        name="slow_one",
    )
    total2 = all_sum(sums, hooked([far], [far]))
    weights = far.result()
    space = flat_of(weights, 0, w_slow_space, CM)
    rows_out = flat_of(weights, space_rows, w_slow_out, CM)

    state, cat_one, fact_two, sums, slow_space = call(
        bind(k_two, steps=1, count=count),
        micro,
        [
            ("one", per), ("ftwo", per), stream(total2, 1), whole(gb), whole(fgb),
            whole(space), whole(fproj), whole(masks),
        ],
        [
            og(3 * CM, BF, per), ("two", per), og(128, BF, per), ("fthree", per),
            os(per, 2, CM + 4 * CF), out_whole((3 * CM, 3 * CM), BF),
        ],
        state=state,
        flops=2 * rows * 768 * 768,
        name="slow_space",
    )
    total3 = all_sum(sums)

    state, act_two, sums, slow_proj = call(
        bind(k_three, steps=1, count=count),
        micro,
        [
            ("two", per), stream(total3, 1), whole(gb), whole(rows_out),
            whole(masks),
        ],
        [og(CM, BF, per), os(per, 2, CS), out_whole((CM, CS), BF)],
        state=state,
        scratch=[pltpu.VMEM((2, 4 * CM, 128), F32)],
        flops=2 * rows * 256 * 1024,
        name="slow_three",
    )
    per = 2 if frames % 2 == 0 else 1
    steps = frames // per
    quarters = ((groups, 4, PIX, CF), BF)
    state, fast_out, fsums = call(
        bind(k_fast_out, steps=steps, count=count),
        groups // per,
        [
            ("fthree", per), group(fast, per), group(fcot, per), stream(total3, steps),
            whole(fgb),
        ],
        [out_group(*quarters, per, False), ("fgrad", per), os(per, 2, 4 * CF)],
        state=state,
        scratch=[pltpu.VMEM((2, 8, 4 * CF), F32)],
        flops=rows * 512 * 200,
        name="fast_out",
    )
    total4 = all_sum(sums)

    state, slow_out, sums = call(
        bind(k_out, steps=steps, count=count),
        groups // per,
        [
            group(act_two, per), whole(slow_proj), ("short", per), group(cot, per),
            stream(total4, steps), stream(total2, steps), whole(gb), stream(fsums, steps),
        ],
        [
            out_group((groups, PIX, CS), BF, per, False), ("grad", per), os(per, 3, CS + 4 * CF),
        ],
        state=state,
        scratch=[pltpu.VMEM((ROWS, CS), F32), pltpu.VMEM((3, 8, CS), F32)],
        flops=2 * rows * 256 * 1024,
        name="slow_out",
    )
    sums_a = all_sum(sums)

    def pixels_first(value, whole_shape):
        return jnp.swapaxes(value.reshape(whole_shape), 1, 2)

    state, d_three, d_short, sums = call(
        bind(k_back_three, steps=steps, count=count),
        groups // per,
        [
            group(act_two, per), whole(slow_proj), ("short", per), ("grad", per),
            stream(total4, steps), stream(total2, steps), stream(sums_a, steps), whole(gb),
            ("two", per), stream(total3, steps),
        ],
        [og(CS, BF, per), og(CS, BF, per), ("grad_two", per), os(per, 2, CM)],
        state=state,
        scratch=[pltpu.VMEM((ROWS, CS), F32)],
        flops=4 * rows * 256 * 1024,
        name="back_three",
    )
    state, d_fthree, sums = call(
        bind(k_back_fast_three, steps=steps, count=count),
        groups // per,
        [
            stream(sums, steps), stream(sums_a, steps), stream(total3, steps),
            ("fgrad", per), ("fthree", per), ("ftwo", per), whole(fgb), whole(fproj),
            stream(total2, steps),
        ],
        [og(4 * CF, BF, per), ("fgrad_two", per), os(per, 2, CM + 128)],
        state=state,
        flops=2 * rows * 128 * 512,
        name="back_fast_three",
    )

    def shares(value):
        return value.reshape(devices, -1, value.shape[-1])

    flows = {}

    def weights_of_three(value, stage):
        if stage == 0:
            proj_grad = outer_joined(slow, lat_act, d_short, 1, "projection_grad")
            out_grad, flows["fast_out"] = call(
                k_outer_out,
                1,
                [whole(act_two), whole(d_three), whole(fact_two), whole(d_fthree)],
                [out_whole((CM, CS), BF), out_whole((CFM, CF), BF)],
                flops=2 * rows * 256 * 1024,
                name="slow_out_grad",
            )
            value, proj_grad, out_grad = tie([], value, proj_grad, out_grad)
            both = jnp.concatenate([shares(proj_grad), shares(out_grad)], 1)
            flows["a"] = Shares(spots, both)
            flows["proj_rows"] = proj_grad.shape[0] // devices
        elif stage == 1:
            value = tie([flows["a"]], value)
        return value

    sums_b = all_sum(sums, weights_of_three)

    per = frames
    state, two_taps, ftwo_taps, sums = call(
        bind(k_back_two, steps=1, count=count),
        micro,
        [
            ("two", per), stream(total3, 1), ("grad_two", per),
            stream(sums_b, 1), whole(gb), whole(slow_space), ("one", per),
            stream(total2, 1), ("ftwo", per), ("fgrad_two", per), whole(fgb),
            whole(fspace), group(fone, per), stream(total1, 1), whole(masks),
        ],
        [
            og(3 * CM, BF, per), ("grad_one", per), og(384, BF, per), ("fgrad_one", per),
            os(per, 2, CM + 128),
        ],
        state=state,
        flops=2 * rows * 768 * 768,
        name="back_two",
    )
    block = (groups, ROWS, CM)
    slim = (groups, ROWS, 128)

    def weights_of_two(value, stage):
        if stage == 0:
            flows["space"], flows["fspace"] = call(
                k_outer_space,
                3,
                [
                    (cat_one, block, lambda g: (0, 0, g)), whole(two_taps),
                    (fact_cat, slim, lambda g: (0, 0, g)), whole(ftwo_taps),
                ],
                [
                    ((3, 3, CM, CM), BF, (3, 1, CM, CM), lambda g: (0, g, 0, 0), True),
                    ((3, 3, CFM, CFM), BF, (3, 1, CFM, CFM), lambda g: (0, g, 0, 0), True),
                ],
                flops=2 * rows * 768 * 768,
                name="slow_space_grad",
                unroll=True,
            )
            value, flows["space"] = tie([], value, flows["space"])
        elif stage == 1:
            value = tie([flows["a"]], value)
        return value

    sums_c = all_sum(sums, weights_of_two)

    state, d_one, d_fone, tail, head = call(
        bind(k_back_one, count=count),
        micro,
        [
            scalar(links), ("one", frames), stream(total2, 1), ("grad_one", frames),
            group(fone, frames), stream(total1, 1), ("fgrad_one", frames), stream(sums_c, 1),
            whole(gb), whole(fgb), whole(masks),
        ],
        [og(CM, BF, frames), og(128, BF, frames), edge(CM + 128), edge(CM + 128)],
        state=state,
        name="back_one",
    )
    rim_before, rim_after = from_before(tail), from_after(head)
    slow_out = pixels_first(slow_out, slow_in.shape)
    rim_before, rim_after, slow_out = tie([], rim_before, rim_after, slow_out)
    state, trio, sums = call(
        bind(k_trio, count=count),
        micro,
        [
            scalar(links), scalar(nexts), group(d_one, frames),
            stream(rim_before, 1), stream(rim_after, 1), group(d_short, frames),
            whole(slow_time), whole(projection),
            group(lat_pre, frames), stream(total1, 1), whole(gb),
        ],
        [og(3 * CM, BF, frames), ("lat_grad", frames), os(frames, 2, CL)],
        state=state,
        flops=2 * rows * 1792 * 256,
        name="back_lateral",
    )

    def weights_of_one(value, stage):
        if stage == 0:
            time_grad = outer_joined(slow, lat_act, trio, 3, "slow_time_grad")
            value, time_grad, flows["trio"] = tie([], value, time_grad, trio)
            both = jnp.concatenate([shares(time_grad), shares(flows["space"])], 1)
            flows["b"] = Shares(spots, both)
            flows["time_rows"] = time_grad.shape[0] * time_grad.shape[1] // devices
        elif stage == 1:
            value, later = tie([flows["b"]], value, flows["trio"])
            flows["slow_in_grad"] = call(
                k_slow_grad,
                micro,
                [group(later, per), group(d_short, per), whole(slow_time), whole(projection)],
                [out_group((groups, PIX, CS), BF, per, False)],
                flops=2 * rows * 1792 * 1024,
                name="slow_in_grad",
            )[0]
        return value

    sums_d = all_sum(sums, weights_of_one)
    slow_in_grad = pixels_first(flows["slow_in_grad"], slow_in.shape)

    state, d_lat, head = call(
        bind(k_back_lat, count=count),
        micro,
        [
            scalar(links), group(lat_pre, frames), stream(total1, 1), ("lat_grad", frames),
            stream(sums_d, 1), whole(gb), whole(masks),
        ],
        [og(CL, BF, frames), edge(CL)],
        state=state,
        name="back_lat",
    )
    d_lat, head = tie([flows["b"]], d_lat, head)
    lat_rim = from_after(head)
    packed = devices <= CFM
    tops = [
        scalar(links), scalar(nexts), whole(fast), whole(edge_down), whole(edge_up),
        whole(d_lat), whole(d_fone),
    ]
    if packed:
        ends = [flows["fspace"].reshape(-1, CFM), flows["fast_out"]]
        sizes = [5 * CF, 5 * CF, 3 * CF, 9 * CFM, CFM]
        sizes = [size // devices for size in sizes]
        tops += [whole(part) for part in ends]
        outs = [out_whole((devices, -(-sum(sizes) // 8) * 8, 128), BF)]
    else:
        outs = [out_whole((5 * CF, CL), BF), out_whole((3, CF, CFM), BF)]
    first_grad = call(
        bind(k_outer_first, micro=micro),
        1,
        tops,
        outs,
        scratch=[pltpu.VMEM((groups, ROWS, 7 * CF), BF)],
        flops=2 * rows * 896 * 384,
        name="lateral_grad",
    )
    if packed:
        flat = first_grad[0]
    else:
        flat = [
            part.reshape(devices, -1)
            for part in (*first_grad, flows["fspace"], flows["fast_out"])
        ]
        sizes = [part.shape[1] for part in flat]
        flat = jnp.concatenate(flat, 1)
        flat = jnp.pad(flat, ((0, 0), (0, -flat.shape[1] % 1024)))
        flat = flat.reshape(devices, -1, 128)
    last = Shares(spots, flat)
    fast_out = pixels_first(fast_out, fast_in.shape)
    lat_rim, fast_out = tie([flows["a"], last], lat_rim, fast_out)
    state, fast_in_grad = call(
        k_fast_grad,
        micro,
        [
            scalar(links), scalar(nexts), ("fgrad", frames), group(d_lat, frames),
            stream(lat_rim, 1), group(d_fone, frames), stream(rim_before, 1),
            stream(rim_after, 1), whole(w_back),
        ],
        [out_group(*quarters, frames, False)],
        state=state,
        scratch=[pltpu.VMEM((frames, ROWS, 768), BF)],
        flops=2 * rows * 768 * 512,
        name="fast_in_grad",
    )
    fast_in_grad, slow_in_grad = tie([flows["b"], last], fast_in_grad, slow_in_grad)
    fast_in_grad = pixels_first(fast_in_grad, fast_in.shape)
    both_out = flows["a"].result().reshape(-1, CS)
    cut = flows["proj_rows"]
    proj_out, out_out = both_out[:cut].reshape(-1), both_out[cut:].reshape(-1)
    both_out = flows["b"].result().reshape(-1, CM)
    cut = flows["time_rows"]
    time_out, space_out = both_out[:cut].reshape(-1), both_out[cut:].reshape(-1)
    flat = last.result()
    smalls = []
    at = 0
    if packed:
        flat = flat.reshape(-1, 128)
        parts = []
        for size, lanes in zip(sizes, (128, 128, CFM, CFM, CF)):
            parts.append(flat[at : at + size, :lanes])
            at += size
        parts = [jnp.concatenate(parts[:2], 1)] + parts[2:]
        smalls = [part.reshape(-1) for part in parts]
    else:
        for size in sizes:
            smalls.append(flat[at : at + size])
            at += size

    norms, fnorms = call(
        k_params,
        1,
        [whole(sums_a), whole(sums_b), whole(sums_c), whole(sums_d)],
        [out_whole((2, 2816), F32), out_whole((8, 128), F32)],
        name="norm_grads",
    )
    norms = pick(norms, share_start, share, 1)
    fast_gain_grad, fast_bias_grad = (
        jnp.concatenate([fnorms[row, :CFM], fnorms[row + 2, :CFM], fnorms[row + 4]])
        for row in range(2)
    )
    return (
        jnp.swapaxes(slow_out, 1, 2),
        jnp.swapaxes(fast_out, 1, 2),
        jnp.swapaxes(slow_in_grad, 1, 2),
        jnp.swapaxes(fast_in_grad, 1, 2),
        smalls[0],
        time_out,
        space_out,
        out_out,
        proj_out,
        smalls[1],
        smalls[2],
        smalls[3],
        norms[0],
        norms[1],
        fast_gain_grad,
        fast_bias_grad,
    )


def solution(mesh):
    frames = P(None, AXES, None, None)
    flat = P(AXES)
    return jax.shard_map(
        local,
        mesh=mesh,
        in_specs=(frames, frames, P(None, AXES))
        + (flat,) * 10
        + (P(), P(), frames, frames),
        out_specs=(frames,) * 4 + (flat,) * 10 + (P(), P()),
        check_vma=False,
    )
```

```python
import functools
import math

import jax
import jax.numpy as jnp
import numpy as np
from jax import lax
from jax.experimental import pallas as pl
from jax.experimental.pallas import tpu as pltpu
from jax.sharding import PartitionSpec as P

CS = 1024
CL = 256
CM = 256
CF = 128
CFM = 32
HH = 14
WW = 14
PIX = HH * WW
ROWS = 208
EPS = 1e-05
AXES = ("path", "dp")
BF = jnp.bfloat16
F32 = jnp.float32


def swap(value, bit):
    count = lax.axis_size(AXES)
    return lax.ppermute(value, AXES, [(i, i ^ bit) for i in range(count)])


def dp_pairs():
    bits = []
    bit = 1
    while bit < lax.axis_size("dp"):
        bits.append(bit)
        bit *= 2
    return [bits[at : at + 2] for at in range(0, len(bits), 2)]


def all_sum(value, hook=lambda value, stage: value):
    value = hook(value + swap(value, lax.axis_size("dp")), 0)
    for stage, pair in enumerate(dp_pairs()):
        if len(pair) == 1:
            value = value + swap(value, pair[0])
        else:
            one, two = pair
            first, second, third = swap(value, one), swap(value, two), swap(value, one + two)
            value = (value + first) + (second + third)
        value = hook(value, stage + 1)
    return value


def has_bits(me):
    bits = [bit for pair in dp_pairs() for bit in pair] + [lax.axis_size("dp")]
    return {bit: (me & bit) != 0 for bit in bits}


def in_order(parts, bits, mine):
    parts = [part[None] for part in parts]
    step = 1
    for bit in bits:
        parts = [jnp.where(mine[bit], parts[k ^ step], parts[k]) for k in range(len(parts))]
        step *= 2
    return jnp.concatenate(parts, 0)


class Gather:
    def __init__(self, mine, value):
        self.mine = mine
        self.shape = value.shape
        self.value = value[None]
        self.stages = dp_pairs()[::-1] + [[lax.axis_size("dp")]]
        self.flight = None
        self.start()

    def start(self):
        if not self.stages:
            self.value = self.value.reshape((-1,) + self.shape)
            return
        self.bits = self.stages.pop(0)
        steps = [
            sum(bit for n, bit in enumerate(self.bits) if k >> n & 1)
            for k in range(1, 2 ** len(self.bits))
        ]
        self.flight = [swap(self.value, step) for step in steps]

    def finish(self):
        stacked = in_order([self.value] + self.flight, self.bits, self.mine)
        if self.stages:
            stacked = jnp.swapaxes(stacked, 0, 1)
        self.value = stacked.reshape((-1,) + self.shape)
        self.flight = None
        self.start()

    def result(self):
        while self.flight is not None:
            self.finish()
        return self.value


def pick(value, start, extent, axis):
    starts = [jnp.int32(0)] * value.ndim
    starts[axis] = start
    sizes = list(value.shape)
    sizes[axis] = extent
    return lax.dynamic_slice(value, starts, sizes, allow_negative_indices=False)


def share_stages():
    return [[lax.axis_size("dp")]] + dp_pairs()


def slice_spots(me):
    spots = []
    for bits in share_stages():
        count = 2 ** len(bits)
        spot = lax.shift_right_logical(me, bits[0].bit_length() - 1) & (count - 1)
        spots.append([spot ^ k for k in range(count)])
    return spots


class Shares:
    def __init__(self, spots, value):
        self.value = value
        self.stages = list(zip(share_stages(), spots))
        self.flight = None
        self.start()

    def start(self):
        if not self.stages:
            return
        bits, spots = self.stages.pop(0)
        count = 2 ** len(bits)
        rest = self.value.shape[-2:]
        axis = 0 if bits[0] == lax.axis_size("dp") else 1
        shaped = self.value.reshape(((2, -1), (-1, count))[axis] + rest)
        parts = [pick(shaped, spot, 1, axis) for spot in spots]
        parts = [part.reshape((-1,) + rest) for part in parts]
        self.keep = parts[0]
        steps = [sum(bit for n, bit in enumerate(bits) if k >> n & 1) for k in range(1, count)]
        self.flight = [swap(part.astype(BF), step) for part, step in zip(parts[1:], steps)]

    def finish(self):
        terms = [self.keep.astype(F32)] + [part.astype(F32) for part in self.flight]
        while len(terms) > 1:
            terms = [sum(terms[at : at + 2]) for at in range(0, len(terms), 2)]
        self.value = terms[0]
        self.flight = None
        self.start()

    def result(self):
        while self.flight is not None:
            self.finish()
        return self.value.reshape(-1)


def tie(flows, *values):
    flows = [flow for flow in flows if flow.flight is not None]
    values, flights = lax.optimization_barrier((values, [flow.flight for flow in flows]))
    for flow, flight in zip(flows, flights):
        flow.flight = flight
        flow.finish()
    return values if len(values) > 1 else values[0]


def from_before(value):
    count = lax.axis_size(AXES)
    return lax.ppermute(value, AXES, [(i, i + 1) for i in range(count - 1)])


def from_after(value):
    count = lax.axis_size(AXES)
    return lax.ppermute(value, AXES, [(i + 1, i) for i in range(count - 1)])


def gelu_tan(value):
    return jnp.tanh(value * (0.7978845608028654 + 0.035677408136300125 * (value * value)))


def gelu(value):
    return value * (0.5 + 0.5 * gelu_tan(value))


def gelu_slope(value):
    tan = gelu_tan(value)
    inner = 0.7978845608028654 + 0.10703222440890037 * (value * value)
    return (0.5 + 0.5 * tan) + (0.5 * value) * (1.0 - tan * tan) * inner


def pad_rows(value):
    return jnp.pad(value, [(0, 0)] * (value.ndim - 2) + [(0, ROWS - PIX), (0, 0)])


def to_quads(value):
    micro, frames, _, lanes = value.shape
    quads = pad_rows(value).reshape(micro * frames // 4, 4, ROWS, lanes)
    return jnp.concatenate([quads[:, place] for place in range(4)], -1)


PARTS = dict(
    short=CS,
    grad=CS,
    grad_two=CM,
    fgrad_two=128,
    grad_one=CM,
    fgrad_one=128,
    lat_grad=CL,
    fthree=4 * CF,
    fgrad=4 * CF,
    one=CM,
    two=CM,
    ftwo=128,
)


def in_vmem(array):
    return pltpu.with_memory_space_constraint(array, pltpu.VMEM)


def call(body, steps, ins, outs, scratch=(), flops=0, name=None, limit=8, unroll=False, state=None, cheap=False):
    names = [given[0] if len(given) == 2 else None for given in outs]
    ins = [group(state[given[0]], given[1]) if len(given) == 2 else given for given in ins]
    if state is not None:
        groups = ins[0][0].shape[0] if not state else next(iter(state.values())).shape[0]
    outs = [
        out_group((groups, ROWS, PARTS[given[0]]), F32, given[1]) if len(given) == 2 else given
        for given in outs
    ]
    arrays = [array for array, _, _ in ins]
    blocks = [(array.shape, block, index) for array, block, index in ins]
    blocks += [(shape, block, index) for shape, _, block, index, _ in outs]

    def view(ref, shape, block, index, step):
        if block in (None, "hbm") or tuple(block) == tuple(shape):
            return ref
        spot = [
            slice(None) if size == full else pl.ds(place * size, size)
            for place, size, full in zip(index(step), block, shape)
        ]
        return ref.at[tuple(spot)]

    def kernel(*refs):
        def run(step, carry):
            views = [view(ref, *given, step) for ref, given in zip(refs, blocks)]
            body(step, *views, *refs[len(blocks) :])
            return carry

        if steps == 1 or unroll:
            for step in range(steps):
                run(step, 0)
        else:
            lax.fori_loop(0, steps, run, 0)

    moved = sum(array.size * array.dtype.itemsize for array in arrays)
    moved += sum(math.prod(shape) * jnp.dtype(dtype).itemsize for shape, dtype, *_ in outs)
    if cheap:
        flops = moved = 1
    vmem = pl.BlockSpec(memory_space=pltpu.VMEM)

    def placed(array, block):
        if block is None:
            return array
        return pltpu.with_memory_space_constraint(
            array, pltpu.HBM if block == "hbm" else pltpu.VMEM
        )

    kinds = {None: pl.BlockSpec(memory_space=pltpu.SMEM), "hbm": pl.BlockSpec(memory_space=pl.ANY)}
    result = pl.pallas_call(
        kernel,
        in_specs=[
            kinds[block] if block in (None, "hbm") else vmem for _, block, _ in ins
        ],
        out_specs=[vmem] * len(outs),
        out_shape=[
            pltpu.VMEM(shape, dtype) if stays else jax.ShapeDtypeStruct(shape, dtype)
            for shape, dtype, _, _, stays in outs
        ],
        scratch_shapes=list(scratch),
        compiler_params=pltpu.CompilerParams(vmem_limit_bytes=limit * 1024 * 1024),
        cost_estimate=pl.CostEstimate(
            flops=int(flops), bytes_accessed=int(moved), transcendentals=0
        ),
        name=name,
    )(*[placed(array, block) for array, block, _ in ins])
    if state is None:
        return result
    fresh = {name: array for name, array in zip(names, result) if name}
    return [{**state, **fresh}] + [array for name, array in zip(names, result) if not name]


def group(array, per):
    tail = (0,) * (array.ndim - 1)
    return (array, (per,) + array.shape[1:], lambda g: (g,) + tail)


def whole(array):
    return (array, array.shape, None)


def scalar(array):
    return (array, None, None)


def stream(array, steps):
    tail = (0,) * (array.ndim - 1)
    return (array, (1,) + array.shape[1:], lambda g: (g // steps,) + tail)


def out_group(shape, dtype, per, stays=True):
    tail = (0,) * (len(shape) - 1)
    return (shape, dtype, (per,) + shape[1:], lambda g: (g,) + tail, stays)


def out_stream(shape, dtype, steps, stays=True):
    tail = (0,) * (len(shape) - 1)
    return (shape, dtype, (1,) + shape[1:], lambda g: (g // steps,) + tail, stays)


def out_whole(shape, dtype, stays=True):
    return (shape, dtype, shape, None, stays)


def rows_of(ref):
    return ref[...].reshape(-1, ref.shape[-1])


def put(ref, value):
    ref[...] = value.reshape(ref.shape).astype(ref.dtype)


def spread(value, mask):
    lanes = value.shape[-1]
    shaped = value.reshape(-1, ROWS, lanes) * mask[None, :, :lanes]
    return shaped.reshape(value.shape)


def add_rows(ref, step, steps, lanes, *values):
    first = step % steps == 0
    for row, value in enumerate(values):
        total = jnp.sum(value, 0, keepdims=True)
        spot = (0, slice(row, row + 1), slice(lanes, lanes + value.shape[-1]))
        if steps > 1:
            total = jnp.where(first, 0.0, ref[spot]) + total
        ref[spot] = total


def stats(total, start, extent, count, folded=0):
    first = total[0, 0:1, start : start + extent]
    second = total[0, 1:2, start : start + extent]
    if folded:
        first, second = fold_lanes(first, folded), fold_lanes(second, folded)
    mean = first / count
    return mean, lax.rsqrt(second / count - mean * mean + EPS)


def fold_lanes(vector, width):
    lanes = vector.shape[-1]
    if width % 128 == 0:
        parts = [vector[:, at : at + width] for at in range(0, lanes, width)]
        one = (parts[0] + parts[1]) + (parts[2] + parts[3])
        return jnp.concatenate([one] * 4, -1)
    wide = jnp.broadcast_to(vector, (8, lanes))
    wide = wide + pltpu.roll(wide, 2 * width, 1)
    wide = wide + pltpu.roll(wide, width, 1)
    return wide[0:1]


def back_parts(sums, start, extent, count, folded=0, rows=(0, 1)):
    one = sums[0, rows[0] : rows[0] + 1, start : start + extent]
    two = sums[0, rows[1] : rows[1] + 1, start : start + extent]
    if folded:
        one, two = fold_lanes(one, folded), fold_lanes(two, folded)
    return one / count, two / count


def norm_back(grad, hat, factor, one, two):
    return factor * (grad - one - hat * two)


def turn(value, step):
    return pltpu.roll(value, step % value.shape[0], 0)


def mul(left, right):
    return jnp.dot(left, right, preferred_element_type=F32)


def mul_t(left, right):
    return lax.dot_general(left, right, (((1,), (1,)), ((), ())), preferred_element_type=F32)


def mul_rows(left, right):
    return lax.dot_general(
        rows_of(left), rows_of(right), (((0,), (0,)), ((), ())), preferred_element_type=F32
    )


def column_cat(act, masks):
    act = act.astype(BF).astype(F32)
    left = spread(turn(act, 1), masks[1])
    right = spread(turn(act, -1), masks[2])
    return jnp.concatenate([left.astype(BF), act.astype(BF), right.astype(BF)], -1)


def row_sum(taps, masks):
    lanes = taps.shape[-1] // 3
    return (
        spread(turn(taps[:, :lanes], WW), masks[3])
        + taps[:, lanes : 2 * lanes]
        + spread(turn(taps[:, 2 * lanes :], -WW), masks[4])
    )


def row_cat(grad, masks):
    grad = grad.astype(BF).astype(F32)
    above = spread(turn(grad, -WW), masks[4])
    below = spread(turn(grad, WW), masks[3])
    return jnp.concatenate([above.astype(BF), grad.astype(BF), below.astype(BF)], -1)


def column_sum(taps, masks):
    lanes = taps.shape[-1] // 3
    return (
        spread(turn(taps[:, :lanes], -1), masks[2])
        + taps[:, lanes : 2 * lanes]
        + spread(turn(taps[:, 2 * lanes :], 1), masks[1])
    )


def k_prep(
    step, near, w_time, w_first, w_back, fproj, fspace, gb, wide, lat, fast, *, shares
):
    places = [sum(shares[:n]) for n in range(len(shares))]
    devices = near.shape[0]
    starts = [0, 3 * CF, 3 * CF + 9 * CFM]
    for d in range(devices):
        block = near[d].astype(F32)
        parts = [block[at : at + rows] for at, rows in zip(places, shares)]
        wide[d * shares[0] : (d + 1) * shares[0]] = parts[0]
        lat[d * shares[1] : (d + 1) * shares[1]] = parts[1]
        for start, part in zip(starts, parts[2:5]):
            at = start + d * part.shape[0]
            fast[at : at + part.shape[0]] = part[:, :128]
    for tap in range(3):
        rows = CS + CL
        w_time[:, tap * CM : (tap + 1) * CM] = wide[tap * rows : (tap + 1) * rows].astype(BF)

    w_first[...] = jnp.zeros_like(w_first)
    w_first[: 3 * CF, :CL] = lat[2 * CF :].astype(BF)
    w_first[4 * CF : 6 * CF, :CL] = lat[: 2 * CF].astype(BF)
    taps = [fast[k * CF : (k + 1) * CF] for k in range(3)]
    order = [5, 0, 1, 2, 3, 6]
    for block in range(7):
        band = [
            pltpu.roll(taps[k], q * CFM, 1) if q else taps[k]
            for q in range(4)
            for k in range(3)
            if order[q + k] == block
        ]
        if band:
            w_first[block * CF : (block + 1) * CF, CL:] = sum(band).astype(BF)
    w_back[...] = jnp.zeros_like(w_back)
    w_back[:, : CL + 128] = w_first[: 4 * CF]
    w_back[2 * CF :, CL + 128 : 2 * CL + 128] = lat[: 2 * CF].astype(BF)
    w_back[:CF, 2 * CL + 128 :] = pltpu.roll(taps[2], 3 * CFM, 1).astype(BF)
    w_back[3 * CF :, 2 * CL + 128 :] = taps[0].astype(BF)

    fproj[...] = jnp.zeros_like(fproj)
    last = fast[starts[2] : starts[2] + CFM].astype(BF)
    for q in range(4):
        fproj[q * CFM : (q + 1) * CFM, q * CF : (q + 1) * CF] = last
    for a in range(3):
        for c in range(3):
            at = starts[1] + (3 * a + c) * CFM
            tap = fast[at : at + CFM]
            for q in range(4):
                rows = c * 128 + q * CFM
                moved = pltpu.roll(tap, q * CFM, 1) if q else tap
                fspace[rows : rows + CFM, a * 128 : (a + 1) * 128] = moved.astype(BF)

    lane = lax.broadcasted_iota(jnp.int32, (8, 128), 1)
    extent = gb.shape[1] // devices
    for row in range(2):
        own = [
            jnp.broadcast_to(
                near[d, places[5 + row] : places[5 + row] + 1, :128].astype(F32), (8, 128)
            )
            for d in range(devices)
        ]
        for tile in range(gb.shape[1] // 128):
            value = jnp.zeros((8, 128), F32)
            for d in range(devices):
                at = d * extent - tile * 128
                if -extent < at < 128:
                    mine = (lane >= at) & (lane < at + extent)
                    moved = pltpu.roll(own[d], at % 128, 1) if at % 128 else own[d]
                    value = jnp.where(mine, moved, value)
            gb[row : row + 1, tile * 128 : (tile + 1) * 128] = value[0:1]


def fill_z(z, at, links, nexts, fast, edge_down, edge_up):
    frames = fast.shape[0]
    for f in range(frames):
        link, following = links[at + f], nexts[at + f]
        for q in range(4):
            z[f, :PIX, q * CF : (q + 1) * CF] = fast[f, q]
        for q in range(2):
            prev = edge_down[0, q] if f == 0 else fast[f - 1, 2 + q]
            z[f, :PIX, (4 + q) * CF : (5 + q) * CF] = (link * prev.astype(F32)).astype(BF)
        follow = edge_up[0, 0] if f == frames - 1 else fast[f + 1, 0]
        z[f, :PIX, 6 * CF :] = (following * follow.astype(F32)).astype(BF)


def k_first(
    step, links, nexts, fast, edge_down, edge_up, weight, lat, fone, total, z
):
    z[...] = jnp.zeros_like(z)
    fill_z(z, step * fast.shape[0], links, nexts, fast, edge_down, edge_up)
    value = mul(rows_of(z), weight[...])
    put(lat, value[:, :CL])
    put(fone, value[:, CL:])
    add_rows(total, step, 1, 0, value, value * value)


def k_taps(step, links, lat, total, gb, slow, w_time, masks, lat_act, taps, tail, head, *, count):
    frames = slow.shape[0]
    mean, scale = stats(total, 0, CL, count)
    hat = (rows_of(lat) - mean) * scale
    act = spread(gelu(hat * gb[0:1, :CL] + gb[1:2, :CL]), masks[0]).astype(BF)
    put(lat_act, act)
    value = mul(rows_of(slow), w_time[:CS]) + mul(act, w_time[CS:])
    put(taps, value)
    tail[0] = value[(frames - 1) * ROWS :, :CM].astype(BF)
    head[0] = (links[step * frames] * value[:ROWS, 2 * CM :]).astype(BF)


def k_short(
    step, slow, lat_act, w_proj, fone, total, fgb, fspace, masks,
    short, fact, ftwo, sums, *, steps, count
):
    value = mul(rows_of(slow), w_proj[:CS]) + mul(rows_of(lat_act), w_proj[CS:])
    put(short, value)
    add_rows(sums, step, steps, 0, value, value * value)
    mean, scale = stats(total, CL, 128, 4.0 * count, CFM)
    hat = (rows_of(fone) - mean) * scale
    act = spread(gelu(hat * fgb[0:1, :128] + fgb[1:2, :128]), masks[0])
    cat = column_cat(act, masks)
    put(fact, cat)
    value = row_sum(mul(cat, fspace[...]), masks)
    put(ftwo, value)
    add_rows(sums, step, steps, CS, value, value * value)


def k_one(step, links, nexts, taps, rim_before, rim_after, given, slow_one, sums):
    frames = taps.shape[0]
    base = step * frames
    one = two = 0.0
    for f in range(frames):
        prev = rim_before[0].astype(F32) if f == 0 else taps[f - 1, :, :CM]
        follow = rim_after[0].astype(F32) if f == frames - 1 else taps[f + 1, :, 2 * CM :]
        value = links[base + f] * prev + taps[f, :, CM : 2 * CM] + nexts[base + f] * follow
        slow_one[f] = value
        one += jnp.sum(value, 0, keepdims=True)
        two += jnp.sum(value * value, 0, keepdims=True)
    sums[0, :, : CS + 128] = given[0]
    sums[0, 0:1, CS + 128 :] = one
    sums[0, 1:2, CS + 128 :] = two


def k_two(
    step, slow_one, ftwo, total, gb, fgb, space, fproj, masks,
    cat_out, two_out, fact_out, fthree, sums, w_space, *, steps, count
):
    @pl.when(step == 0)
    def _():
        for a in range(3):
            for c in range(3):
                tap = space[(3 * a + c) * CM : (3 * a + c + 1) * CM]
                w_space[c * CM : (c + 1) * CM, a * CM : (a + 1) * CM] = tap

    mean, scale = stats(total, CS + 128, CM, count)
    hat = (rows_of(slow_one) - mean) * scale
    act = spread(gelu(hat * gb[0:1, CL : 2 * CL] + gb[1:2, CL : 2 * CL]), masks[0])
    cat = column_cat(act, masks)
    put(cat_out, cat)
    value = row_sum(mul(cat, w_space[...]), masks)
    put(two_out, value)
    add_rows(sums, step, steps, 0, value, value * value)
    mean, scale = stats(total, CS, 128, 4.0 * count, CFM)
    hat = (rows_of(ftwo) - mean) * scale
    act = spread(gelu(hat * fgb[0:1, 128:256] + fgb[1:2, 128:256]), masks[0]).astype(BF)
    put(fact_out, act)
    value = mul(act, fproj[...])
    put(fthree, value)
    add_rows(sums, step, steps, CM, value, value * value)


def k_three(
    step, slow_two, total, gb, rows_out, masks, act_out, sums, w_out, wide, *, steps, count
):
    @pl.when(step == 0)
    def _():
        for half in range(2):
            wide[half] = rows_out[:, half * 128 : (half + 1) * 128].astype(F32)
            for j in range(4):
                at = j * CM + half * 128
                w_out[:, at : at + 128] = wide[half, pl.ds(j, CM, stride=4), :].astype(BF)
    mean, scale = stats(total, 0, CM, count)
    hat = (rows_of(slow_two) - mean) * scale
    act = gelu(hat * gb[0:1, 2 * CL : 3 * CL] + gb[1:2, 2 * CL : 3 * CL])
    act = spread(act, masks[0]).astype(BF)
    put(act_out, act)
    value = mul(act, w_out[...])
    add_rows(sums, step, steps, 0, value, value * value)


CHUNK = 16
SPAN = 512


def gelu_both(value):
    square = value * value
    tan = jnp.tanh(value * (0.7978845608028654 + 0.035677408136300125 * square))
    half = 0.5 + 0.5 * tan
    inner = 0.7978845608028654 + 0.10703222440890037 * square
    slope = half + (0.5 * value) * (1.0 - tan * tan) * inner
    return value * half, slope


def chunked(body, frames, lanes, first=lambda f: None, sums=None):
    full = PIX // CHUNK
    last = full * CHUNK

    def frame(f, carry):
        first(f)
        for start in range(0, lanes, SPAN):
            span = slice(start, start + SPAN)

            def step(i, totals):
                at = pl.ds(pl.multiple_of(i * CHUNK, CHUNK), CHUNK)
                terms = body(f, at, CHUNK, span) or ()
                return tuple(total + halves(term) for total, term in zip(totals, terms))

            count = 0 if sums is None else sums.shape[0]
            totals = tuple(jnp.zeros((8, SPAN), F32) for _ in range(count))
            totals = lax.fori_loop(0, full, step, totals, unroll=full if lanes == SPAN else 4)
            terms = body(f, pl.ds(last, CHUNK), PIX - last, span) or ()
            for n, (total, term) in enumerate(zip(totals, terms)):
                sums[n, :, span] += total + halves(term)
        return carry

    lax.fori_loop(0, frames, frame, 0)


def halves(value):
    return value[:8] + value[8:]


def k_fast_out(step, fthree, fast, cot, total, fgb, out, grad, sums, acc, *, steps, count):
    mean, scale = stats(total, CM, 4 * CF, 4.0 * count, CF)
    factor = fgb[0:1, 256:] * scale
    shift = fgb[1:2, 256:] - mean * factor

    @pl.when(step % steps == 0)
    def _():
        acc[...] = jnp.zeros_like(acc)

    def body(f, rows, real, lanes):
        value = fthree[f, rows, lanes]
        quads = [fast[f, q, pl.ds(rows.start, real), :].astype(F32) for q in range(4)]
        if real < CHUNK:
            blank = jnp.zeros((CHUNK - real, CF), F32)
            quads = [jnp.concatenate([part, blank], 0) for part in quads]
        act, slope = gelu_both(
            value * factor[:, lanes] + (shift[:, lanes] + jnp.concatenate(quads, -1))
        )
        act = act.astype(BF)
        for q in range(4):
            piece = act[:real, q * CF : (q + 1) * CF]
            out[f, q, pl.ds(rows.start, real), :] = piece
        slope = slope * cot[f, rows, lanes].astype(F32)
        grad[f, rows, lanes] = slope
        return slope, slope * value

    chunked(body, fthree.shape[0], 4 * CF, sums=acc)

    @pl.when(step % steps == steps - 1)
    def _():
        one = jnp.sum(acc[0], 0, keepdims=True)
        sums[0, 0:1] = one
        sums[0, 1:2] = scale * (jnp.sum(acc[1], 0, keepdims=True) - mean * one)


def k_out(
    step, act, w_out, short, cot, total, short_total, gb, given, out, grad_out, sums, three, acc,
    *, steps, count
):
    def expand(f):
        three[...] = mul(act[f], w_out[...])

    mean_a, scale_a = stats(total, 0, CS, count)
    mean_b, scale_b = stats(short_total, 0, CS, count)
    factor_a = gb[0:1, 768:1792] * scale_a
    factor_b = gb[0:1, 1792:] * scale_b
    shift = gb[1:2, 768:1792] - mean_a * factor_a + (gb[1:2, 1792:] - mean_b * factor_b)

    @pl.when(step % steps == 0)
    def _():
        acc[...] = jnp.zeros_like(acc)

    def body(f, rows, real, lanes):
        value_a, value_b = three[rows, lanes], short[f, rows, lanes]
        smooth, slope = gelu_both(
            value_a * factor_a[:, lanes] + (value_b * factor_b[:, lanes] + shift[:, lanes])
        )
        out[f, pl.ds(rows.start, real), lanes] = smooth.astype(BF)[:real]
        grad = slope * cot[f, rows, lanes].astype(F32)
        grad_out[f, rows, lanes] = grad
        return grad, grad * value_a, grad * value_b

    chunked(body, act.shape[0], CS, expand, acc)

    @pl.when(step % steps == steps - 1)
    def _():
        one, two_a, two_b = (jnp.sum(acc[row], 0, keepdims=True) for row in range(3))
        sums[0, 0:1, :CS] = one
        sums[0, 1:2, :CS] = scale_a * (two_a - mean_a * one)
        sums[0, 2:3, :CS] = scale_b * (two_b - mean_b * one)
        sums[0, 0:2, CS:] = given[0]
        sums[0, 2:3, CS:] = jnp.zeros((1, 4 * CF), F32)


def k_back_three(
    step, act, w_out, short, grad, total, short_total, sums, gb, slow_two, total3,
    d_three, d_short, grad_two, sums_out, three, *, steps, count
):
    def expand(f):
        three[...] = mul(act[f], w_out[...])

    mean_a, scale_a = stats(total, 0, CS, count)
    mean_b, scale_b = stats(short_total, 0, CS, count)
    one, two_a = back_parts(sums, 0, CS, count)
    _, two_b = back_parts(sums, 0, CS, count, rows=(0, 2))
    factor_a = gb[0:1, 768:1792] * scale_a
    factor_b = gb[0:1, 1792:] * scale_b
    slant_a, slant_b = -factor_a * two_a * scale_a, -factor_b * two_b * scale_b
    shift_a = -factor_a * one - slant_a * mean_a
    shift_b = -factor_b * one - slant_b * mean_b

    def body(f, rows, real, lanes):
        given = grad[f, rows, lanes]
        value_a = three[rows, lanes] * slant_a[:, lanes] + shift_a[:, lanes]
        value_b = short[f, rows, lanes] * slant_b[:, lanes] + shift_b[:, lanes]
        value_a = value_a + given * factor_a[:, lanes]
        value_b = value_b + given * factor_b[:, lanes]
        if real < CHUNK:
            row = lax.broadcasted_iota(jnp.int32, value_a.shape, 0)
            value_a = jnp.where(row < real, value_a, 0.0)
            value_b = jnp.where(row < real, value_b, 0.0)
        d_three[f, rows, lanes] = value_a.astype(BF)
        d_short[f, rows, lanes] = value_b.astype(BF)

    chunked(body, act.shape[0], CS, expand)
    mean, scale = stats(total3, 0, CM, count)
    hat = (rows_of(slow_two) - mean) * scale
    slope = gelu_slope(hat * gb[0:1, 2 * CL : 3 * CL] + gb[1:2, 2 * CL : 3 * CL])
    value = slope * mul_t(rows_of(d_three), w_out[...])
    put(grad_two, value)
    add_rows(sums_out, step, steps, 0, value, value * hat)


def k_back_fast_three(
    step, given, sums, total3, fgrad, fthree, ftwo, fgb, fproj, total2,
    d_fthree, fgrad_two, sums_out, *, steps, count
):
    @pl.when(step % steps == 0)
    def _():
        sums_out[0, :, :CM] = given[0]

    mean, scale = stats(total3, CM, 4 * CF, 4.0 * count, CF)
    one, two = back_parts(sums, CS, 4 * CF, 4.0 * count, CF)
    factor = fgb[0:1, 256:] * scale
    slant = -factor * two * scale
    shift = -factor * one - slant * mean

    def fast_body(f, rows, real, lanes):
        value = fthree[f, rows, lanes] * slant[:, lanes] + shift[:, lanes]
        value = value + fgrad[f, rows, lanes] * factor[:, lanes]
        if real < CHUNK:
            row = lax.broadcasted_iota(jnp.int32, value.shape, 0)
            value = jnp.where(row < real, value, 0.0)
        d_fthree[f, rows, lanes] = value.astype(BF)

    chunked(fast_body, fthree.shape[0], 4 * CF)
    mean, scale = stats(total2, CS, 128, 4.0 * count, CFM)
    hat = (rows_of(ftwo) - mean) * scale
    slope = gelu_slope(hat * fgb[0:1, 128:256] + fgb[1:2, 128:256])
    value = slope * mul_t(rows_of(d_fthree), fproj[...])
    put(fgrad_two, value)
    add_rows(sums_out, step, steps, CM, value, value * hat)


def k_back_two(
    step, slow_two, total3, grad_two, sums, gb, w_space, slow_one, total2,
    ftwo, fgrad_two, fgb, fspace, fone, total1, masks,
    taps_out, grad_one, ftaps_out, fgrad_one, sums_out, *, steps, count
):
    mean, scale = stats(total3, 0, CM, count)
    one, two = back_parts(sums, 0, CM, count)
    hat = (rows_of(slow_two) - mean) * scale
    value = norm_back(rows_of(grad_two), hat, gb[0:1, 2 * CL : 3 * CL] * scale, one, two)
    cat = row_cat(spread(value, masks[0]), masks)
    put(taps_out, cat)
    value = column_sum(mul_t(cat, w_space[...]), masks)
    mean, scale = stats(total2, CS + 128, CM, count)
    hat = (rows_of(slow_one) - mean) * scale
    value = gelu_slope(hat * gb[0:1, CL : 2 * CL] + gb[1:2, CL : 2 * CL]) * value
    put(grad_one, value)
    add_rows(sums_out, step, steps, 0, value, value * hat)

    mean, scale = stats(total2, CS, 128, 4.0 * count, CFM)
    one, two = back_parts(sums, CM, 128, 4.0 * count, CFM)
    hat = (rows_of(ftwo) - mean) * scale
    value = norm_back(rows_of(fgrad_two), hat, fgb[0:1, 128:256] * scale, one, two)
    cat = row_cat(spread(value, masks[0]), masks)
    put(ftaps_out, cat)
    value = column_sum(mul_t(cat, fspace[...]), masks)
    mean, scale = stats(total1, CL, 128, 4.0 * count, CFM)
    hat = (rows_of(fone) - mean) * scale
    value = gelu_slope(hat * fgb[0:1, :128] + fgb[1:2, :128]) * value
    put(fgrad_one, value)
    add_rows(sums_out, step, steps, CM, value, value * hat)


def k_back_one(
    step, links, slow_one, total2, grad_one, fone, total1, fgrad_one, sums, gb, fgb, masks,
    d_one, d_fone, tail, head, *, count
):
    frames = slow_one.shape[0]
    mean, scale = stats(total2, CS + 128, CM, count)
    one, two = back_parts(sums, 0, CM, count)
    hat = (rows_of(slow_one) - mean) * scale
    value = norm_back(rows_of(grad_one), hat, gb[0:1, CL : 2 * CL] * scale, one, two)
    value = spread(value, masks[0])
    put(d_one, value)
    mean, scale = stats(total1, CL, 128, 4.0 * count, CFM)
    one, two = back_parts(sums, CM, 128, 4.0 * count, CFM)
    hat = (rows_of(fone) - mean) * scale
    fvalue = norm_back(rows_of(fgrad_one), hat, fgb[0:1, :128] * scale, one, two)
    fvalue = spread(fvalue, masks[0])
    put(d_fone, fvalue)
    last = (frames - 1) * ROWS
    tail[0, :, :CM] = value[last:].astype(BF)
    tail[0, :, CM:] = fvalue[last:].astype(BF)
    link = links[step * frames]
    head[0, :, :CM] = (link * value[:ROWS]).astype(BF)
    head[0, :, CM:] = (link * fvalue[:ROWS]).astype(BF)


def k_trio(
    step, links, nexts, d_one, rim_before, rim_after, d_short, w_time, w_proj, lat, total1, gb,
    trio, grad, sums, *, count
):
    frames = d_one.shape[0]
    base = step * frames
    for f in range(frames):
        prev = rim_before[0, :, :CM] if f == 0 else d_one[f - 1]
        follow = rim_after[0, :, :CM] if f == frames - 1 else d_one[f + 1]
        trio[f, :, :CM] = (nexts[base + f] * follow.astype(F32)).astype(BF)
        trio[f, :, CM : 2 * CM] = d_one[f]
        trio[f, :, 2 * CM :] = (links[base + f] * prev.astype(F32)).astype(BF)
    value = mul_t(rows_of(trio), w_time[CS:]) + mul_t(rows_of(d_short), w_proj[CS:])
    mean, scale = stats(total1, 0, CL, count)
    hat = (rows_of(lat) - mean) * scale
    value = gelu_slope(hat * gb[0:1, :CL] + gb[1:2, :CL]) * value
    put(grad, value)
    add_rows(sums, step, 1, 0, value, value * hat)


def k_slow_grad(step, trio, d_short, w_time, w_proj, out):
    value = mul_t(rows_of(trio), w_time[:CS]) + mul_t(rows_of(d_short), w_proj[:CS])
    out[...] = value.reshape(-1, ROWS, CS)[:, :PIX].astype(BF)


def k_back_lat(step, links, lat, total1, grad, sums, gb, masks, d_lat, head, *, count):
    frames = lat.shape[0]
    mean, scale = stats(total1, 0, CL, count)
    one, two = back_parts(sums, 0, CL, count)
    hat = (rows_of(lat) - mean) * scale
    value = norm_back(rows_of(grad), hat, gb[0:1, :CL] * scale, one, two)
    value = spread(value, masks[0])
    put(d_lat, value)
    head[0] = (links[step * frames] * value[:ROWS]).astype(BF)


def k_fast_grad(
    step, links, nexts, fgrad, d_lat, lat_rim, d_fone, rim_before, rim_after, w_back, out, cat
):
    frames = d_lat.shape[0]
    base = step * frames
    for f in range(frames):
        last = f == frames - 1
        follow = lat_rim[0] if last else d_lat[f + 1]
        prev_f = rim_before[0, :, CM:] if f == 0 else d_fone[f - 1]
        next_f = rim_after[0, :, CM:] if last else d_fone[f + 1]
        lane = lax.broadcasted_iota(jnp.int32, prev_f.shape, 1)
        rim = jnp.where(lane >= 96, links[base + f] * prev_f.astype(F32), 0.0)
        rim += jnp.where(lane < 32, nexts[base + f] * next_f.astype(F32), 0.0)
        cat[f, :, :CL] = d_lat[f]
        cat[f, :, CL : CL + 128] = d_fone[f]
        cat[f, :, CL + 128 : 2 * CL + 128] = (nexts[base + f] * follow.astype(F32)).astype(BF)
        cat[f, :, 2 * CL + 128 :] = rim.astype(BF)
    value = rows_of(fgrad) + mul_t(rows_of(cat), w_back[...])
    value = value.reshape(-1, ROWS, 4 * CF)
    for q in range(4):
        out[:, q] = value[:, :PIX, q * CF : (q + 1) * CF].astype(BF)


def k_outer_joined(step, slow, lat, right, out, slots, done, *, parts, taps):
    wide = slots.shape[-1]

    def fetch(part):
        source = slow.at[:, :, part * wide : (part + 1) * wide]
        return pltpu.make_async_copy(source, slots.at[part % 2], done.at[part % 2])

    part = step - 1
    if step == 0:
        fetch(0).start()
    else:
        fetch(part).wait()
        if step < parts:
            fetch(step).start()
    value = mul_rows(slots.at[part % 2] if step else lat, right).astype(BF)
    if taps == 1:
        out[...] = value
    else:
        for tap in range(taps):
            out[tap] = value[:, tap * CM : (tap + 1) * CM]


def outer_joined(slow, lat, right, taps, name):
    wide = 256
    parts = slow.shape[-1] // wide
    block = slow.shape[:2] + (wide,)
    rows, lanes = slow.shape[-1] + lat.shape[-1], right.shape[-1]
    if taps == 1:
        out = ((rows, lanes), BF, (wide, lanes), lambda g: ((g - 1) % (parts + 1), 0), True)
    else:
        out = (
            (taps, rows, CM), BF, (taps, wide, CM), lambda g: (0, (g - 1) % (parts + 1), 0), True
        )
    return call(
        functools.partial(k_outer_joined, parts=parts, taps=taps),
        rows // wide,
        [
            (slow, "hbm", None),
            whole(lat),
            whole(right),
        ],
        [out],
        scratch=[pltpu.VMEM((2,) + block, slow.dtype), pltpu.SemaphoreType.DMA((2,))],
        flops=2 * slow.shape[0] * slow.shape[1] * rows * lanes,
        name=name,
        unroll=True,
    )[0]


def k_outer_out(step, left, right, fleft, fright, out, fout):
    out[...] = mul_rows(left, right).astype(BF)
    value = mul_rows(fleft, fright)
    fout[...] = sum(
        value[q * CFM : (q + 1) * CFM, q * CF : (q + 1) * CF] for q in range(4)
    ).astype(BF)


def lanes_at(value, at):
    return (pltpu.roll(value, (128 - at) % 128, 1) if at else value)[:, :CFM]


def k_outer_space(step, left, right, fleft, fright, out, fout):
    value = mul_rows(left, right).astype(BF)
    for a in range(3):
        out[a, 0] = value[:, a * CM : (a + 1) * CM]
    value = mul_rows(fleft, fright)
    for a in range(3):
        block = value[:, a * 128 : (a + 1) * 128]
        folded = sum(
            lanes_at(block[q * CFM : (q + 1) * CFM], q * CFM) for q in range(4)
        )
        fout[a, 0] = folded.astype(BF)


def k_outer_first(
    step, links, nexts, fast, edge_down, edge_up, d_lat, d_fone, *rest, micro
):
    z = rest[-1]
    z[...] = jnp.zeros_like(z)
    frames = z.shape[0] // micro
    for m in range(micro):
        part = pl.ds(m * frames, frames)
        fill_z(
            z.at[part], m * frames, links, nexts, fast.at[part],
            edge_down.at[pl.ds(m, 1)], edge_up.at[pl.ds(m, 1)],
        )
    blocks = [4, 5, 0, 1, 2]
    taps = [0.0, 0.0, 0.0]
    fast = mul_rows(z, d_fone)
    lat = mul_rows(z, d_lat)
    lat = jnp.concatenate([lat[block * CF : (block + 1) * CF] for block in blocks], 0)
    for q in range(4):
        for k in range(3):
            block = [5, 0, 1, 2, 3, 6][q + k]
            taps[k] += lanes_at(fast[block * CF : (block + 1) * CF], q * CFM)
    if len(rest) == 3:
        out, fout, _ = rest
        out[...] = lat.astype(BF)
        for k in range(3):
            fout[k] = taps[k].astype(BF)
        return
    fspace, fproj, out, _ = rest
    devices = out.shape[0]
    taps = jnp.concatenate(taps, 0)
    at = 0
    for value in (lat[:, :128], lat[:, 128:], taps, fspace[...].astype(F32), fproj[...].astype(F32)):
        rows, lanes = value.shape[0] // devices, value.shape[1]
        for d in range(devices):
            out[d, at : at + rows, :lanes] = value[d * rows : (d + 1) * rows].astype(BF)
        at += rows


def k_params(step, sums_a, sums_b, sums_c, sums_d, out, fast):
    a, b, c, d = (ref[0] + ref[1] for ref in (sums_a, sums_b, sums_c, sums_d))
    for row, place in enumerate((1, 0)):
        out[row : row + 1, :CL] = d[place : place + 1]
        out[row : row + 1, CL : 2 * CL] = c[place : place + 1, :CM]
        out[row : row + 1, 2 * CL : 3 * CL] = b[place : place + 1, :CM]
        out[row : row + 1, 768:1792] = a[place : place + 1, :CS]
        third = 2 if row == 0 else 0
        out[row : row + 1, 1792:] = a[third : third + 1, :CS]
        fast[row : row + 1] = fold_lanes(c[place : place + 1, CM:], CFM)
        fast[row + 2 : row + 3] = fold_lanes(b[place : place + 1, CM:], CFM)
        fast[row + 4 : row + 5] = fold_lanes(a[place : place + 1, CS:], CF)[:, :128]


def mask_table():
    row = np.arange(ROWS)
    col = row % WW
    real = row < PIX
    table = [real, real & (col != 0), real & (col != WW - 1), real & (row >= WW), row < PIX - WW]
    return np.broadcast_to(np.stack(table)[:, :, None], (5, ROWS, CM)).astype(np.float32)


def as_rows(shard):
    return jnp.pad(shard, (0, -shard.shape[0] % CM)).reshape(-1, CM)


def flat_of(gathered, at, shard, lanes):
    rows = -(-shard.shape[0] // CM)
    part = gathered[:, at : at + rows]
    if shard.shape[0] % CM:
        part = part.reshape(part.shape[0], -1)[:, : shard.shape[0]]
    return part.reshape(-1, lanes)


def local(
    slow_in,
    fast_in,
    clip_starts,
    w_lateral,
    w_slow_time,
    w_slow_space,
    w_slow_out,
    w_projection,
    w_fast_time,
    w_fast_space,
    w_fast_out,
    slow_gain,
    slow_bias,
    fast_gain,
    fast_bias,
    slow_cotangent,
    fast_cotangent,
):
    devices = lax.axis_size(AXES)
    micro, frames = slow_in.shape[:2]
    groups = micro * frames
    masks = jnp.asarray(mask_table())
    count = float(frames * PIX * devices)
    me = lax.axis_index(AXES)
    share = slow_gain.shape[0]
    mine, spots, share_start = has_bits(me), slice_spots(me), me * share

    wide = w_projection.reshape(-1, CS)
    shards = [
        w_slow_time, w_lateral, w_fast_time, w_fast_space, w_fast_out, slow_gain, slow_bias
    ]
    widths = (CM, CM, CFM, CFM, CF, share, share)
    whole_rows = all(shard.shape[0] % width == 0 for shard, width in zip(shards, widths))
    if whole_rows:
        packed = [shard.reshape(-1, width) for shard, width in zip(shards, widths)]
        packed = [jnp.pad(part, ((0, 0), (0, CM - part.shape[1]))) for part in packed]
    else:
        packed = [as_rows(shard) for shard in shards]
    near_rows = [part.shape[0] for part in packed]
    places = np.cumsum([0] + near_rows)
    packed = jnp.concatenate(packed, 0)
    near = Gather(mine, jnp.pad(packed, ((0, -packed.shape[0] % 8), (0, 0))))

    fast = tie([], fast_in.reshape(groups, 4, PIX, CF))
    fast, fast_in, wide, slow_in, slow_cotangent, fast_cotangent = tie(
        [near], fast, fast_in, wide, slow_in, slow_cotangent, fast_cotangent
    )
    wide = Gather(mine, wide)
    link = (1 - clip_starts).astype(F32)
    links = link.reshape(groups)
    nexts = jnp.concatenate([link[:, 1:], jnp.ones((micro, 1), F32)], 1).reshape(groups)
    edge_down = from_before(fast_in[:, -2:])
    edge_up = from_after(fast_in[:, :1] * link[:, :1, None, None].astype(BF))
    slow = pad_rows(slow_in).reshape(groups, ROWS, CS)
    cot = pad_rows(slow_cotangent).reshape(groups, ROWS, CS)
    fcot = to_quads(fast_cotangent)
    slow, fcot = tie([near, wide], slow, fcot)
    cot, edge_down, edge_up = tie([near], cot, edge_down, edge_up)

    fast_both = jnp.stack([fast_gain, fast_bias]).astype(F32)
    fgb = jnp.concatenate(
        [
            jnp.tile(part, (1, 4))
            for part in (fast_both[:, :CFM], fast_both[:, CFM : 2 * CFM], fast_both[:, 2 * CFM :])
        ],
        1,
    )

    if whole_rows:
        slow_time, w_first, w_back, fproj, fspace, gb = call(
            functools.partial(k_prep, shares=near_rows),
            1,
            [whole(near.result())],
            [
                out_whole((CS + CL, 3 * CM), BF), out_whole((7 * CF, CL + 128), BF),
                out_whole((4 * CF, 768), BF), out_whole((128, 4 * CF), BF),
                out_whole((384, 384), BF), out_whole((2, 2816), F32),
            ],
            scratch=[
                pltpu.VMEM((3 * (CS + CL), CM), F32), pltpu.VMEM((5 * CF, CL), F32),
                pltpu.VMEM((3 * CF + 9 * CFM + CFM, 128), F32),
            ],
            name="first_weights",
            limit=16,
        )
    else:
        weights = near.result()
        cuts = [
            flat_of(weights, int(at), shard, lanes)
            for at, shard, lanes in zip(places, shards, (CM, CL, CFM, CFM, CF, share, share))
        ]
        slow_time = cuts[0].reshape(3, CS + CL, CM)
        slow_time = jnp.concatenate([slow_time[tap] for tap in range(3)], -1)
        lateral, fast_time, fast_space, fast_proj = cuts[1:5]
        gb = jnp.stack([cuts[5].reshape(-1), cuts[6].reshape(-1)]).astype(F32)
        fast_time = fast_time.reshape(3, CF, CFM)
        order = [5, 0, 1, 2, 3, 6]
        band = np.zeros((3, 7, 4), np.float32)
        for q in range(4):
            for k in range(3):
                band[k, order[q + k], q] = 1
        band = jnp.asarray(band, BF)
        fast_band = jnp.sum(
            band[:, :, None, :, None] * fast_time[:, None, :, None, :], 0, dtype=F32
        ).astype(BF).reshape(7 * CF, 4 * CFM)
        none = jnp.zeros((CF, CL), BF)
        lat_band = jnp.concatenate([lateral[2 * CF :], none, lateral[: 2 * CF], none], 0)
        w_first = jnp.concatenate([lat_band, fast_band], -1)
        eye4 = jnp.eye(4, dtype=BF)
        fproj = (fast_proj[None, :, None, :] * eye4[:, None, :, None]).reshape(4 * CFM, 4 * CF)
        lat_prev = jnp.concatenate([jnp.zeros((2 * CF, CL), BF), lateral[: 2 * CF]], 0)
        blank = jnp.zeros((CF, 3 * CFM), BF)
        rim_rows = jnp.concatenate(
            [
                jnp.concatenate([blank, fast_time[2]], -1),
                jnp.zeros((2 * CF, 4 * CFM), BF),
                jnp.concatenate([fast_time[0], blank], -1),
            ],
            0,
        )
        fspace = fast_space.reshape(3, 3, CFM, CFM).transpose(1, 2, 0, 3)
        fspace = fspace[:, None, :, :, None, :] * eye4[None, :, None, None, :, None]
        fspace = fspace.reshape(3 * 4 * CFM, 3 * 4 * CFM)
        w_back = jnp.concatenate([w_first[: 4 * CF], lat_prev, rim_rows], -1)

    far = jnp.concatenate([as_rows(w_slow_space), as_rows(w_slow_out)], 0)
    links, nexts, w_first, spots, mine, share_start, far, *mids = tie(
        [], links, nexts, w_first, spots, mine, share_start, far,
        gb, fgb, fspace, fproj, w_back,
    )
    gb, fgb, fspace, fproj, w_back = mids
    fars = []
    space_rows = -(-w_slow_space.shape[0] // CM)

    rows = groups * ROWS
    bind = functools.partial

    def og(lanes, dtype, per):
        return out_group((groups, ROWS, lanes), dtype, per)

    def os(per, n, lanes):
        return out_stream((micro, n, lanes), F32, frames // per)

    def edge(lanes):
        return out_stream((micro, ROWS, lanes), BF, 1)

    def hooked(*stages):
        return lambda value, stage: tie(stages[stage], value) if stage < len(stages) else value

    def first_hook(value, stage):
        if stage == 1:
            value = tie([wide], value)
            fars.append(Gather(mine, far))
        return value

    lat_pre, fone, sums = call(
        k_first,
        micro,
        [
            scalar(links), scalar(nexts), group(fast, frames), stream(edge_down, 1),
            stream(edge_up, 1), whole(w_first),
        ],
        [og(CL, F32, frames), og(128, F32, frames), os(frames, 2, CL + 128)],
        scratch=[pltpu.VMEM((frames, ROWS, 7 * CF), BF)],
        flops=2 * rows * 896 * 384,
        name="lateral_and_fast_time",
    )
    total1 = all_sum(sums, first_hook)

    lat_act, taps, tail, head = call(
        bind(k_taps, count=count),
        micro,
        [
            scalar(links), group(lat_pre, frames), stream(total1, 1), whole(gb),
            group(slow, frames), whole(slow_time), whole(masks),
        ],
        [og(CL, BF, frames), og(3 * CM, F32, frames), edge(CM), edge(CM)],
        flops=2 * rows * 1280 * 768,
        name="slow_time_taps",
    )
    rim_before, rim_after = from_before(tail), from_after(head)
    far = fars[0]
    lat_act = tie([wide, far], lat_act)
    projection = wide.result().reshape(CS + CL, CS)
    per = frames
    state, fact_cat, sums = call(
        bind(k_short, steps=1, count=count),
        micro,
        [
            group(slow, per), group(lat_act, per), whole(projection), group(fone, per),
            stream(total1, 1), whole(fgb), whole(fspace), whole(masks),
        ],
        [
            ("short", per), og(384, BF, per), ("ftwo", per), os(per, 2, CS + 128),
        ],
        state={},
        flops=2 * rows * 1280 * 1024,
        name="shortcut_and_fast_space",
    )
    state, sums = call(
        k_one,
        micro,
        [
            scalar(links), scalar(nexts), group(taps, frames),
            stream(rim_before, 1), stream(rim_after, 1), stream(sums, 1),
        ],
        [("one", frames), os(frames, 2, CS + 128 + CM)],
        state=state,
        name="slow_one",
    )
    total2 = all_sum(sums, hooked([far], [far]))
    weights = far.result()
    space = flat_of(weights, 0, w_slow_space, CM)
    rows_out = flat_of(weights, space_rows, w_slow_out, CM)

    state, cat_one, fact_two, sums, slow_space = call(
        bind(k_two, steps=1, count=count),
        micro,
        [
            ("one", per), ("ftwo", per), stream(total2, 1), whole(gb), whole(fgb),
            whole(space), whole(fproj), whole(masks),
        ],
        [
            og(3 * CM, BF, per), ("two", per), og(128, BF, per), ("fthree", per),
            os(per, 2, CM + 4 * CF), out_whole((3 * CM, 3 * CM), BF),
        ],
        state=state,
        flops=2 * rows * 768 * 768,
        name="slow_space",
    )
    total3 = all_sum(sums)

    state, act_two, sums, slow_proj = call(
        bind(k_three, steps=1, count=count),
        micro,
        [
            ("two", per), stream(total3, 1), whole(gb), whole(rows_out),
            whole(masks),
        ],
        [og(CM, BF, per), os(per, 2, CS), out_whole((CM, CS), BF)],
        state=state,
        scratch=[pltpu.VMEM((2, 4 * CM, 128), F32)],
        flops=2 * rows * 256 * 1024,
        name="slow_three",
    )
    per = 2 if frames % 2 == 0 else 1
    steps = frames // per
    quarters = ((groups, 4, PIX, CF), BF)
    state, fast_out, fsums = call(
        bind(k_fast_out, steps=steps, count=count),
        groups // per,
        [
            ("fthree", per), group(fast, per), group(fcot, per), stream(total3, steps),
            whole(fgb),
        ],
        [out_group(*quarters, per, False), ("fgrad", per), os(per, 2, 4 * CF)],
        state=state,
        scratch=[pltpu.VMEM((2, 8, 4 * CF), F32)],
        flops=rows * 512 * 200,
        name="fast_out",
    )
    total4 = all_sum(sums)

    state, slow_out, sums = call(
        bind(k_out, steps=steps, count=count),
        groups // per,
        [
            group(act_two, per), whole(slow_proj), ("short", per), group(cot, per),
            stream(total4, steps), stream(total2, steps), whole(gb), stream(fsums, steps),
        ],
        [
            out_group((groups, PIX, CS), BF, per, False), ("grad", per), os(per, 3, CS + 4 * CF),
        ],
        state=state,
        scratch=[pltpu.VMEM((ROWS, CS), F32), pltpu.VMEM((3, 8, CS), F32)],
        flops=2 * rows * 256 * 1024,
        name="slow_out",
    )
    sums_a = all_sum(sums)

    def pixels_first(value, whole_shape):
        return jnp.swapaxes(value.reshape(whole_shape), 1, 2)

    state, d_three, d_short, sums = call(
        bind(k_back_three, steps=steps, count=count),
        groups // per,
        [
            group(act_two, per), whole(slow_proj), ("short", per), ("grad", per),
            stream(total4, steps), stream(total2, steps), stream(sums_a, steps), whole(gb),
            ("two", per), stream(total3, steps),
        ],
        [og(CS, BF, per), og(CS, BF, per), ("grad_two", per), os(per, 2, CM)],
        state=state,
        scratch=[pltpu.VMEM((ROWS, CS), F32)],
        flops=4 * rows * 256 * 1024,
        name="back_three",
    )
    state, d_fthree, sums = call(
        bind(k_back_fast_three, steps=steps, count=count),
        groups // per,
        [
            stream(sums, steps), stream(sums_a, steps), stream(total3, steps),
            ("fgrad", per), ("fthree", per), ("ftwo", per), whole(fgb), whole(fproj),
            stream(total2, steps),
        ],
        [og(4 * CF, BF, per), ("fgrad_two", per), os(per, 2, CM + 128)],
        state=state,
        flops=2 * rows * 128 * 512,
        name="back_fast_three",
    )

    def shares(value):
        return value.reshape(devices, -1, value.shape[-1])

    flows = {}

    def weights_of_three(value, stage):
        if stage == 0:
            proj_grad = outer_joined(slow, lat_act, d_short, 1, "projection_grad")
            out_grad, flows["fast_out"] = call(
                k_outer_out,
                1,
                [whole(act_two), whole(d_three), whole(fact_two), whole(d_fthree)],
                [out_whole((CM, CS), BF), out_whole((CFM, CF), BF)],
                flops=2 * rows * 256 * 1024,
                name="slow_out_grad",
            )
            value, proj_grad, out_grad = tie([], value, proj_grad, out_grad)
            both = jnp.concatenate([shares(proj_grad), shares(out_grad)], 1)
            flows["a"] = Shares(spots, both)
            flows["proj_rows"] = proj_grad.shape[0] // devices
        elif stage == 1:
            value = tie([flows["a"]], value)
        return value

    sums_b = all_sum(sums, weights_of_three)

    per = frames
    state, two_taps, ftwo_taps, sums = call(
        bind(k_back_two, steps=1, count=count),
        micro,
        [
            ("two", per), stream(total3, 1), ("grad_two", per),
            stream(sums_b, 1), whole(gb), whole(slow_space), ("one", per),
            stream(total2, 1), ("ftwo", per), ("fgrad_two", per), whole(fgb),
            whole(fspace), group(fone, per), stream(total1, 1), whole(masks),
        ],
        [
            og(3 * CM, BF, per), ("grad_one", per), og(384, BF, per), ("fgrad_one", per),
            os(per, 2, CM + 128),
        ],
        state=state,
        flops=2 * rows * 768 * 768,
        name="back_two",
    )
    block = (groups, ROWS, CM)
    slim = (groups, ROWS, 128)

    def weights_of_two(value, stage):
        return tie([flows["a"]], value) if stage == 1 else value

    sums_c = all_sum(sums, weights_of_two)

    state, d_one, d_fone, tail, head = call(
        bind(k_back_one, count=count),
        micro,
        [
            scalar(links), ("one", frames), stream(total2, 1), ("grad_one", frames),
            group(fone, frames), stream(total1, 1), ("fgrad_one", frames), stream(sums_c, 1),
            whole(gb), whole(fgb), whole(masks),
        ],
        [og(CM, BF, frames), og(128, BF, frames), edge(CM + 128), edge(CM + 128)],
        state=state,
        name="back_one",
    )
    rim_before, rim_after = from_before(tail), from_after(head)
    flows["space"], flows["fspace"] = call(
        k_outer_space,
        3,
        [
            (cat_one, block, lambda g: (0, 0, g)), whole(two_taps),
            (fact_cat, slim, lambda g: (0, 0, g)), whole(ftwo_taps),
        ],
        [
            ((3, 3, CM, CM), BF, (3, 1, CM, CM), lambda g: (0, g, 0, 0), True),
            ((3, 3, CFM, CFM), BF, (3, 1, CFM, CFM), lambda g: (0, g, 0, 0), True),
        ],
        flops=2 * rows * 768 * 768,
        name="slow_space_grad",
        unroll=True,
    )
    slow_out = pixels_first(slow_out, slow_in.shape)
    rim_before, rim_after, slow_out, flows["space"] = tie(
        [], rim_before, rim_after, slow_out, flows["space"]
    )
    state, trio, sums = call(
        bind(k_trio, count=count),
        micro,
        [
            scalar(links), scalar(nexts), group(d_one, frames),
            stream(rim_before, 1), stream(rim_after, 1), group(d_short, frames),
            whole(slow_time), whole(projection),
            group(lat_pre, frames), stream(total1, 1), whole(gb),
        ],
        [og(3 * CM, BF, frames), ("lat_grad", frames), os(frames, 2, CL)],
        state=state,
        flops=2 * rows * 1792 * 256,
        name="back_lateral",
    )

    def weights_of_one(value, stage):
        if stage == 0:
            time_grad = outer_joined(slow, lat_act, trio, 3, "slow_time_grad")
            value, time_grad, flows["trio"] = tie([], value, time_grad, trio)
            both = jnp.concatenate([shares(time_grad), shares(flows["space"])], 1)
            flows["b"] = Shares(spots, both)
            flows["time_rows"] = time_grad.shape[0] * time_grad.shape[1] // devices
        elif stage == 1:
            value, later = tie([flows["b"]], value, flows["trio"])
            flows["slow_in_grad"] = call(
                k_slow_grad,
                micro,
                [group(later, per), group(d_short, per), whole(slow_time), whole(projection)],
                [out_group((groups, PIX, CS), BF, per, False)],
                flops=2 * rows * 1792 * 1024,
                name="slow_in_grad",
            )[0]
        elif stage == 2:
            value, flows["slow_in_grad"] = tie([flows["b"]], value, flows["slow_in_grad"])
        return value

    sums_d = all_sum(sums, weights_of_one)
    slow_in_grad = flows["slow_in_grad"]

    state, d_lat, head = call(
        bind(k_back_lat, count=count),
        micro,
        [
            scalar(links), group(lat_pre, frames), stream(total1, 1), ("lat_grad", frames),
            stream(sums_d, 1), whole(gb), whole(masks),
        ],
        [og(CL, BF, frames), edge(CL)],
        state=state,
        name="back_lat",
    )
    lat_rim = from_after(head)
    packed = devices <= CFM
    tops = [
        scalar(links), scalar(nexts), whole(fast), whole(edge_down), whole(edge_up),
        whole(d_lat), whole(d_fone),
    ]
    if packed:
        ends = [flows["fspace"].reshape(-1, CFM), flows["fast_out"]]
        sizes = [5 * CF, 5 * CF, 3 * CF, 9 * CFM, CFM]
        sizes = [size // devices for size in sizes]
        tops += [whole(part) for part in ends]
        outs = [out_whole((devices, -(-sum(sizes) // 8) * 8, 128), BF)]
    else:
        outs = [out_whole((5 * CF, CL), BF), out_whole((3, CF, CFM), BF)]
    first_grad = call(
        bind(k_outer_first, micro=micro),
        1,
        tops,
        outs,
        scratch=[pltpu.VMEM((groups, ROWS, 7 * CF), BF)],
        flops=2 * rows * 896 * 384,
        name="lateral_grad",
    )
    if packed:
        flat = first_grad[0]
    else:
        flat = [
            part.reshape(devices, -1)
            for part in (*first_grad, flows["fspace"], flows["fast_out"])
        ]
        sizes = [part.shape[1] for part in flat]
        flat = jnp.concatenate(flat, 1)
        flat = jnp.pad(flat, ((0, 0), (0, -flat.shape[1] % 1024)))
        flat = flat.reshape(devices, -1, 128)
    last = Shares(spots, flat)
    fast_out = pixels_first(fast_out, fast_in.shape)
    lat_rim, fast_out, slow_in_grad = tie(
        [flows["a"], last], lat_rim, fast_out, slow_in_grad
    )
    slow_in_grad = pixels_first(slow_in_grad, slow_in.shape)
    state, fast_in_grad = call(
        k_fast_grad,
        micro,
        [
            scalar(links), scalar(nexts), ("fgrad", frames), group(d_lat, frames),
            stream(lat_rim, 1), group(d_fone, frames), stream(rim_before, 1),
            stream(rim_after, 1), whole(w_back),
        ],
        [out_group(*quarters, frames, False)],
        state=state,
        scratch=[pltpu.VMEM((frames, ROWS, 768), BF)],
        flops=2 * rows * 768 * 512,
        name="fast_in_grad",
    )
    fast_in_grad, slow_in_grad = tie([flows["b"], last], fast_in_grad, slow_in_grad)
    fast_in_grad = pixels_first(fast_in_grad, fast_in.shape)
    both_out = flows["a"].result().reshape(-1, CS)
    cut = flows["proj_rows"]
    proj_out, out_out = both_out[:cut].reshape(-1), both_out[cut:].reshape(-1)
    both_out = flows["b"].result().reshape(-1, CM)
    cut = flows["time_rows"]
    time_out, space_out = both_out[:cut].reshape(-1), both_out[cut:].reshape(-1)
    flat = last.result()
    smalls = []
    at = 0
    if packed:
        flat = flat.reshape(-1, 128)
        parts = []
        for size, lanes in zip(sizes, (128, 128, CFM, CFM, CF)):
            parts.append(flat[at : at + size, :lanes])
            at += size
        parts = [jnp.concatenate(parts[:2], 1)] + parts[2:]
        smalls = [part.reshape(-1) for part in parts]
    else:
        for size in sizes:
            smalls.append(flat[at : at + size])
            at += size

    norms, fnorms = call(
        k_params,
        1,
        [whole(sums_a), whole(sums_b), whole(sums_c), whole(sums_d)],
        [out_whole((2, 2816), F32), out_whole((8, 128), F32)],
        name="norm_grads",
    )
    norms = pick(norms, share_start, share, 1)
    fast_gain_grad, fast_bias_grad = (
        jnp.concatenate([fnorms[row, :CFM], fnorms[row + 2, :CFM], fnorms[row + 4]])
        for row in range(2)
    )
    return (
        jnp.swapaxes(slow_out, 1, 2),
        jnp.swapaxes(fast_out, 1, 2),
        jnp.swapaxes(slow_in_grad, 1, 2),
        jnp.swapaxes(fast_in_grad, 1, 2),
        smalls[0],
        time_out,
        space_out,
        out_out,
        proj_out,
        smalls[1],
        smalls[2],
        smalls[3],
        norms[0],
        norms[1],
        fast_gain_grad,
        fast_bias_grad,
    )


def solution(mesh):
    frames = P(None, AXES, None, None)
    flat = P(AXES)
    return jax.shard_map(
        local,
        mesh=mesh,
        in_specs=(frames, frames, P(None, AXES))
        + (flat,) * 10
        + (P(), P(), frames, frames),
        out_specs=(frames,) * 4 + (flat,) * 10 + (P(), P()),
        check_vma=False,
    )
```

```python
import functools
import math

import jax
import jax.numpy as jnp
import numpy as np
from jax import lax
from jax.experimental import pallas as pl
from jax.experimental.pallas import tpu as pltpu
from jax.sharding import PartitionSpec as P

CS = 1024
CL = 256
CM = 256
CF = 128
CFM = 32
HH = 14
WW = 14
PIX = HH * WW
ROWS = 208
EPS = 1e-05
AXES = ("path", "dp")
BF = jnp.bfloat16
F32 = jnp.float32


def swap(value, bit):
    count = lax.axis_size(AXES)
    return lax.ppermute(value, AXES, [(i, i ^ bit) for i in range(count)])


def dp_pairs():
    bits = []
    bit = 1
    while bit < lax.axis_size("dp"):
        bits.append(bit)
        bit *= 2
    return [bits[at : at + 2] for at in range(0, len(bits), 2)]


def all_sum(value, hook=lambda value, stage: value):
    value = hook(value + swap(value, lax.axis_size("dp")), 0)
    for stage, pair in enumerate(dp_pairs()):
        if len(pair) == 1:
            value = value + swap(value, pair[0])
        else:
            one, two = pair
            first, second, third = swap(value, one), swap(value, two), swap(value, one + two)
            value = (value + first) + (second + third)
        value = hook(value, stage + 1)
    return value


def has_bits(me):
    bits = [bit for pair in dp_pairs() for bit in pair] + [lax.axis_size("dp")]
    return {bit: (me & bit) != 0 for bit in bits}


def in_order(parts, bits, mine):
    parts = [part[None] for part in parts]
    step = 1
    for bit in bits:
        parts = [jnp.where(mine[bit], parts[k ^ step], parts[k]) for k in range(len(parts))]
        step *= 2
    return jnp.concatenate(parts, 0)


class Gather:
    def __init__(self, mine, value):
        self.mine = mine
        self.shape = value.shape
        self.value = value[None]
        self.stages = dp_pairs()[::-1] + [[lax.axis_size("dp")]]
        self.flight = None
        self.start()

    def start(self):
        if not self.stages:
            self.value = self.value.reshape((-1,) + self.shape)
            return
        self.bits = self.stages.pop(0)
        steps = [
            sum(bit for n, bit in enumerate(self.bits) if k >> n & 1)
            for k in range(1, 2 ** len(self.bits))
        ]
        self.flight = [swap(self.value, step) for step in steps]

    def finish(self):
        stacked = in_order([self.value] + self.flight, self.bits, self.mine)
        if self.stages:
            stacked = jnp.swapaxes(stacked, 0, 1)
        self.value = stacked.reshape((-1,) + self.shape)
        self.flight = None
        self.start()

    def result(self):
        while self.flight is not None:
            self.finish()
        return self.value


def pick(value, start, extent, axis):
    starts = [jnp.int32(0)] * value.ndim
    starts[axis] = start
    sizes = list(value.shape)
    sizes[axis] = extent
    return lax.dynamic_slice(value, starts, sizes, allow_negative_indices=False)


def share_stages():
    return [[lax.axis_size("dp")]] + dp_pairs()


def slice_spots(me):
    spots = []
    for bits in share_stages():
        count = 2 ** len(bits)
        spot = lax.shift_right_logical(me, bits[0].bit_length() - 1) & (count - 1)
        spots.append([spot ^ k for k in range(count)])
    return spots


class Shares:
    def __init__(self, spots, value):
        self.value = value
        self.stages = list(zip(share_stages(), spots))
        self.flight = None
        self.start()

    def start(self):
        if not self.stages:
            return
        bits, spots = self.stages.pop(0)
        count = 2 ** len(bits)
        rest = self.value.shape[-2:]
        axis = 0 if bits[0] == lax.axis_size("dp") else 1
        shaped = self.value.reshape(((2, -1), (-1, count))[axis] + rest)
        parts = [pick(shaped, spot, 1, axis) for spot in spots]
        parts = [part.reshape((-1,) + rest) for part in parts]
        self.keep = parts[0]
        steps = [sum(bit for n, bit in enumerate(bits) if k >> n & 1) for k in range(1, count)]
        self.flight = [swap(part.astype(BF), step) for part, step in zip(parts[1:], steps)]

    def finish(self):
        terms = [self.keep.astype(F32)] + [part.astype(F32) for part in self.flight]
        while len(terms) > 1:
            terms = [sum(terms[at : at + 2]) for at in range(0, len(terms), 2)]
        self.value = terms[0]
        self.flight = None
        self.start()

    def result(self):
        while self.flight is not None:
            self.finish()
        return self.value.reshape(-1)


def tie(flows, *values):
    flows = [flow for flow in flows if flow.flight is not None]
    values, flights = lax.optimization_barrier((values, [flow.flight for flow in flows]))
    for flow, flight in zip(flows, flights):
        flow.flight = flight
        flow.finish()
    return values if len(values) > 1 else values[0]


def from_before(value):
    count = lax.axis_size(AXES)
    return lax.ppermute(value, AXES, [(i, i + 1) for i in range(count - 1)])


def from_after(value):
    count = lax.axis_size(AXES)
    return lax.ppermute(value, AXES, [(i + 1, i) for i in range(count - 1)])


def gelu_tan(value):
    return jnp.tanh(value * (0.7978845608028654 + 0.035677408136300125 * (value * value)))


def gelu(value):
    return value * (0.5 + 0.5 * gelu_tan(value))


def gelu_slope(value):
    tan = gelu_tan(value)
    inner = 0.7978845608028654 + 0.10703222440890037 * (value * value)
    return (0.5 + 0.5 * tan) + (0.5 * value) * (1.0 - tan * tan) * inner


def pad_rows(value):
    return jnp.pad(value, [(0, 0)] * (value.ndim - 2) + [(0, ROWS - PIX), (0, 0)])


def to_quads(value):
    micro, frames, _, lanes = value.shape
    quads = pad_rows(value).reshape(micro * frames // 4, 4, ROWS, lanes)
    return jnp.concatenate([quads[:, place] for place in range(4)], -1)


PARTS = dict(
    short=CS,
    grad=CS,
    grad_two=CM,
    fgrad_two=128,
    grad_one=CM,
    fgrad_one=128,
    lat_grad=CL,
    fthree=4 * CF,
    fgrad=4 * CF,
    one=CM,
    two=CM,
    ftwo=128,
)


def in_vmem(array):
    return pltpu.with_memory_space_constraint(array, pltpu.VMEM)


def call(body, steps, ins, outs, scratch=(), flops=0, name=None, limit=8, unroll=False, state=None, cheap=False):
    names = [given[0] if len(given) == 2 else None for given in outs]
    ins = [group(state[given[0]], given[1]) if len(given) == 2 else given for given in ins]
    if state is not None:
        groups = ins[0][0].shape[0] if not state else next(iter(state.values())).shape[0]
    outs = [
        out_group((groups, ROWS, PARTS[given[0]]), F32, given[1]) if len(given) == 2 else given
        for given in outs
    ]
    arrays = [array for array, _, _ in ins]
    blocks = [(array.shape, block, index) for array, block, index in ins]
    blocks += [(shape, block, index) for shape, _, block, index, _ in outs]

    def view(ref, shape, block, index, step):
        if block in (None, "hbm") or tuple(block) == tuple(shape):
            return ref
        spot = [
            slice(None) if size == full else pl.ds(place * size, size)
            for place, size, full in zip(index(step), block, shape)
        ]
        return ref.at[tuple(spot)]

    def kernel(*refs):
        def run(step, carry):
            views = [view(ref, *given, step) for ref, given in zip(refs, blocks)]
            body(step, *views, *refs[len(blocks) :])
            return carry

        if steps == 1 or unroll:
            for step in range(steps):
                run(step, 0)
        else:
            lax.fori_loop(0, steps, run, 0)

    moved = sum(array.size * array.dtype.itemsize for array in arrays)
    moved += sum(math.prod(shape) * jnp.dtype(dtype).itemsize for shape, dtype, *_ in outs)
    if cheap:
        flops = moved = 1
    vmem = pl.BlockSpec(memory_space=pltpu.VMEM)

    def placed(array, block):
        if block is None:
            return array
        return pltpu.with_memory_space_constraint(
            array, pltpu.HBM if block == "hbm" else pltpu.VMEM
        )

    kinds = {None: pl.BlockSpec(memory_space=pltpu.SMEM), "hbm": pl.BlockSpec(memory_space=pl.ANY)}
    result = pl.pallas_call(
        kernel,
        in_specs=[
            kinds[block] if block in (None, "hbm") else vmem for _, block, _ in ins
        ],
        out_specs=[vmem] * len(outs),
        out_shape=[
            pltpu.VMEM(shape, dtype) if stays else jax.ShapeDtypeStruct(shape, dtype)
            for shape, dtype, _, _, stays in outs
        ],
        scratch_shapes=list(scratch),
        compiler_params=pltpu.CompilerParams(vmem_limit_bytes=limit * 1024 * 1024),
        cost_estimate=pl.CostEstimate(
            flops=int(flops), bytes_accessed=int(moved), transcendentals=0
        ),
        name=name,
    )(*[placed(array, block) for array, block, _ in ins])
    if state is None:
        return result
    fresh = {name: array for name, array in zip(names, result) if name}
    return [{**state, **fresh}] + [array for name, array in zip(names, result) if not name]


def group(array, per):
    tail = (0,) * (array.ndim - 1)
    return (array, (per,) + array.shape[1:], lambda g: (g,) + tail)


def whole(array):
    return (array, array.shape, None)


def scalar(array):
    return (array, None, None)


def stream(array, steps):
    tail = (0,) * (array.ndim - 1)
    return (array, (1,) + array.shape[1:], lambda g: (g // steps,) + tail)


def out_group(shape, dtype, per, stays=True):
    tail = (0,) * (len(shape) - 1)
    return (shape, dtype, (per,) + shape[1:], lambda g: (g,) + tail, stays)


def out_stream(shape, dtype, steps, stays=True):
    tail = (0,) * (len(shape) - 1)
    return (shape, dtype, (1,) + shape[1:], lambda g: (g // steps,) + tail, stays)


def out_whole(shape, dtype, stays=True):
    return (shape, dtype, shape, None, stays)


def rows_of(ref):
    return ref[...].reshape(-1, ref.shape[-1])


def put(ref, value):
    ref[...] = value.reshape(ref.shape).astype(ref.dtype)


def spread(value, mask):
    lanes = value.shape[-1]
    shaped = value.reshape(-1, ROWS, lanes) * mask[None, :, :lanes]
    return shaped.reshape(value.shape)


def add_rows(ref, step, steps, lanes, *values):
    first = step % steps == 0
    for row, value in enumerate(values):
        total = jnp.sum(value, 0, keepdims=True)
        spot = (0, slice(row, row + 1), slice(lanes, lanes + value.shape[-1]))
        if steps > 1:
            total = jnp.where(first, 0.0, ref[spot]) + total
        ref[spot] = total


def stats(total, start, extent, count, folded=0):
    first = total[0, 0:1, start : start + extent]
    second = total[0, 1:2, start : start + extent]
    if folded:
        first, second = fold_lanes(first, folded), fold_lanes(second, folded)
    mean = first / count
    return mean, lax.rsqrt(second / count - mean * mean + EPS)


def fold_lanes(vector, width):
    lanes = vector.shape[-1]
    if width % 128 == 0:
        parts = [vector[:, at : at + width] for at in range(0, lanes, width)]
        one = (parts[0] + parts[1]) + (parts[2] + parts[3])
        return jnp.concatenate([one] * 4, -1)
    wide = jnp.broadcast_to(vector, (8, lanes))
    wide = wide + pltpu.roll(wide, 2 * width, 1)
    wide = wide + pltpu.roll(wide, width, 1)
    return wide[0:1]


def back_parts(sums, start, extent, count, folded=0, rows=(0, 1)):
    one = sums[0, rows[0] : rows[0] + 1, start : start + extent]
    two = sums[0, rows[1] : rows[1] + 1, start : start + extent]
    if folded:
        one, two = fold_lanes(one, folded), fold_lanes(two, folded)
    return one / count, two / count


def norm_back(grad, hat, factor, one, two):
    return factor * (grad - one - hat * two)


def turn(value, step):
    return pltpu.roll(value, step % value.shape[0], 0)


def mul(left, right):
    return jnp.dot(left, right, preferred_element_type=F32)


def mul_t(left, right):
    return lax.dot_general(left, right, (((1,), (1,)), ((), ())), preferred_element_type=F32)


def mul_rows(left, right):
    return lax.dot_general(
        rows_of(left), rows_of(right), (((0,), (0,)), ((), ())), preferred_element_type=F32
    )


def column_cat(act, masks):
    act = act.astype(BF).astype(F32)
    left = spread(turn(act, 1), masks[1])
    right = spread(turn(act, -1), masks[2])
    return jnp.concatenate([left.astype(BF), act.astype(BF), right.astype(BF)], -1)


def row_sum(taps, masks):
    lanes = taps.shape[-1] // 3
    return (
        spread(turn(taps[:, :lanes], WW), masks[3])
        + taps[:, lanes : 2 * lanes]
        + spread(turn(taps[:, 2 * lanes :], -WW), masks[4])
    )


def row_cat(grad, masks):
    grad = grad.astype(BF).astype(F32)
    above = spread(turn(grad, -WW), masks[4])
    below = spread(turn(grad, WW), masks[3])
    return jnp.concatenate([above.astype(BF), grad.astype(BF), below.astype(BF)], -1)


def column_sum(taps, masks):
    lanes = taps.shape[-1] // 3
    return (
        spread(turn(taps[:, :lanes], -1), masks[2])
        + taps[:, lanes : 2 * lanes]
        + spread(turn(taps[:, 2 * lanes :], 1), masks[1])
    )


def k_prep(
    step, near, w_time, w_first, w_back, fproj, fspace, gb, wide, lat, fast, *, shares
):
    places = [sum(shares[:n]) for n in range(len(shares))]
    devices = near.shape[0]
    starts = [0, 3 * CF, 3 * CF + 9 * CFM]
    for d in range(devices):
        block = near[d].astype(F32)
        parts = [block[at : at + rows] for at, rows in zip(places, shares)]
        wide[d * shares[0] : (d + 1) * shares[0]] = parts[0]
        lat[d * shares[1] : (d + 1) * shares[1]] = parts[1]
        for start, part in zip(starts, parts[2:5]):
            at = start + d * part.shape[0]
            fast[at : at + part.shape[0]] = part[:, :128]
    for tap in range(3):
        rows = CS + CL
        w_time[:, tap * CM : (tap + 1) * CM] = wide[tap * rows : (tap + 1) * rows].astype(BF)

    w_first[...] = jnp.zeros_like(w_first)
    w_first[: 3 * CF, :CL] = lat[2 * CF :].astype(BF)
    w_first[4 * CF : 6 * CF, :CL] = lat[: 2 * CF].astype(BF)
    taps = [fast[k * CF : (k + 1) * CF] for k in range(3)]
    order = [5, 0, 1, 2, 3, 6]
    for block in range(7):
        band = [
            pltpu.roll(taps[k], q * CFM, 1) if q else taps[k]
            for q in range(4)
            for k in range(3)
            if order[q + k] == block
        ]
        if band:
            w_first[block * CF : (block + 1) * CF, CL:] = sum(band).astype(BF)
    w_back[...] = jnp.zeros_like(w_back)
    w_back[:, : CL + 128] = w_first[: 4 * CF]
    w_back[2 * CF :, CL + 128 : 2 * CL + 128] = lat[: 2 * CF].astype(BF)
    w_back[:CF, 2 * CL + 128 :] = pltpu.roll(taps[2], 3 * CFM, 1).astype(BF)
    w_back[3 * CF :, 2 * CL + 128 :] = taps[0].astype(BF)

    fproj[...] = jnp.zeros_like(fproj)
    last = fast[starts[2] : starts[2] + CFM].astype(BF)
    for q in range(4):
        fproj[q * CFM : (q + 1) * CFM, q * CF : (q + 1) * CF] = last
    for a in range(3):
        for c in range(3):
            at = starts[1] + (3 * a + c) * CFM
            tap = fast[at : at + CFM]
            for q in range(4):
                rows = c * 128 + q * CFM
                moved = pltpu.roll(tap, q * CFM, 1) if q else tap
                fspace[rows : rows + CFM, a * 128 : (a + 1) * 128] = moved.astype(BF)

    lane = lax.broadcasted_iota(jnp.int32, (8, 128), 1)
    extent = gb.shape[1] // devices
    for row in range(2):
        own = [
            jnp.broadcast_to(
                near[d, places[5 + row] : places[5 + row] + 1, :128].astype(F32), (8, 128)
            )
            for d in range(devices)
        ]
        for tile in range(gb.shape[1] // 128):
            value = jnp.zeros((8, 128), F32)
            for d in range(devices):
                at = d * extent - tile * 128
                if -extent < at < 128:
                    mine = (lane >= at) & (lane < at + extent)
                    moved = pltpu.roll(own[d], at % 128, 1) if at % 128 else own[d]
                    value = jnp.where(mine, moved, value)
            gb[row : row + 1, tile * 128 : (tile + 1) * 128] = value[0:1]


def fill_z(z, at, links, nexts, fast, edge_down, edge_up):
    frames = fast.shape[0]
    for f in range(frames):
        link, following = links[at + f], nexts[at + f]
        for q in range(4):
            z[f, :PIX, q * CF : (q + 1) * CF] = fast[f, q]
        for q in range(2):
            prev = edge_down[0, q] if f == 0 else fast[f - 1, 2 + q]
            z[f, :PIX, (4 + q) * CF : (5 + q) * CF] = (link * prev.astype(F32)).astype(BF)
        follow = edge_up[0, 0] if f == frames - 1 else fast[f + 1, 0]
        z[f, :PIX, 6 * CF :] = (following * follow.astype(F32)).astype(BF)


def k_first(
    step, links, nexts, fast, edge_down, edge_up, weight, lat, fone, total, z
):
    z[...] = jnp.zeros_like(z)
    fill_z(z, step * fast.shape[0], links, nexts, fast, edge_down, edge_up)
    value = mul(rows_of(z), weight[...])
    put(lat, value[:, :CL])
    put(fone, value[:, CL:])
    add_rows(total, step, 1, 0, value, value * value)


def k_taps(step, links, lat, total, gb, slow, w_time, masks, lat_act, taps, tail, head, *, count):
    frames = slow.shape[0]
    mean, scale = stats(total, 0, CL, count)
    hat = (rows_of(lat) - mean) * scale
    act = spread(gelu(hat * gb[0:1, :CL] + gb[1:2, :CL]), masks[0]).astype(BF)
    put(lat_act, act)
    value = mul(rows_of(slow), w_time[:CS]) + mul(act, w_time[CS:])
    put(taps, value)
    tail[0] = value[(frames - 1) * ROWS :, :CM].astype(BF)
    head[0] = (links[step * frames] * value[:ROWS, 2 * CM :]).astype(BF)


def k_short(
    step, slow, lat_act, w_proj, fone, total, fgb, fspace, masks,
    short, fact, ftwo, sums, *, steps, count
):
    value = mul(rows_of(slow), w_proj[:CS]) + mul(rows_of(lat_act), w_proj[CS:])
    put(short, value)
    add_rows(sums, step, steps, 0, value, value * value)
    mean, scale = stats(total, CL, 128, 4.0 * count, CFM)
    hat = (rows_of(fone) - mean) * scale
    act = spread(gelu(hat * fgb[0:1, :128] + fgb[1:2, :128]), masks[0])
    cat = column_cat(act, masks)
    put(fact, cat)
    value = row_sum(mul(cat, fspace[...]), masks)
    put(ftwo, value)
    add_rows(sums, step, steps, CS, value, value * value)


def k_one(step, links, nexts, taps, rim_before, rim_after, given, slow_one, sums):
    frames = taps.shape[0]
    base = step * frames
    one = two = 0.0
    for f in range(frames):
        prev = rim_before[0].astype(F32) if f == 0 else taps[f - 1, :, :CM]
        follow = rim_after[0].astype(F32) if f == frames - 1 else taps[f + 1, :, 2 * CM :]
        value = links[base + f] * prev + taps[f, :, CM : 2 * CM] + nexts[base + f] * follow
        slow_one[f] = value
        one += jnp.sum(value, 0, keepdims=True)
        two += jnp.sum(value * value, 0, keepdims=True)
    sums[0, :, : CS + 128] = given[0]
    sums[0, 0:1, CS + 128 :] = one
    sums[0, 1:2, CS + 128 :] = two


def k_two(
    step, slow_one, ftwo, total, gb, fgb, space, fproj, masks,
    cat_out, two_out, fact_out, fthree, sums, w_space, *, steps, count
):
    @pl.when(step == 0)
    def _():
        for a in range(3):
            for c in range(3):
                tap = space[(3 * a + c) * CM : (3 * a + c + 1) * CM]
                w_space[c * CM : (c + 1) * CM, a * CM : (a + 1) * CM] = tap

    mean, scale = stats(total, CS + 128, CM, count)
    hat = (rows_of(slow_one) - mean) * scale
    act = spread(gelu(hat * gb[0:1, CL : 2 * CL] + gb[1:2, CL : 2 * CL]), masks[0])
    cat = column_cat(act, masks)
    put(cat_out, cat)
    value = row_sum(mul(cat, w_space[...]), masks)
    put(two_out, value)
    add_rows(sums, step, steps, 0, value, value * value)
    mean, scale = stats(total, CS, 128, 4.0 * count, CFM)
    hat = (rows_of(ftwo) - mean) * scale
    act = spread(gelu(hat * fgb[0:1, 128:256] + fgb[1:2, 128:256]), masks[0]).astype(BF)
    put(fact_out, act)
    value = mul(act, fproj[...])
    put(fthree, value)
    add_rows(sums, step, steps, CM, value, value * value)


def k_three(
    step, slow_two, total, gb, rows_out, masks, act_out, sums, w_out, wide, *, steps, count
):
    @pl.when(step == 0)
    def _():
        for half in range(2):
            wide[half] = rows_out[:, half * 128 : (half + 1) * 128].astype(F32)
            for j in range(4):
                at = j * CM + half * 128
                w_out[:, at : at + 128] = wide[half, pl.ds(j, CM, stride=4), :].astype(BF)
    mean, scale = stats(total, 0, CM, count)
    hat = (rows_of(slow_two) - mean) * scale
    act = gelu(hat * gb[0:1, 2 * CL : 3 * CL] + gb[1:2, 2 * CL : 3 * CL])
    act = spread(act, masks[0]).astype(BF)
    put(act_out, act)
    value = mul(act, w_out[...])
    add_rows(sums, step, steps, 0, value, value * value)


CHUNK = 16
SPAN = 512


def gelu_both(value):
    square = value * value
    tan = jnp.tanh(value * (0.7978845608028654 + 0.035677408136300125 * square))
    half = 0.5 + 0.5 * tan
    inner = 0.7978845608028654 + 0.10703222440890037 * square
    slope = half + (0.5 * value) * (1.0 - tan * tan) * inner
    return value * half, slope


def chunked(body, frames, lanes, first=lambda f: None, sums=None):
    full = PIX // CHUNK
    last = full * CHUNK

    def frame(f, carry):
        first(f)
        for start in range(0, lanes, SPAN):
            span = slice(start, start + SPAN)

            def step(i, totals):
                at = pl.ds(pl.multiple_of(i * CHUNK, CHUNK), CHUNK)
                terms = body(f, at, CHUNK, span) or ()
                return tuple(total + halves(term) for total, term in zip(totals, terms))

            count = 0 if sums is None else sums.shape[0]
            totals = tuple(jnp.zeros((8, SPAN), F32) for _ in range(count))
            totals = lax.fori_loop(0, full, step, totals, unroll=full if lanes == SPAN else 4)
            terms = body(f, pl.ds(last, CHUNK), PIX - last, span) or ()
            for n, (total, term) in enumerate(zip(totals, terms)):
                sums[n, :, span] += total + halves(term)
        return carry

    lax.fori_loop(0, frames, frame, 0)


def halves(value):
    return value[:8] + value[8:]


def k_fast_out(step, fthree, fast, cot, total, fgb, out, grad, sums, acc, *, steps, count):
    mean, scale = stats(total, CM, 4 * CF, 4.0 * count, CF)
    factor = fgb[0:1, 256:] * scale
    shift = fgb[1:2, 256:] - mean * factor

    @pl.when(step % steps == 0)
    def _():
        acc[...] = jnp.zeros_like(acc)

    def body(f, rows, real, lanes):
        value = fthree[f, rows, lanes]
        quads = [fast[f, q, pl.ds(rows.start, real), :].astype(F32) for q in range(4)]
        if real < CHUNK:
            blank = jnp.zeros((CHUNK - real, CF), F32)
            quads = [jnp.concatenate([part, blank], 0) for part in quads]
        act, slope = gelu_both(
            value * factor[:, lanes] + (shift[:, lanes] + jnp.concatenate(quads, -1))
        )
        act = act.astype(BF)
        for q in range(4):
            piece = act[:real, q * CF : (q + 1) * CF]
            out[f, q, pl.ds(rows.start, real), :] = piece
        slope = slope * cot[f, rows, lanes].astype(F32)
        grad[f, rows, lanes] = slope
        return slope, slope * value

    chunked(body, fthree.shape[0], 4 * CF, sums=acc)

    @pl.when(step % steps == steps - 1)
    def _():
        one = jnp.sum(acc[0], 0, keepdims=True)
        sums[0, 0:1] = one
        sums[0, 1:2] = scale * (jnp.sum(acc[1], 0, keepdims=True) - mean * one)


def k_out(
    step, act, w_out, short, cot, total, short_total, gb, given, out, grad_out, sums, three, acc,
    *, steps, count
):
    def expand(f):
        three[...] = mul(act[f], w_out[...])

    mean_a, scale_a = stats(total, 0, CS, count)
    mean_b, scale_b = stats(short_total, 0, CS, count)
    factor_a = gb[0:1, 768:1792] * scale_a
    factor_b = gb[0:1, 1792:] * scale_b
    shift = gb[1:2, 768:1792] - mean_a * factor_a + (gb[1:2, 1792:] - mean_b * factor_b)

    @pl.when(step % steps == 0)
    def _():
        acc[...] = jnp.zeros_like(acc)

    def body(f, rows, real, lanes):
        value_a, value_b = three[rows, lanes], short[f, rows, lanes]
        smooth, slope = gelu_both(
            value_a * factor_a[:, lanes] + (value_b * factor_b[:, lanes] + shift[:, lanes])
        )
        out[f, pl.ds(rows.start, real), lanes] = smooth.astype(BF)[:real]
        grad = slope * cot[f, rows, lanes].astype(F32)
        grad_out[f, rows, lanes] = grad
        return grad, grad * value_a, grad * value_b

    chunked(body, act.shape[0], CS, expand, acc)

    @pl.when(step % steps == steps - 1)
    def _():
        one, two_a, two_b = (jnp.sum(acc[row], 0, keepdims=True) for row in range(3))
        sums[0, 0:1, :CS] = one
        sums[0, 1:2, :CS] = scale_a * (two_a - mean_a * one)
        sums[0, 2:3, :CS] = scale_b * (two_b - mean_b * one)
        sums[0, 0:2, CS:] = given[0]
        sums[0, 2:3, CS:] = jnp.zeros((1, 4 * CF), F32)


def k_back_three(
    step, act, w_out, short, grad, total, short_total, sums, gb, slow_two, total3,
    d_three, d_short, grad_two, sums_out, three, *, steps, count
):
    def expand(f):
        three[...] = mul(act[f], w_out[...])

    mean_a, scale_a = stats(total, 0, CS, count)
    mean_b, scale_b = stats(short_total, 0, CS, count)
    one, two_a = back_parts(sums, 0, CS, count)
    _, two_b = back_parts(sums, 0, CS, count, rows=(0, 2))
    factor_a = gb[0:1, 768:1792] * scale_a
    factor_b = gb[0:1, 1792:] * scale_b
    slant_a, slant_b = -factor_a * two_a * scale_a, -factor_b * two_b * scale_b
    shift_a = -factor_a * one - slant_a * mean_a
    shift_b = -factor_b * one - slant_b * mean_b

    def body(f, rows, real, lanes):
        given = grad[f, rows, lanes]
        value_a = three[rows, lanes] * slant_a[:, lanes] + shift_a[:, lanes]
        value_b = short[f, rows, lanes] * slant_b[:, lanes] + shift_b[:, lanes]
        value_a = value_a + given * factor_a[:, lanes]
        value_b = value_b + given * factor_b[:, lanes]
        if real < CHUNK:
            row = lax.broadcasted_iota(jnp.int32, value_a.shape, 0)
            value_a = jnp.where(row < real, value_a, 0.0)
            value_b = jnp.where(row < real, value_b, 0.0)
        d_three[f, rows, lanes] = value_a.astype(BF)
        d_short[f, rows, lanes] = value_b.astype(BF)

    chunked(body, act.shape[0], CS, expand)
    mean, scale = stats(total3, 0, CM, count)
    hat = (rows_of(slow_two) - mean) * scale
    slope = gelu_slope(hat * gb[0:1, 2 * CL : 3 * CL] + gb[1:2, 2 * CL : 3 * CL])
    value = slope * mul_t(rows_of(d_three), w_out[...])
    put(grad_two, value)
    add_rows(sums_out, step, steps, 0, value, value * hat)


def k_back_fast_three(
    step, given, sums, total3, fgrad, fthree, ftwo, fgb, fproj, total2,
    d_fthree, fgrad_two, sums_out, *, steps, count
):
    @pl.when(step % steps == 0)
    def _():
        sums_out[0, :, :CM] = given[0]

    mean, scale = stats(total3, CM, 4 * CF, 4.0 * count, CF)
    one, two = back_parts(sums, CS, 4 * CF, 4.0 * count, CF)
    factor = fgb[0:1, 256:] * scale
    slant = -factor * two * scale
    shift = -factor * one - slant * mean

    def fast_body(f, rows, real, lanes):
        value = fthree[f, rows, lanes] * slant[:, lanes] + shift[:, lanes]
        value = value + fgrad[f, rows, lanes] * factor[:, lanes]
        if real < CHUNK:
            row = lax.broadcasted_iota(jnp.int32, value.shape, 0)
            value = jnp.where(row < real, value, 0.0)
        d_fthree[f, rows, lanes] = value.astype(BF)

    chunked(fast_body, fthree.shape[0], 4 * CF)
    mean, scale = stats(total2, CS, 128, 4.0 * count, CFM)
    hat = (rows_of(ftwo) - mean) * scale
    slope = gelu_slope(hat * fgb[0:1, 128:256] + fgb[1:2, 128:256])
    value = slope * mul_t(rows_of(d_fthree), fproj[...])
    put(fgrad_two, value)
    add_rows(sums_out, step, steps, CM, value, value * hat)


def k_back_two(
    step, slow_two, total3, grad_two, sums, gb, w_space, slow_one, total2,
    ftwo, fgrad_two, fgb, fspace, fone, total1, masks,
    taps_out, grad_one, ftaps_out, fgrad_one, sums_out, *, steps, count
):
    mean, scale = stats(total3, 0, CM, count)
    one, two = back_parts(sums, 0, CM, count)
    hat = (rows_of(slow_two) - mean) * scale
    value = norm_back(rows_of(grad_two), hat, gb[0:1, 2 * CL : 3 * CL] * scale, one, two)
    cat = row_cat(spread(value, masks[0]), masks)
    put(taps_out, cat)
    value = column_sum(mul_t(cat, w_space[...]), masks)
    mean, scale = stats(total2, CS + 128, CM, count)
    hat = (rows_of(slow_one) - mean) * scale
    value = gelu_slope(hat * gb[0:1, CL : 2 * CL] + gb[1:2, CL : 2 * CL]) * value
    put(grad_one, value)
    add_rows(sums_out, step, steps, 0, value, value * hat)

    mean, scale = stats(total2, CS, 128, 4.0 * count, CFM)
    one, two = back_parts(sums, CM, 128, 4.0 * count, CFM)
    hat = (rows_of(ftwo) - mean) * scale
    value = norm_back(rows_of(fgrad_two), hat, fgb[0:1, 128:256] * scale, one, two)
    cat = row_cat(spread(value, masks[0]), masks)
    put(ftaps_out, cat)
    value = column_sum(mul_t(cat, fspace[...]), masks)
    mean, scale = stats(total1, CL, 128, 4.0 * count, CFM)
    hat = (rows_of(fone) - mean) * scale
    value = gelu_slope(hat * fgb[0:1, :128] + fgb[1:2, :128]) * value
    put(fgrad_one, value)
    add_rows(sums_out, step, steps, CM, value, value * hat)


def k_back_one(
    step, links, slow_one, total2, grad_one, fone, total1, fgrad_one, sums, gb, fgb, masks,
    d_one, d_fone, tail, head, *, count
):
    frames = slow_one.shape[0]
    mean, scale = stats(total2, CS + 128, CM, count)
    one, two = back_parts(sums, 0, CM, count)
    hat = (rows_of(slow_one) - mean) * scale
    value = norm_back(rows_of(grad_one), hat, gb[0:1, CL : 2 * CL] * scale, one, two)
    value = spread(value, masks[0])
    put(d_one, value)
    mean, scale = stats(total1, CL, 128, 4.0 * count, CFM)
    one, two = back_parts(sums, CM, 128, 4.0 * count, CFM)
    hat = (rows_of(fone) - mean) * scale
    fvalue = norm_back(rows_of(fgrad_one), hat, fgb[0:1, :128] * scale, one, two)
    fvalue = spread(fvalue, masks[0])
    put(d_fone, fvalue)
    last = (frames - 1) * ROWS
    tail[0, :, :CM] = value[last:].astype(BF)
    tail[0, :, CM:] = fvalue[last:].astype(BF)
    link = links[step * frames]
    head[0, :, :CM] = (link * value[:ROWS]).astype(BF)
    head[0, :, CM:] = (link * fvalue[:ROWS]).astype(BF)


def k_trio(
    step, links, nexts, d_one, rim_before, rim_after, d_short, w_time, w_proj, lat, total1, gb,
    trio, grad, sums, *, count
):
    frames = d_one.shape[0]
    base = step * frames
    for f in range(frames):
        prev = rim_before[0, :, :CM] if f == 0 else d_one[f - 1]
        follow = rim_after[0, :, :CM] if f == frames - 1 else d_one[f + 1]
        trio[f, :, :CM] = (nexts[base + f] * follow.astype(F32)).astype(BF)
        trio[f, :, CM : 2 * CM] = d_one[f]
        trio[f, :, 2 * CM :] = (links[base + f] * prev.astype(F32)).astype(BF)
    value = mul_t(rows_of(trio), w_time[CS:]) + mul_t(rows_of(d_short), w_proj[CS:])
    mean, scale = stats(total1, 0, CL, count)
    hat = (rows_of(lat) - mean) * scale
    value = gelu_slope(hat * gb[0:1, :CL] + gb[1:2, :CL]) * value
    put(grad, value)
    add_rows(sums, step, 1, 0, value, value * hat)


def k_slow_grad(step, trio, d_short, w_time, w_proj, out):
    value = mul_t(rows_of(trio), w_time[:CS]) + mul_t(rows_of(d_short), w_proj[:CS])
    out[...] = value.reshape(-1, ROWS, CS)[:, :PIX].astype(BF)


def k_back_lat(step, links, lat, total1, grad, sums, gb, masks, d_lat, head, *, count):
    frames = lat.shape[0]
    mean, scale = stats(total1, 0, CL, count)
    one, two = back_parts(sums, 0, CL, count)
    hat = (rows_of(lat) - mean) * scale
    value = norm_back(rows_of(grad), hat, gb[0:1, :CL] * scale, one, two)
    value = spread(value, masks[0])
    put(d_lat, value)
    head[0] = (links[step * frames] * value[:ROWS]).astype(BF)


def k_fast_grad(
    step, links, nexts, fgrad, d_lat, lat_rim, d_fone, rim_before, rim_after, w_back, out, cat
):
    frames = d_lat.shape[0]
    base = step * frames
    for f in range(frames):
        last = f == frames - 1
        follow = lat_rim[0] if last else d_lat[f + 1]
        prev_f = rim_before[0, :, CM:] if f == 0 else d_fone[f - 1]
        next_f = rim_after[0, :, CM:] if last else d_fone[f + 1]
        lane = lax.broadcasted_iota(jnp.int32, prev_f.shape, 1)
        rim = jnp.where(lane >= 96, links[base + f] * prev_f.astype(F32), 0.0)
        rim += jnp.where(lane < 32, nexts[base + f] * next_f.astype(F32), 0.0)
        cat[f, :, :CL] = d_lat[f]
        cat[f, :, CL : CL + 128] = d_fone[f]
        cat[f, :, CL + 128 : 2 * CL + 128] = (nexts[base + f] * follow.astype(F32)).astype(BF)
        cat[f, :, 2 * CL + 128 :] = rim.astype(BF)
    value = rows_of(fgrad) + mul_t(rows_of(cat), w_back[...])
    value = value.reshape(-1, ROWS, 4 * CF)
    for q in range(4):
        out[:, q] = value[:, :PIX, q * CF : (q + 1) * CF].astype(BF)


def k_outer_joined(step, slow, lat, right, out, slots, done, *, parts, taps):
    wide = slots.shape[-1]

    def fetch(part):
        source = slow.at[:, :, part * wide : (part + 1) * wide]
        return pltpu.make_async_copy(source, slots.at[part % 2], done.at[part % 2])

    part = step - 1
    if step == 0:
        fetch(0).start()
    else:
        fetch(part).wait()
        if step < parts:
            fetch(step).start()
    value = mul_rows(slots.at[part % 2] if step else lat, right).astype(BF)
    if taps == 1:
        out[...] = value
    else:
        for tap in range(taps):
            out[tap] = value[:, tap * CM : (tap + 1) * CM]


def outer_joined(slow, lat, right, taps, name):
    wide = 256
    parts = slow.shape[-1] // wide
    block = slow.shape[:2] + (wide,)
    rows, lanes = slow.shape[-1] + lat.shape[-1], right.shape[-1]
    if taps == 1:
        out = ((rows, lanes), BF, (wide, lanes), lambda g: ((g - 1) % (parts + 1), 0), True)
    else:
        out = (
            (taps, rows, CM), BF, (taps, wide, CM), lambda g: (0, (g - 1) % (parts + 1), 0), True
        )
    return call(
        functools.partial(k_outer_joined, parts=parts, taps=taps),
        rows // wide,
        [
            (slow, "hbm", None),
            whole(lat),
            whole(right),
        ],
        [out],
        scratch=[pltpu.VMEM((2,) + block, slow.dtype), pltpu.SemaphoreType.DMA((2,))],
        flops=2 * slow.shape[0] * slow.shape[1] * rows * lanes,
        name=name,
        unroll=True,
    )[0]


def k_outer_out(step, left, right, fleft, fright, out, fout):
    out[...] = mul_rows(left, right).astype(BF)
    value = mul_rows(fleft, fright)
    fout[...] = sum(
        value[q * CFM : (q + 1) * CFM, q * CF : (q + 1) * CF] for q in range(4)
    ).astype(BF)


def lanes_at(value, at):
    return (pltpu.roll(value, (128 - at) % 128, 1) if at else value)[:, :CFM]


def k_outer_space(step, left, right, fleft, fright, out, fout):
    value = mul_rows(left, right).astype(BF)
    for a in range(3):
        out[a, 0] = value[:, a * CM : (a + 1) * CM]
    value = mul_rows(fleft, fright)
    for a in range(3):
        block = value[:, a * 128 : (a + 1) * 128]
        folded = sum(
            lanes_at(block[q * CFM : (q + 1) * CFM], q * CFM) for q in range(4)
        )
        fout[a, 0] = folded.astype(BF)


def k_outer_first(
    step, links, nexts, fast, edge_down, edge_up, d_lat, d_fone, *rest, micro
):
    z = rest[-1]
    z[...] = jnp.zeros_like(z)
    frames = z.shape[0] // micro
    for m in range(micro):
        part = pl.ds(m * frames, frames)
        fill_z(
            z.at[part], m * frames, links, nexts, fast.at[part],
            edge_down.at[pl.ds(m, 1)], edge_up.at[pl.ds(m, 1)],
        )
    blocks = [4, 5, 0, 1, 2]
    taps = [0.0, 0.0, 0.0]
    fast = mul_rows(z, d_fone)
    lat = mul_rows(z, d_lat)
    lat = jnp.concatenate([lat[block * CF : (block + 1) * CF] for block in blocks], 0)
    for q in range(4):
        for k in range(3):
            block = [5, 0, 1, 2, 3, 6][q + k]
            taps[k] += lanes_at(fast[block * CF : (block + 1) * CF], q * CFM)
    if len(rest) == 3:
        out, fout, _ = rest
        out[...] = lat.astype(BF)
        for k in range(3):
            fout[k] = taps[k].astype(BF)
        return
    fspace, fproj, out, _ = rest
    devices = out.shape[0]
    taps = jnp.concatenate(taps, 0)
    at = 0
    for value in (lat[:, :128], lat[:, 128:], taps, fspace[...].astype(F32), fproj[...].astype(F32)):
        rows, lanes = value.shape[0] // devices, value.shape[1]
        for d in range(devices):
            out[d, at : at + rows, :lanes] = value[d * rows : (d + 1) * rows].astype(BF)
        at += rows


def k_params(step, sums_a, sums_b, sums_c, sums_d, out, fast):
    a, b, c, d = (ref[0] + ref[1] for ref in (sums_a, sums_b, sums_c, sums_d))
    for row, place in enumerate((1, 0)):
        out[row : row + 1, :CL] = d[place : place + 1]
        out[row : row + 1, CL : 2 * CL] = c[place : place + 1, :CM]
        out[row : row + 1, 2 * CL : 3 * CL] = b[place : place + 1, :CM]
        out[row : row + 1, 768:1792] = a[place : place + 1, :CS]
        third = 2 if row == 0 else 0
        out[row : row + 1, 1792:] = a[third : third + 1, :CS]
        fast[row : row + 1] = fold_lanes(c[place : place + 1, CM:], CFM)
        fast[row + 2 : row + 3] = fold_lanes(b[place : place + 1, CM:], CFM)
        fast[row + 4 : row + 5] = fold_lanes(a[place : place + 1, CS:], CF)[:, :128]


def mask_table():
    row = np.arange(ROWS)
    col = row % WW
    real = row < PIX
    table = [real, real & (col != 0), real & (col != WW - 1), real & (row >= WW), row < PIX - WW]
    return np.broadcast_to(np.stack(table)[:, :, None], (5, ROWS, CM)).astype(np.float32)


def as_rows(shard):
    return jnp.pad(shard, (0, -shard.shape[0] % CM)).reshape(-1, CM)


def flat_of(gathered, at, shard, lanes):
    rows = -(-shard.shape[0] // CM)
    part = gathered[:, at : at + rows]
    if shard.shape[0] % CM:
        part = part.reshape(part.shape[0], -1)[:, : shard.shape[0]]
    return part.reshape(-1, lanes)


def local(
    slow_in,
    fast_in,
    clip_starts,
    w_lateral,
    w_slow_time,
    w_slow_space,
    w_slow_out,
    w_projection,
    w_fast_time,
    w_fast_space,
    w_fast_out,
    slow_gain,
    slow_bias,
    fast_gain,
    fast_bias,
    slow_cotangent,
    fast_cotangent,
):
    devices = lax.axis_size(AXES)
    micro, frames = slow_in.shape[:2]
    groups = micro * frames
    masks = jnp.asarray(mask_table())
    count = float(frames * PIX * devices)
    me = lax.axis_index(AXES)
    share = slow_gain.shape[0]
    mine, spots, share_start = has_bits(me), slice_spots(me), me * share

    wide = w_projection.reshape(-1, CS)
    shards = [
        w_slow_time, w_lateral, w_fast_time, w_fast_space, w_fast_out, slow_gain, slow_bias
    ]
    widths = (CM, CM, CFM, CFM, CF, share, share)
    whole_rows = all(shard.shape[0] % width == 0 for shard, width in zip(shards, widths))
    if whole_rows:
        packed = [shard.reshape(-1, width) for shard, width in zip(shards, widths)]
        packed = [jnp.pad(part, ((0, 0), (0, CM - part.shape[1]))) for part in packed]
    else:
        packed = [as_rows(shard) for shard in shards]
    near_rows = [part.shape[0] for part in packed]
    places = np.cumsum([0] + near_rows)
    packed = jnp.concatenate(packed, 0)
    near = Gather(mine, jnp.pad(packed, ((0, -packed.shape[0] % 8), (0, 0))))

    fast_in, slow_in, slow_cotangent, fast_cotangent = tie(
        [near], fast_in, slow_in, slow_cotangent, fast_cotangent
    )
    fast = fast_in.reshape(groups, 4, PIX, CF)
    fast, wide = tie([], fast, wide)
    wide = Gather(mine, wide)
    link = (1 - clip_starts).astype(F32)
    links = link.reshape(groups)
    nexts = jnp.concatenate([link[:, 1:], jnp.ones((micro, 1), F32)], 1).reshape(groups)
    edge_down = from_before(fast_in[:, -2:])
    edge_up = from_after(fast_in[:, :1] * link[:, :1, None, None].astype(BF))
    slow = pad_rows(slow_in).reshape(groups, ROWS, CS)
    cot = pad_rows(slow_cotangent).reshape(groups, ROWS, CS)
    fcot = to_quads(fast_cotangent)
    slow, fcot = tie([near, wide], slow, fcot)
    cot, edge_down, edge_up = tie([near], cot, edge_down, edge_up)

    fast_both = jnp.stack([fast_gain, fast_bias]).astype(F32)
    fgb = jnp.concatenate(
        [
            jnp.tile(part, (1, 4))
            for part in (fast_both[:, :CFM], fast_both[:, CFM : 2 * CFM], fast_both[:, 2 * CFM :])
        ],
        1,
    )

    if whole_rows:
        slow_time, w_first, w_back, fproj, fspace, gb = call(
            functools.partial(k_prep, shares=near_rows),
            1,
            [whole(near.result())],
            [
                out_whole((CS + CL, 3 * CM), BF), out_whole((7 * CF, CL + 128), BF),
                out_whole((4 * CF, 768), BF), out_whole((128, 4 * CF), BF),
                out_whole((384, 384), BF), out_whole((2, 2816), F32),
            ],
            scratch=[
                pltpu.VMEM((3 * (CS + CL), CM), F32), pltpu.VMEM((5 * CF, CL), F32),
                pltpu.VMEM((3 * CF + 9 * CFM + CFM, 128), F32),
            ],
            name="first_weights",
            limit=16,
        )
    else:
        weights = near.result()
        cuts = [
            flat_of(weights, int(at), shard, lanes)
            for at, shard, lanes in zip(places, shards, (CM, CL, CFM, CFM, CF, share, share))
        ]
        slow_time = cuts[0].reshape(3, CS + CL, CM)
        slow_time = jnp.concatenate([slow_time[tap] for tap in range(3)], -1)
        lateral, fast_time, fast_space, fast_proj = cuts[1:5]
        gb = jnp.stack([cuts[5].reshape(-1), cuts[6].reshape(-1)]).astype(F32)
        fast_time = fast_time.reshape(3, CF, CFM)
        order = [5, 0, 1, 2, 3, 6]
        band = np.zeros((3, 7, 4), np.float32)
        for q in range(4):
            for k in range(3):
                band[k, order[q + k], q] = 1
        band = jnp.asarray(band, BF)
        fast_band = jnp.sum(
            band[:, :, None, :, None] * fast_time[:, None, :, None, :], 0, dtype=F32
        ).astype(BF).reshape(7 * CF, 4 * CFM)
        none = jnp.zeros((CF, CL), BF)
        lat_band = jnp.concatenate([lateral[2 * CF :], none, lateral[: 2 * CF], none], 0)
        w_first = jnp.concatenate([lat_band, fast_band], -1)
        eye4 = jnp.eye(4, dtype=BF)
        fproj = (fast_proj[None, :, None, :] * eye4[:, None, :, None]).reshape(4 * CFM, 4 * CF)
        lat_prev = jnp.concatenate([jnp.zeros((2 * CF, CL), BF), lateral[: 2 * CF]], 0)
        blank = jnp.zeros((CF, 3 * CFM), BF)
        rim_rows = jnp.concatenate(
            [
                jnp.concatenate([blank, fast_time[2]], -1),
                jnp.zeros((2 * CF, 4 * CFM), BF),
                jnp.concatenate([fast_time[0], blank], -1),
            ],
            0,
        )
        fspace = fast_space.reshape(3, 3, CFM, CFM).transpose(1, 2, 0, 3)
        fspace = fspace[:, None, :, :, None, :] * eye4[None, :, None, None, :, None]
        fspace = fspace.reshape(3 * 4 * CFM, 3 * 4 * CFM)
        w_back = jnp.concatenate([w_first[: 4 * CF], lat_prev, rim_rows], -1)

    far = jnp.concatenate([as_rows(w_slow_space), as_rows(w_slow_out)], 0)
    links, nexts, w_first, spots, mine, share_start, far, *mids = tie(
        [], links, nexts, w_first, spots, mine, share_start, far,
        gb, fgb, fspace, fproj, w_back,
    )
    gb, fgb, fspace, fproj, w_back = mids
    fars = []
    space_rows = -(-w_slow_space.shape[0] // CM)

    rows = groups * ROWS
    bind = functools.partial

    def og(lanes, dtype, per):
        return out_group((groups, ROWS, lanes), dtype, per)

    def os(per, n, lanes):
        return out_stream((micro, n, lanes), F32, frames // per)

    def edge(lanes):
        return out_stream((micro, ROWS, lanes), BF, 1)

    def hooked(*stages):
        return lambda value, stage: tie(stages[stage], value) if stage < len(stages) else value

    def first_hook(value, stage):
        if stage == 0:
            fars.append(Gather(mine, far))
        elif stage == 1:
            value = tie([wide], value)
        elif stage == 2:
            value = tie(fars, value)
        return value

    lat_pre, fone, sums = call(
        k_first,
        micro,
        [
            scalar(links), scalar(nexts), group(fast, frames), stream(edge_down, 1),
            stream(edge_up, 1), whole(w_first),
        ],
        [og(CL, F32, frames), og(128, F32, frames), os(frames, 2, CL + 128)],
        scratch=[pltpu.VMEM((frames, ROWS, 7 * CF), BF)],
        flops=2 * rows * 896 * 384,
        name="lateral_and_fast_time",
    )
    total1 = all_sum(sums, first_hook)

    lat_act, taps, tail, head = call(
        bind(k_taps, count=count),
        micro,
        [
            scalar(links), group(lat_pre, frames), stream(total1, 1), whole(gb),
            group(slow, frames), whole(slow_time), whole(masks),
        ],
        [og(CL, BF, frames), og(3 * CM, F32, frames), edge(CM), edge(CM)],
        flops=2 * rows * 1280 * 768,
        name="slow_time_taps",
    )
    rim_before, rim_after = from_before(tail), from_after(head)
    far = fars[0]
    lat_act = tie([wide], lat_act)
    projection = wide.result().reshape(CS + CL, CS)
    per = frames
    state, fact_cat, sums = call(
        bind(k_short, steps=1, count=count),
        micro,
        [
            group(slow, per), group(lat_act, per), whole(projection), group(fone, per),
            stream(total1, 1), whole(fgb), whole(fspace), whole(masks),
        ],
        [
            ("short", per), og(384, BF, per), ("ftwo", per), os(per, 2, CS + 128),
        ],
        state={},
        flops=2 * rows * 1280 * 1024,
        name="shortcut_and_fast_space",
    )
    state, sums = call(
        k_one,
        micro,
        [
            scalar(links), scalar(nexts), group(taps, frames),
            stream(rim_before, 1), stream(rim_after, 1), stream(sums, 1),
        ],
        [("one", frames), os(frames, 2, CS + 128 + CM)],
        state=state,
        name="slow_one",
    )
    total2 = all_sum(sums, hooked([far], [far]))
    weights = far.result()
    space = flat_of(weights, 0, w_slow_space, CM)
    rows_out = flat_of(weights, space_rows, w_slow_out, CM)

    state, cat_one, fact_two, sums, slow_space = call(
        bind(k_two, steps=1, count=count),
        micro,
        [
            ("one", per), ("ftwo", per), stream(total2, 1), whole(gb), whole(fgb),
            whole(space), whole(fproj), whole(masks),
        ],
        [
            og(3 * CM, BF, per), ("two", per), og(128, BF, per), ("fthree", per),
            os(per, 2, CM + 4 * CF), out_whole((3 * CM, 3 * CM), BF),
        ],
        state=state,
        flops=2 * rows * 768 * 768,
        name="slow_space",
    )
    total3 = all_sum(sums)

    state, act_two, sums, slow_proj = call(
        bind(k_three, steps=1, count=count),
        micro,
        [
            ("two", per), stream(total3, 1), whole(gb), whole(rows_out),
            whole(masks),
        ],
        [og(CM, BF, per), os(per, 2, CS), out_whole((CM, CS), BF)],
        state=state,
        scratch=[pltpu.VMEM((2, 4 * CM, 128), F32)],
        flops=2 * rows * 256 * 1024,
        name="slow_three",
    )
    per = 2 if frames % 2 == 0 else 1
    steps = frames // per
    quarters = ((groups, 4, PIX, CF), BF)
    state, fast_out, fsums = call(
        bind(k_fast_out, steps=steps, count=count),
        groups // per,
        [
            ("fthree", per), group(fast, per), group(fcot, per), stream(total3, steps),
            whole(fgb),
        ],
        [out_group(*quarters, per, False), ("fgrad", per), os(per, 2, 4 * CF)],
        state=state,
        scratch=[pltpu.VMEM((2, 8, 4 * CF), F32)],
        flops=rows * 512 * 200,
        name="fast_out",
    )
    total4 = all_sum(sums)

    state, slow_out, sums = call(
        bind(k_out, steps=steps, count=count),
        groups // per,
        [
            group(act_two, per), whole(slow_proj), ("short", per), group(cot, per),
            stream(total4, steps), stream(total2, steps), whole(gb), stream(fsums, steps),
        ],
        [
            out_group((groups, PIX, CS), BF, per, False), ("grad", per), os(per, 3, CS + 4 * CF),
        ],
        state=state,
        scratch=[pltpu.VMEM((ROWS, CS), F32), pltpu.VMEM((3, 8, CS), F32)],
        flops=2 * rows * 256 * 1024,
        name="slow_out",
    )
    sums_a = all_sum(sums)

    def pixels_first(value, whole_shape):
        return jnp.swapaxes(value.reshape(whole_shape), 1, 2)

    state, d_three, d_short, sums = call(
        bind(k_back_three, steps=steps, count=count),
        groups // per,
        [
            group(act_two, per), whole(slow_proj), ("short", per), ("grad", per),
            stream(total4, steps), stream(total2, steps), stream(sums_a, steps), whole(gb),
            ("two", per), stream(total3, steps),
        ],
        [og(CS, BF, per), og(CS, BF, per), ("grad_two", per), os(per, 2, CM)],
        state=state,
        scratch=[pltpu.VMEM((ROWS, CS), F32)],
        flops=4 * rows * 256 * 1024,
        name="back_three",
    )
    state, d_fthree, sums = call(
        bind(k_back_fast_three, steps=steps, count=count),
        groups // per,
        [
            stream(sums, steps), stream(sums_a, steps), stream(total3, steps),
            ("fgrad", per), ("fthree", per), ("ftwo", per), whole(fgb), whole(fproj),
            stream(total2, steps),
        ],
        [og(4 * CF, BF, per), ("fgrad_two", per), os(per, 2, CM + 128)],
        state=state,
        flops=2 * rows * 128 * 512,
        name="back_fast_three",
    )

    def shares(value):
        return value.reshape(devices, -1, value.shape[-1])

    flows = {}

    def weights_of_three(value, stage):
        if stage == 0:
            proj_grad = outer_joined(slow, lat_act, d_short, 1, "projection_grad")
            out_grad, flows["fast_out"] = call(
                k_outer_out,
                1,
                [whole(act_two), whole(d_three), whole(fact_two), whole(d_fthree)],
                [out_whole((CM, CS), BF), out_whole((CFM, CF), BF)],
                flops=2 * rows * 256 * 1024,
                name="slow_out_grad",
            )
            value, proj_grad, out_grad = tie([], value, proj_grad, out_grad)
            both = jnp.concatenate([shares(proj_grad), shares(out_grad)], 1)
            flows["a"] = Shares(spots, both)
            flows["proj_rows"] = proj_grad.shape[0] // devices
        elif stage == 1:
            value = tie([flows["a"]], value)
        return value

    sums_b = all_sum(sums, weights_of_three)

    per = frames
    state, two_taps, ftwo_taps, sums = call(
        bind(k_back_two, steps=1, count=count),
        micro,
        [
            ("two", per), stream(total3, 1), ("grad_two", per),
            stream(sums_b, 1), whole(gb), whole(slow_space), ("one", per),
            stream(total2, 1), ("ftwo", per), ("fgrad_two", per), whole(fgb),
            whole(fspace), group(fone, per), stream(total1, 1), whole(masks),
        ],
        [
            og(3 * CM, BF, per), ("grad_one", per), og(384, BF, per), ("fgrad_one", per),
            os(per, 2, CM + 128),
        ],
        state=state,
        flops=2 * rows * 768 * 768,
        name="back_two",
    )
    block = (groups, ROWS, CM)
    slim = (groups, ROWS, 128)

    def weights_of_two(value, stage):
        return tie([flows["a"]], value) if stage == 1 else value

    sums_c = all_sum(sums, weights_of_two)

    state, d_one, d_fone, tail, head = call(
        bind(k_back_one, count=count),
        micro,
        [
            scalar(links), ("one", frames), stream(total2, 1), ("grad_one", frames),
            group(fone, frames), stream(total1, 1), ("fgrad_one", frames), stream(sums_c, 1),
            whole(gb), whole(fgb), whole(masks),
        ],
        [og(CM, BF, frames), og(128, BF, frames), edge(CM + 128), edge(CM + 128)],
        state=state,
        name="back_one",
    )
    rim_before, rim_after = from_before(tail), from_after(head)
    flows["space"], flows["fspace"] = call(
        k_outer_space,
        3,
        [
            (cat_one, block, lambda g: (0, 0, g)), whole(two_taps),
            (fact_cat, slim, lambda g: (0, 0, g)), whole(ftwo_taps),
        ],
        [
            ((3, 3, CM, CM), BF, (3, 1, CM, CM), lambda g: (0, g, 0, 0), True),
            ((3, 3, CFM, CFM), BF, (3, 1, CFM, CFM), lambda g: (0, g, 0, 0), True),
        ],
        flops=2 * rows * 768 * 768,
        name="slow_space_grad",
        unroll=True,
    )
    slow_out = pixels_first(slow_out, slow_in.shape)
    rim_before, rim_after, slow_out, flows["space"] = tie(
        [], rim_before, rim_after, slow_out, flows["space"]
    )
    state, trio, sums = call(
        bind(k_trio, count=count),
        micro,
        [
            scalar(links), scalar(nexts), group(d_one, frames),
            stream(rim_before, 1), stream(rim_after, 1), group(d_short, frames),
            whole(slow_time), whole(projection),
            group(lat_pre, frames), stream(total1, 1), whole(gb),
        ],
        [og(3 * CM, BF, frames), ("lat_grad", frames), os(frames, 2, CL)],
        state=state,
        flops=2 * rows * 1792 * 256,
        name="back_lateral",
    )

    def weights_of_one(value, stage):
        if stage == 0:
            time_grad = outer_joined(slow, lat_act, trio, 3, "slow_time_grad")
            value, time_grad, flows["trio"] = tie([], value, time_grad, trio)
            both = jnp.concatenate([shares(time_grad), shares(flows["space"])], 1)
            flows["b"] = Shares(spots, both)
            flows["time_rows"] = time_grad.shape[0] * time_grad.shape[1] // devices
        elif stage == 1:
            value, later = tie([flows["b"]], value, flows["trio"])
            flows["slow_in_grad"] = call(
                k_slow_grad,
                micro,
                [group(later, per), group(d_short, per), whole(slow_time), whole(projection)],
                [out_group((groups, PIX, CS), BF, per, False)],
                flops=2 * rows * 1792 * 1024,
                name="slow_in_grad",
            )[0]
        elif stage == 2:
            value, flows["slow_in_grad"] = tie(
                [flows["b"]], value, pixels_first(flows["slow_in_grad"], slow_in.shape)
            )
        return value

    sums_d = all_sum(sums, weights_of_one)
    slow_in_grad = flows["slow_in_grad"]

    state, d_lat, head = call(
        bind(k_back_lat, count=count),
        micro,
        [
            scalar(links), group(lat_pre, frames), stream(total1, 1), ("lat_grad", frames),
            stream(sums_d, 1), whole(gb), whole(masks),
        ],
        [og(CL, BF, frames), edge(CL)],
        state=state,
        name="back_lat",
    )
    packed = devices <= CFM
    tops = [
        scalar(links), scalar(nexts), whole(fast), whole(edge_down), whole(edge_up),
        whole(d_lat), whole(d_fone),
    ]
    if packed:
        ends = [flows["fspace"].reshape(-1, CFM), flows["fast_out"]]
        sizes = [5 * CF, 5 * CF, 3 * CF, 9 * CFM, CFM]
        sizes = [size // devices for size in sizes]
        tops += [whole(part) for part in ends]
        outs = [out_whole((devices, -(-sum(sizes) // 8) * 8, 128), BF)]
    else:
        outs = [out_whole((5 * CF, CL), BF), out_whole((3, CF, CFM), BF)]
    first_grad = call(
        bind(k_outer_first, micro=micro),
        1,
        tops,
        outs,
        scratch=[pltpu.VMEM((groups, ROWS, 7 * CF), BF)],
        flops=2 * rows * 896 * 384,
        name="lateral_grad",
    )
    *first_grad, head = tie([], *first_grad, head)
    if packed:
        flat = first_grad[0]
    else:
        flat = [
            part.reshape(devices, -1)
            for part in (*first_grad, flows["fspace"], flows["fast_out"])
        ]
        sizes = [part.shape[1] for part in flat]
        flat = jnp.concatenate(flat, 1)
        flat = jnp.pad(flat, ((0, 0), (0, -flat.shape[1] % 1024)))
        flat = flat.reshape(devices, -1, 128)
    last = Shares(spots, flat)
    lat_rim = from_after(head)
    fast_out = pixels_first(fast_out, fast_in.shape)
    lat_rim, fast_out, slow_in_grad = tie(
        [flows["a"], last], lat_rim, fast_out, slow_in_grad
    )
    state, fast_in_grad = call(
        k_fast_grad,
        micro,
        [
            scalar(links), scalar(nexts), ("fgrad", frames), group(d_lat, frames),
            stream(lat_rim, 1), group(d_fone, frames), stream(rim_before, 1),
            stream(rim_after, 1), whole(w_back),
        ],
        [out_group(*quarters, frames, False)],
        state=state,
        scratch=[pltpu.VMEM((frames, ROWS, 768), BF)],
        flops=2 * rows * 768 * 512,
        name="fast_in_grad",
    )
    fast_in_grad, slow_in_grad = tie([flows["b"], last], fast_in_grad, slow_in_grad)
    fast_in_grad = pixels_first(fast_in_grad, fast_in.shape)
    both_out = flows["a"].result().reshape(-1, CS)
    cut = flows["proj_rows"]
    proj_out, out_out = both_out[:cut].reshape(-1), both_out[cut:].reshape(-1)
    both_out = flows["b"].result().reshape(-1, CM)
    cut = flows["time_rows"]
    time_out, space_out = both_out[:cut].reshape(-1), both_out[cut:].reshape(-1)
    flat = last.result()
    smalls = []
    at = 0
    if packed:
        flat = flat.reshape(-1, 128)
        parts = []
        for size, lanes in zip(sizes, (128, 128, CFM, CFM, CF)):
            parts.append(flat[at : at + size, :lanes])
            at += size
        parts = [jnp.concatenate(parts[:2], 1)] + parts[2:]
        smalls = [part.reshape(-1) for part in parts]
    else:
        for size in sizes:
            smalls.append(flat[at : at + size])
            at += size

    norms, fnorms = call(
        k_params,
        1,
        [whole(sums_a), whole(sums_b), whole(sums_c), whole(sums_d)],
        [out_whole((2, 2816), F32), out_whole((8, 128), F32)],
        name="norm_grads",
    )
    norms = pick(norms, share_start, share, 1)
    fast_gain_grad, fast_bias_grad = (
        jnp.concatenate([fnorms[row, :CFM], fnorms[row + 2, :CFM], fnorms[row + 4]])
        for row in range(2)
    )
    return (
        jnp.swapaxes(slow_out, 1, 2),
        jnp.swapaxes(fast_out, 1, 2),
        jnp.swapaxes(slow_in_grad, 1, 2),
        jnp.swapaxes(fast_in_grad, 1, 2),
        smalls[0],
        time_out,
        space_out,
        out_out,
        proj_out,
        smalls[1],
        smalls[2],
        smalls[3],
        norms[0],
        norms[1],
        fast_gain_grad,
        fast_bias_grad,
    )


def solution(mesh):
    frames = P(None, AXES, None, None)
    flat = P(AXES)
    return jax.shard_map(
        local,
        mesh=mesh,
        in_specs=(frames, frames, P(None, AXES))
        + (flat,) * 10
        + (P(), P(), frames, frames),
        out_specs=(frames,) * 4 + (flat,) * 10 + (P(), P()),
        check_vma=False,
    )
```
